256 devices in a mesh: gx: 4 (over x_lo, core), gy: 8 (over y, x_hi), gz: 8 (over z).
Axes of the slice: x: 4 (x_hi: 2, x_lo: 2; x = x_hi * 2 + x_lo), y: 4, z: 8, core: 2. Of those that a mesh axis runs over, the one named last changes fastest.
Arguments:
- phi_start: float32 [128, 384, 2048], P('gx', 'gy', 'gz'), may hold values from -6 to 6
- band_ids: int32 [4, 8, 8, 64], P('gx', 'gy', 'gz'), may hold values from 0 to 95, as said below
- band_count: int32 [4, 8, 8], P('gx', 'gy', 'gz'), may hold values from 2 to 64, as said below
- owners: int32 [4, 8, 8, 64], P('gx', 'gy', 'gz'), may hold values from 0 to 31, as said below
Outputs:
- level_set: float32 [128, 384, 2048], P('gx', 'gy', 'gz')
- brick_stats: float32 [4, 8, 8, 5, 64], P('gx', 'gy', 'gz')
The draws below stay inside these ranges and needn't reach their ends.
Inputs may be any that keep to these rules, and one draw needn't show every extreme that they name: `band_ids`: a device's 64 entries are distinct brick numbers. `band_count`: some device has 64 live entries and some has 2. `owners`: no owner appears more than 2 times in one device's list; some owner appears 2 times among the first 2 entries of every device's list.
All inputs are finite; a program needn't handle non-finite values.
Results may differ from the reference program's by a relative error of at most 0.0003.
Values sent between devices are 32-bit elements; how exact they have to be, the bound alone decides.
No kernel may reach another device: no remote copies, remote signals or barrier semaphores. Data moves between devices by JAX's collectives and lax.ppermute only.
A program may use at most 128 MiB of HBM per device.

```python
import math
import jax
import jax.numpy as jnp
from jax import lax

CX = 32
CY = 48
CZ = 256
STEPS = 3
BRICK = 16
SLOTS = 64
NX = 128
NY = 384
NZ = 2048
OWNERS = 32
CAP = 2
BAND_MAX = 64
COUNT_MIN = 2
N_GX = 4
N_GY = 8
N_GZ = 8


def draw_band_ids(key, part):
    devices = N_GX * N_GY * N_GZ
    bricks = CX // BRICK * (CY // BRICK) * (CZ // BRICK)
    scores = jax.random.randint(key, (devices, bricks), 0, 2 ** 20) * bricks + jnp.arange(bricks, dtype=jnp.int32)[None, :]
    ordering = jnp.sort(scores, axis=1) % bricks
    return ordering[:, :BAND_MAX].astype(jnp.int32).reshape(N_GX, N_GY, N_GZ, BAND_MAX)


def draw_band_count(key, part):
    devices = N_GX * N_GY * N_GZ
    counts = jax.random.randint(jax.random.fold_in(key, 1), (devices,), COUNT_MIN, BAND_MAX + 1)
    busiest = jax.random.randint(jax.random.fold_in(key, 2), (), 0, devices)
    quietest = (busiest + 1) % devices
    device_ids = jnp.arange(devices, dtype=jnp.int32)
    counts = jnp.where(device_ids == quietest, COUNT_MIN, counts)
    counts = jnp.where(device_ids == busiest, BAND_MAX, counts)
    return counts.astype(jnp.int32).reshape(N_GX, N_GY, N_GZ)


def draw_owners(key, part):
    devices = N_GX * N_GY * N_GZ
    window = COUNT_MIN
    favored = jax.random.randint(jax.random.fold_in(key, 7), (), 0, OWNERS)
    others = jnp.arange(SLOTS - CAP, dtype=jnp.int32)
    others = others + CAP * (others >= favored * CAP).astype(jnp.int32)
    shuffle_scores = jax.random.randint(jax.random.fold_in(key, 8), (devices, SLOTS - CAP), 0, 2 ** 20) * SLOTS + others[None, :]
    shuffled = jnp.sort(shuffle_scores, axis=1) % SLOTS
    place_scores = jax.random.randint(jax.random.fold_in(key, 9), (devices, window), 0, 2 ** 20) * window + jnp.arange(window, dtype=jnp.int32)[None, :]
    place_order = jnp.sort(place_scores, axis=1) % window
    favored_pos = place_order[:, :CAP]
    tail_pos = jnp.broadcast_to(jnp.arange(window, SLOTS, dtype=jnp.int32)[None, :], (devices, SLOTS - window))
    rest_pos = jnp.concatenate([place_order[:, CAP:], tail_pos], axis=1)
    row_ids = jnp.arange(devices, dtype=jnp.int32)[:, None]
    owner_table = jnp.zeros((devices, SLOTS), jnp.int32)
    owner_table = owner_table.at[row_ids, favored_pos].set(jnp.broadcast_to(favored, (devices, CAP)).astype(jnp.int32))
    owner_table = owner_table.at[row_ids, rest_pos].set((shuffled // CAP).astype(jnp.int32))
    return owner_table[:, :BAND_MAX].reshape(N_GX, N_GY, N_GZ, BAND_MAX)


def block_levels(stream_key, dims, cuts, smallest, top_value):
    def one(axis_at, blocks):
        heights = jax.random.uniform(jax.random.fold_in(jax.random.fold_in(stream_key, 6), axis_at), (blocks,), jnp.float32, smallest / len(cuts), top_value / len(cuts))
        return jnp.repeat(jnp.exp(heights), dims[axis_at] // blocks).reshape((-1,) + (1,) * (len(dims) - axis_at - 1))

    factor_of = one(*cuts[0])
    for cut in cuts[1:]:
        factor_of = factor_of * one(*cut)
    return factor_of


def centred(rng, shape, width, most, split=(), held_as=jnp.bfloat16):
    values = width * jax.random.normal(rng, shape, jnp.float32)
    if split:
        values = values * block_levels(rng, shape, split, -0.22, 0.18)
    return jnp.clip(values, -most, most).astype(held_as)


def setup_inputs(seed: int = 0) -> dict:
    key_of = jax.random.split(jax.random.key(seed), 5)
    return {
        "phi_start": centred(key_of[0], (NX, NY, NZ), 1.0, 6.0, ((0, 4), (1, 8), (2, 8)), jnp.float32),
        "band_ids": draw_band_ids(jax.random.fold_in(key_of[4], 71), 0),
        "band_count": draw_band_count(jax.random.fold_in(key_of[4], 71), 0),
        "owners": draw_owners(jax.random.fold_in(key_of[4], 71), 0),
    }


pseudo_dt = 0.3
weno_eps = 1e-06
band_eps = 1.5
grad_floor = 0.25

def weno_value(v_one, v_two, v_three, v_four, v_five):
    poly_one = v_one / 3.0 - 7.0 * v_two / 6.0 + 11.0 * v_three / 6.0
    poly_two = -v_two / 6.0 + 5.0 * v_three / 6.0 + v_four / 3.0
    poly_three = v_three / 3.0 + 5.0 * v_four / 6.0 - v_five / 6.0
    smooth_one = 13.0 / 12.0 * (v_one - 2.0 * v_two + v_three) ** 2 + 0.25 * (v_one - 4.0 * v_two + 3.0 * v_three) ** 2
    smooth_two = 13.0 / 12.0 * (v_two - 2.0 * v_three + v_four) ** 2 + 0.25 * (v_two - v_four) ** 2
    smooth_three = 13.0 / 12.0 * (v_three - 2.0 * v_four + v_five) ** 2 + 0.25 * (3.0 * v_three - 4.0 * v_four + v_five) ** 2
    alpha_one = 0.1 / (weno_eps + smooth_one) ** 2
    alpha_two = 0.6 / (weno_eps + smooth_two) ** 2
    alpha_three = 0.3 / (weno_eps + smooth_three) ** 2
    return (alpha_one * poly_one + alpha_two * poly_two + alpha_three * poly_three) / (alpha_one + alpha_two + alpha_three)

def sign_of(values):
    return values / jnp.sqrt(values * values + 1.0)

def hamiltonian(padded, sign_part):
    summed = jnp.zeros(sign_part.shape, jnp.float32)
    for axis_now in range(3):
        stripe = padded
        for across in range(3):
            if across != axis_now:
                stripe = lax.slice_in_dim(stripe, 3, stripe.shape[across] - 3, axis=across)
        length = stripe.shape[axis_now] - 6
        differences = lax.slice_in_dim(stripe, 1, length + 6, axis=axis_now) - lax.slice_in_dim(stripe, 0, length + 5, axis=axis_now)
        shifted = [lax.slice_in_dim(differences, offset, offset + length, axis=axis_now) for offset in range(6)]
        left_slope = weno_value(shifted[0], shifted[1], shifted[2], shifted[3], shifted[4])
        right_slope = weno_value(shifted[5], shifted[4], shifted[3], shifted[2], shifted[1])
        rising = jnp.maximum(jnp.maximum(left_slope, 0.0) ** 2, jnp.minimum(right_slope, 0.0) ** 2)
        falling = jnp.maximum(jnp.minimum(left_slope, 0.0) ** 2, jnp.maximum(right_slope, 0.0) ** 2)
        summed = summed + jnp.where(sign_part > 0.0, rising, falling)
    return jnp.sqrt(summed) - 1.0

def brick_stats(cubes):
    brick_edge = cubes.shape[0] - 2

    def window(step_x, step_y, step_z):
        return cubes[1 + step_x:1 + step_x + brick_edge, 1 + step_y:1 + step_y + brick_edge, :, 1 + step_z:1 + step_z + brick_edge]
    center = window(0, 0, 0)
    grad_x = 0.5 * (window(1, 0, 0) - window(-1, 0, 0))
    grad_y = 0.5 * (window(0, 1, 0) - window(0, -1, 0))
    grad_z = 0.5 * (window(0, 0, 1) - window(0, 0, -1))
    curve_xx = window(1, 0, 0) - 2.0 * center + window(-1, 0, 0)
    curve_yy = window(0, 1, 0) - 2.0 * center + window(0, -1, 0)
    curve_zz = window(0, 0, 1) - 2.0 * center + window(0, 0, -1)
    curve_xy = 0.25 * (window(1, 1, 0) - window(1, -1, 0) - window(-1, 1, 0) + window(-1, -1, 0))
    curve_xz = 0.25 * (window(1, 0, 1) - window(1, 0, -1) - window(-1, 0, 1) + window(-1, 0, -1))
    curve_yz = 0.25 * (window(0, 1, 1) - window(0, 1, -1) - window(0, -1, 1) + window(0, -1, -1))
    squares = grad_x * grad_x + grad_y * grad_y + grad_z * grad_z
    magnitude = jnp.sqrt(jnp.maximum(squares, grad_floor))
    bending = (curve_xx * (grad_y * grad_y + grad_z * grad_z) + curve_yy * (grad_x * grad_x + grad_z * grad_z) + curve_zz * (grad_x * grad_x + grad_y * grad_y) - 2.0 * (grad_x * grad_y * curve_xy + grad_x * grad_z * curve_xz + grad_y * grad_z * curve_yz)) / magnitude ** 3
    spread = jnp.where(jnp.abs(center) < band_eps, 0.5 * (1.0 + jnp.cos(math.pi * center / band_eps)) / band_eps, 0.0)
    weight = spread * magnitude
    area_scale = 1.0 / (brick_edge * brick_edge)
    factors = [weight, weight * bending, weight * grad_x / magnitude, weight * grad_y / magnitude, weight * grad_z / magnitude]
    return jnp.stack([lax.optimization_barrier(jnp.sum(factor, axis=(0, 1, 3))) for factor in factors], axis=0) * area_scale

def reinit_step(values, sign_field):
    padded = jnp.pad(values, 3, mode='wrap')
    blocks = values.shape[0] // 8

    def one_block(block_index):
        x_slab = lax.dynamic_slice_in_dim(padded, block_index * 8, 14, 0)
        sign_part = lax.dynamic_slice_in_dim(sign_field, block_index * 8, 8, 0)
        current = lax.dynamic_slice_in_dim(values, block_index * 8, 8, 0)
        return current - pseudo_dt * sign_part * hamiltonian(x_slab, sign_part)
    stacked = lax.map(one_block, jnp.arange(blocks, dtype=jnp.int32))
    return stacked.reshape(values.shape)

def reference(phi_start, band_ids, band_count, owners):
    sign_field = sign_of(phi_start)
    level_set = phi_start
    for number in range(STEPS):
        level_set = reinit_step(level_set, sign_field)
    bordered = jnp.pad(level_set, 1, mode='wrap')
    devices = N_GX * N_GY * N_GZ
    capacity = SLOTS // (N_GX * N_GY)
    count_y = CY // BRICK
    count_z = CZ // BRICK

    def one_device(packed):
        device_index, device_ids, live_count, targets = packed
        pos_x = device_index // (N_GY * N_GZ)
        pos_y = device_index // N_GZ % N_GY
        pos_z = device_index % N_GZ

        def cube_of(brick_id):
            start_x = pos_x * CX + brick_id // (count_y * count_z) * BRICK
            start_y = pos_y * CY + brick_id // count_z % count_y * BRICK
            start_z = pos_z * CZ + brick_id % count_z * BRICK
            return lax.dynamic_slice(bordered, (start_x, start_y, start_z), (BRICK + 2, BRICK + 2, BRICK + 2))
        brick_cubes = jax.vmap(cube_of, out_axes=2)(device_ids)
        entries = jnp.arange(BAND_MAX, dtype=jnp.int32)
        is_live = entries < live_count
        brick_terms = brick_stats(brick_cubes) * is_live.astype(jnp.float32)[None, :]
        earlier = entries[None, :] < entries[:, None]
        same_owner = targets[None, :] == targets[:, None]
        owner_rank = lax.optimization_barrier(jnp.sum((earlier & same_owner & is_live[None, :]).astype(jnp.int32), axis=1))
        columns = jnp.where(is_live, targets * capacity + owner_rank, SLOTS).astype(jnp.int32)
        return jnp.zeros((5, SLOTS), jnp.float32).at[:, columns].set(brick_terms, mode='drop')
    outgoing = lax.map(one_device, (jnp.arange(devices, dtype=jnp.int32), band_ids.reshape(devices, BAND_MAX), band_count.reshape(devices), owners.reshape(devices, BAND_MAX)))
    grouped = outgoing.reshape(N_GX * N_GY, N_GZ, 5, N_GX * N_GY, capacity)
    arranged = jnp.transpose(grouped, (3, 1, 2, 0, 4)).reshape(N_GX, N_GY, N_GZ, 5, SLOTS)
    return (level_set, arranged)
```

```python
import jax
import jax.numpy as jnp
from jax import lax
from jax.experimental import pallas as pl
from jax.experimental.pallas import tpu as pltpu
from jax.sharding import PartitionSpec as P

STEPS = 3
BRICK = 16
SLOTS = 64
CX, CY, CZ = 32, 48, 256
ROWS = CX * CY
YT = CY // 8
SUB = 2
WENO_EPS = 1e-06
F32 = jnp.float32
VMEM_LIMIT = 48 * 1024 * 1024


def rcp(value):
    return pltpu.reciprocal(value, approx=True)


def smooth_weights(e_low, e_high, third):
    base = third * third * (4.0 / 3.0) + WENO_EPS
    q_a = rcp(e_low * (e_low - third) + base)
    q_b = rcp(e_low * e_high + base)
    q_c = rcp(e_high * (e_high + third) + base)
    return q_a * q_a, 6.0 * (q_b * q_b), q_c * q_c


def biased_parts(wa_next, wb, wc_prev, t_prev, t_here, t_next):
    x = wc_prev * (t_here - t_prev)
    y = wa_next * (t_next - t_here)
    both = x + y
    both = both + both
    total = (wa_next + wb) + wc_prev
    left = t_here + (both + y) * rcp(total + (wa_next + wa_next))
    right = (both + x) * rcp(total + (wc_prev + wc_prev)) - t_here
    return left, right


def upwind_square(centre, left, right, sigma):
    best = jnp.maximum(sigma * (centre - left), (-sigma) * (centre + right))
    best = jnp.maximum(best, 0.0)
    return best * best


def sigma_of(value):
    return jnp.where(value > 0.0, F32(1.0), F32(-1.0))


def from_values(v_m, v_0, v_1, v_2):
    d_m, d_0, d_1 = v_0 - v_m, v_1 - v_0, v_2 - v_1
    e_0, e_1 = d_0 - d_m, d_1 - d_0
    return e_0, e_1, e_1 - e_0


def z_column(even, odd, sigma_even, sigma_odd):
    def down(part):
        return pltpu.roll(part, 1, 1)

    def up(part):
        return pltpu.roll(part, 127, 1)

    v = {-2: down(even), -1: down(odd), 0: even, 1: odd, 2: up(even), 3: up(odd)}
    d = {k: v[k + 1] - v[k] for k in range(-2, 3)}
    e = {k: d[k] - d[k - 1] for k in range(-1, 3)}
    t = {k: e[k + 1] - e[k] for k in range(-1, 2)}
    t[2] = up(t[0])
    w_0 = smooth_weights(e[0], e[1], t[0])
    w_1 = smooth_weights(e[1], e[2], t[1])
    left_0, right_0 = biased_parts(w_1[0], w_0[1], down(w_1[2]), t[-1], t[0], t[1])
    left_1, right_1 = biased_parts(up(w_0[0]), w_1[1], w_0[2], t[0], t[1], t[2])
    return (
        upwind_square(3.0 * (d[-1] + d[0]), down(left_1), right_0, sigma_even),
        upwind_square(3.0 * (d[0] + d[1]), left_0, right_1, sigma_odd),
    )


def edge_column(window, u_ref, p_ref, u_row, p_row, sigma):
    def rows(start):
        return window[pl.ds(start, 8), :]

    e_0, e_1, t = from_values(rows(u_row - 1), rows(u_row), rows(u_row + 1), rows(u_row + 2))
    w_a, w_b, w_c = smooth_weights(e_0, e_1, t)
    for slot, part in enumerate((w_a, w_b, w_c, t)):
        u_ref[slot, pl.ds(u_row, 8), :] = part
    left, right = biased_parts(
        u_ref[0, pl.ds(p_row + 1, 8), :],
        u_ref[1, pl.ds(p_row, 8), :],
        u_ref[2, pl.ds(p_row - 1, 8), :],
        u_ref[3, pl.ds(p_row - 1, 8), :],
        u_ref[3, pl.ds(p_row, 8), :],
        u_ref[3, pl.ds(p_row + 1, 8), :],
    )
    p_ref[0, pl.ds(p_row, 8), :] = left
    p_ref[1, pl.ds(p_row, 8), :] = right
    centre = 3.0 * (rows(9) - rows(7))
    return upwind_square(
        centre, p_ref[0, pl.ds(7, 8), :], p_ref[1, pl.ds(8, 8), :], sigma
    )


def write_faces(source, xlo, xhi, ylo, yhi, zlo, zhi):
    xlo[...] = source[0:3]
    xhi[...] = source[CX - 3 : CX]

    for x in range(CX):
        for k in range(3):
            ylo[k, x : x + 1, :] = source[x, k : k + 1, :]
            yhi[k, x : x + 1, :] = source[x, CY - 3 + k : CY - 2 + k, :]
    for chunk in range(CX // 8):
        columns = slice(8 * CY * chunk, 8 * CY * (chunk + 1))
        for parity in range(2):
            part = source[8 * chunk : 8 * chunk + 8, :, 128 * parity : 128 * parity + 128]
            part = part.reshape(8 * CY, 128).T
            for k in range(4):
                zlo[2 * k + parity : 2 * k + parity + 1, columns] = part[k : k + 1]
                zhi[2 * k + parity : 2 * k + parity + 1, columns] = part[124 + k : 125 + k]


def pack_kernel(phi, mixed, xlo, xhi, ylo, yhi, zlo, zhi, turned):
    for chunk in range(CX // 8):
        planes = slice(8 * chunk, 8 * chunk + 8)
        for half in range(2):
            part = phi[planes, :, 128 * half : 128 * half + 128]
            part = part.reshape(8 * CY, 128).T
            for c in range(3):
                turned[c, 128 * half : 128 * half + 128, :] = part[:, 128 * c : 128 * c + 128]
        for parity in range(2):
            part = [turned[c, pl.ds(parity, 128, stride=2), :].T for c in range(3)]
            part = jnp.concatenate(part, axis=0)
            mixed[planes, :, 128 * parity : 128 * parity + 128] = part.reshape(8, CY, 128)
    write_faces(mixed, xlo, xhi, ylo, yhi, zlo, zhi)


def unpack_kernel(mixed, out, turned):
    for chunk in range(CX // 8):
        planes = slice(8 * chunk, 8 * chunk + 8)
        for parity in range(2):
            part = mixed[planes, :, 128 * parity : 128 * parity + 128]
            part = part.reshape(8 * CY, 128).T
            for c in range(3):
                turned[c, pl.ds(parity, 128, stride=2), :] = part[:, 128 * c : 128 * c + 128]
        for half in range(2):
            part = [turned[c, 128 * half : 128 * half + 128, :].T for c in range(3)]
            part = jnp.concatenate(part, axis=0)
            out[planes, :, 128 * half : 128 * half + 128] = part.reshape(8, CY, 128)


def step_kernel(
    phi0, zlo0, zhi0, v, zlo_own, zhi_own, x_low, x_high, y_low, y_high, z_low, z_high,
    out, xlo, xhi, ylo, yhi, zlo, zhi,
    vs, summed, u_ref, p_ref, window, zu_ref, zp_ref, edges, fixes,
):
    def fill(x, carry):
        for zt in range(2):
            lanes = pl.ds(128 * zt, 128)
            vs[zt, x, 8 : 8 + CY, :] = v[x, :, lanes]
        return carry

    lax.fori_loop(0, CX, fill, 0)
    for x in range(CX):
        for zt in range(2):
            for k in range(3):
                lanes = slice(128 * zt, 128 * zt + 128)
                vs[zt, x, 5 + k : 6 + k, :] = y_low[k, x : x + 1, lanes]
                vs[zt, x, 8 + CY + k : 9 + CY + k, :] = y_high[k, x : x + 1, lanes]

    window[pl.ds(5, 3), :] = z_low[5:8, :]
    window[pl.ds(8, 8), :] = zlo_own[...]
    fixed = edge_column(window, zu_ref, zp_ref, 6, 7, sigma_of(zlo0[...]))
    for parity, lane_at, cell_at in ((0, 0, 0), (0, 1, 2), (1, 0, 1)):
        edges[parity, lane_at : lane_at + 1, :] = fixed[cell_at : cell_at + 1]
    window[pl.ds(8, 8), :] = zhi_own[...]
    window[pl.ds(16, 3), :] = z_high[0:3, :]
    fixed = edge_column(window, zu_ref, zp_ref, 9, 8, sigma_of(zhi0[...]))
    for parity, lane_at, cell_at in ((0, 127, 6), (1, 126, 5), (1, 127, 7)):
        edges[parity, lane_at : lane_at + 1, :] = fixed[cell_at : cell_at + 1]
    for parity in range(2):
        fixes[parity] = edges[parity].T

    def x_pass(yt, carry):
        row = pl.multiple_of(8 * yt, 8)
        for zt in range(2):
            lanes = pl.ds(128 * zt, 128)

            def cell(x):
                if x < 0:
                    return x_low[3 + x, pl.ds(row, 8), lanes]
                if x >= CX:
                    return x_high[x - CX, pl.ds(row, 8), lanes]
                return v[x, pl.ds(row, 8), lanes]

            d, e, t, weights, lefts, rights = {}, {}, {}, {}, {}, {}
            d[-3] = cell(-2) - cell(-3)
            d[-2] = cell(-1) - cell(-2)
            e[-2] = d[-2] - d[-3]
            for j in range(-2, CX + 1):
                d[j + 1] = cell(j + 2) - cell(j + 1)
                e[j + 1] = d[j + 1] - d[j]
                t[j] = e[j + 1] - e[j]
                weights[j] = smooth_weights(e[j], e[j + 1], t[j])
                p = j - 1
                if p >= -1:
                    lefts[p], rights[p] = biased_parts(
                        weights[p + 1][0], weights[p][1], weights[p - 1][2], t[p - 1], t[p], t[p + 1]
                    )
                if p >= 0:
                    sigma = sigma_of(phi0[p, pl.ds(row, 8), lanes])
                    centre = 3.0 * (d[p - 1] + d[p])
                    summed[zt, p, pl.ds(row, 8), :] = upwind_square(
                        centre, lefts[p - 1], rights[p], sigma
                    )
        return carry

    lax.fori_loop(0, YT, x_pass, 0)

    lane = lax.broadcasted_iota(jnp.int32, (8, 128), 1)
    fix_even = (lane < 2) | (lane == 127)
    fix_odd = (lane < 1) | (lane > 125)

    def y_weights(x, sub, zt, k):
        start = 6 + 8 * k
        e_0, e_1, t = from_values(
            *[vs[zt, x, pl.ds(start + shift, 8), :] for shift in (-1, 0, 1, 2)]
        )
        w_a, w_b, w_c = smooth_weights(e_0, e_1, t)
        for slot, part in enumerate((w_a, w_b, w_c, t)):
            u_ref[sub, zt, slot, pl.ds(8 * k, 8), :] = part

    def y_parts(sub, zt, k):
        def read(slot, row):
            return u_ref[sub, zt, slot, pl.ds(row, 8), :]

        row = 8 * k + 1
        left, right = biased_parts(
            read(0, row + 1), read(1, row), read(2, row - 1),
            read(3, row - 1), read(3, row), read(3, row + 1),
        )
        p_ref[sub, zt, 0, pl.ds(8 * k, 8), :] = left
        p_ref[sub, zt, 1, pl.ds(8 * k, 8), :] = right

    def update(x, sub, k):
        rows = pl.ds(8 * k, 8)
        values, signs, sigmas, totals = [], [], [], []
        for zt in range(2):
            phi = phi0[x, rows, pl.ds(128 * zt, 128)]
            sigma = sigma_of(phi)
            centre = 3.0 * (
                vs[zt, x, pl.ds(9 + 8 * k, 8), :] - vs[zt, x, pl.ds(7 + 8 * k, 8), :]
            )
            totals.append(
                summed[zt, x, rows, :]
                + upwind_square(
                    centre, p_ref[sub, zt, 0, rows, :], p_ref[sub, zt, 1, pl.ds(8 * k + 1, 8), :], sigma
                )
            )
            values.append(vs[zt, x, pl.ds(8 + 8 * k, 8), :])
            sigmas.append(sigma)
            signs.append(phi * lax.rsqrt(phi * phi + 1.0))
        along = z_column(*values, *sigmas)
        flat = pl.multiple_of(x * CY, 8) + 8 * k
        along = (
            jnp.where(fix_even, fixes[0, pl.ds(flat, 8), :], along[0]),
            jnp.where(fix_odd, fixes[1, pl.ds(flat, 8), :], along[1]),
        )
        for zt in range(2):
            total = totals[zt] + along[zt]
            root = total * lax.rsqrt(jnp.maximum(total, 1e-30))
            out[x, rows, pl.ds(128 * zt, 128)] = values[zt] - signs[zt] * (0.05 * root - 0.3)

    def yz_pass(group, carry):
        for sub in range(SUB):
            for zt in range(2):
                for k in range(YT + 1):
                    y_weights(group * SUB + sub, sub, zt, k)
        for sub in range(SUB):
            for zt in range(2):
                for k in range(YT + 1):
                    y_parts(sub, zt, k)
        for sub in range(SUB):
            for k in range(YT):
                update(group * SUB + sub, sub, k)
        return carry

    lax.fori_loop(0, CX // SUB, yz_pass, 0)
    write_faces(out, xlo, xhi, ylo, yhi, zlo, zhi)


FACES = [
    jax.ShapeDtypeStruct((3, CY, CZ), F32),
    jax.ShapeDtypeStruct((3, CY, CZ), F32),
    jax.ShapeDtypeStruct((3, CX, CZ), F32),
    jax.ShapeDtypeStruct((3, CX, CZ), F32),
    jax.ShapeDtypeStruct((8, ROWS), F32),
    jax.ShapeDtypeStruct((8, ROWS), F32),
]
BLOCK = jax.ShapeDtypeStruct((CX, CY, CZ), F32)


def vmem_specs(count):
    return [pl.BlockSpec(memory_space=pltpu.VMEM)] * count


def pack(phi):
    return pl.pallas_call(
        pack_kernel,
        out_shape=[BLOCK] + FACES,
        in_specs=vmem_specs(1),
        out_specs=vmem_specs(7),
        scratch_shapes=[pltpu.VMEM((3, CZ, 128), F32)],
        compiler_params=pltpu.CompilerParams(vmem_limit_bytes=VMEM_LIMIT),
        name="pack",
    )(phi)


def unpack(mixed):
    return pl.pallas_call(
        unpack_kernel,
        out_shape=BLOCK,
        in_specs=vmem_specs(1),
        out_specs=vmem_specs(1)[0],
        scratch_shapes=[pltpu.VMEM((3, CZ, 128), F32)],
        compiler_params=pltpu.CompilerParams(vmem_limit_bytes=VMEM_LIMIT),
        name="unpack",
    )(mixed)


def step(phi0, zlo0, zhi0, v, zlo_own, zhi_own, halos):
    return pl.pallas_call(
        step_kernel,
        out_shape=[BLOCK] + FACES,
        in_specs=vmem_specs(12),
        out_specs=vmem_specs(7),
        scratch_shapes=[
            pltpu.VMEM((2, CX, 64, 128), F32),
            pltpu.VMEM((2, CX, CY, 128), F32),
            pltpu.VMEM((SUB, 2, 4, 64, 128), F32),
            pltpu.VMEM((SUB, 2, 2, 64, 128), F32),
            pltpu.VMEM((24, ROWS), F32),
            pltpu.VMEM((4, 24, ROWS), F32),
            pltpu.VMEM((2, 24, ROWS), F32),
            pltpu.VMEM((2, 128, ROWS), F32),
            pltpu.VMEM((2, ROWS, 128), F32),
        ],
        compiler_params=pltpu.CompilerParams(vmem_limit_bytes=VMEM_LIMIT),
        name="step",
    )(phi0, zlo0, zhi0, v, zlo_own, zhi_own, *halos)


HALF_COS = [
    0.9999999991256178, -0.23370050635094053, 0.019968606689123116,
    -0.0008935362743290266, 2.3601076640059624e-05,
]
BAND_SQUARE = 1.5 * 1.5


def half_cosine(value):
    square = jnp.minimum(value * value, BAND_SQUARE)
    shape = F32(HALF_COS[4] / BAND_SQUARE**5)
    for k in (3, 2, 1, 0):
        shape = shape * square + F32(HALF_COS[k] / BAND_SQUARE ** (k + 1))
    return (BAND_SQUARE - square) * shape


def five_terms(centre, keep, dx, sx, dy, sy, dz, sz, dxy, dxz, dyz):
    twice = centre + centre
    xx, yy, zz = dx * dx, dy * dy, dz * dz
    squares = jnp.maximum(xx + yy + zz, 1.0)
    root = lax.rsqrt(squares)
    bend = (sx - twice) * (yy + zz) + (sy - twice) * (xx + zz) + (sz - twice) * (xx + yy)
    bend = bend - 0.5 * (dx * (dy * dxy + dz * dxz) + dy * dz * dyz)
    cosine = half_cosine(centre)
    spread = cosine * cosine
    if keep is not None:
        spread = jnp.where(keep, spread, 0.0)
    return (
        spread * (squares * root),
        spread * bend * (root * root),
        spread * dx,
        spread * dy,
        spread * dz,
    )


def brick_kernel(v, x_low, x_high, y_low, y_high, z_window, places, z_places, record, vs, stack):
    def fill(x, carry):
        for zt in range(2):
            vs[zt, x + 1, 8 : 8 + CY, :] = v[x, :, pl.ds(128 * zt, 128)]
        return carry

    lax.fori_loop(0, CX, fill, 0)
    for zt in range(2):
        lanes = slice(128 * zt, 128 * zt + 128)
        vs[zt, 0, 8 : 8 + CY, :] = x_low[0, :, lanes]
        vs[zt, CX + 1, 8 : 8 + CY, :] = x_high[0, :, lanes]
        for x in range(CX + 2):
            vs[zt, x, 7:8, :] = y_low[x : x + 1, lanes]
            vs[zt, x, 8 + CY : 9 + CY, :] = y_high[x : x + 1, lanes]

    lane = lax.broadcasted_iota(jnp.int32, (8, 128), 1)
    keeps = (lane != 0, lane != 127)

    def down(part):
        return pltpu.roll(part, 1, 1)

    def up(part):
        return pltpu.roll(part, 127, 1)

    def neighbours(pair):
        return ((down(pair[1]), pair[1]), (pair[0], up(pair[0])))

    def tile_terms(x, k):
        def read(zt, plane, shift):
            return vs[zt, plane, pl.ds(8 + 8 * k + shift, 8), :]

        two = range(2)
        centre = [read(zt, x + 1, 0) for zt in two]
        high = [read(zt, x + 2, 0) for zt in two]
        low = [read(zt, x, 0) for zt in two]
        dx = [high[zt] - low[zt] for zt in two]
        sx = [high[zt] + low[zt] for zt in two]
        right = [read(zt, x + 1, 1) for zt in two]
        left = [read(zt, x + 1, -1) for zt in two]
        dy = [right[zt] - left[zt] for zt in two]
        sy = [right[zt] + left[zt] for zt in two]
        dxy = [
            (read(zt, x + 2, 1) - read(zt, x, 1)) - (read(zt, x + 2, -1) - read(zt, x, -1))
            for zt in two
        ]
        around, dx_around, dy_around = neighbours(centre), neighbours(dx), neighbours(dy)
        results = []
        for zt in two:
            results.append(
                five_terms(
                    centre[zt], keeps[zt], dx[zt], sx[zt], dy[zt], sy[zt],
                    around[zt][1] - around[zt][0], around[zt][1] + around[zt][0],
                    dxy[zt],
                    dx_around[zt][1] - dx_around[zt][0],
                    dy_around[zt][1] - dy_around[zt][0],
                )
            )
        return [results[0][n] + results[1][n] for n in range(5)]

    zeros = jnp.zeros((8, 128), F32)
    for bx in range(2):

        def body(step_at, sums):
            sums = list(sums)
            for sub in range(2):
                x = BRICK * bx + 2 * step_at + sub
                for k in range(YT):
                    parts = tile_terms(x, k)
                    for n in range(5):
                        slot = 5 * (k // 2) + n
                        sums[slot] = sums[slot] + parts[n]
            return tuple(sums)

        sums = lax.fori_loop(0, BRICK // 2, body, (zeros,) * 15)
        for by in range(3):
            for n in range(5):
                row = 8 * (3 * bx + by) + n
                stack[row : row + 1, :] = jnp.sum(sums[5 * by + n], axis=0, keepdims=True)
            row = 8 * (3 * bx + by)
            stack[row + 5 : row + 8, :] = jnp.zeros((3, 128), F32)

    total = jnp.zeros((8, SLOTS), F32)
    for b in range(6):
        total = total + jnp.dot(
            stack[8 * b : 8 * b + 8, :], places[b],
            precision=lax.Precision.HIGHEST, preferred_element_type=F32,
        )
    for side in range(2):
        planes = [z_window[3 * side + k] for k in range(3)]

        def cut(plane, step_x, step_y):
            return planes[plane][1 + step_x : 33 + step_x, 1 + step_y : 49 + step_y]

        high, low = cut(1, 1, 0), cut(1, -1, 0)
        right, left = cut(1, 0, 1), cut(1, 0, -1)
        over, under = cut(2, 0, 0), cut(0, 0, 0)
        terms = five_terms(
            cut(1, 0, 0), None,
            high - low, high + low, right - left, right + left, over - under, over + under,
            (cut(1, 1, 1) - cut(1, -1, 1)) - (cut(1, 1, -1) - cut(1, -1, -1)),
            (cut(2, 1, 0) - cut(2, -1, 0)) - (cut(0, 1, 0) - cut(0, -1, 0)),
            (cut(2, 0, 1) - cut(2, 0, -1)) - (cut(0, 0, 1) - cut(0, 0, -1)),
        )
        for bx in range(2):
            rows = [jnp.sum(term[16 * bx : 16 * bx + 16], axis=0, keepdims=True) for term in terms]
            rows = jnp.concatenate(rows + [jnp.zeros((3, CY), F32)], axis=0)
            total = total + jnp.dot(
                rows, z_places[2 * side + bx],
                precision=lax.Precision.HIGHEST, preferred_element_type=F32,
            )
    scale = 2.0 / 3.0 / (BRICK * BRICK)
    row = lax.broadcasted_iota(jnp.int32, (8, SLOTS), 0)
    record[...] = total * jnp.where(row == 1, F32(scale), F32(0.5 * scale))


def bricks(v, x_low, x_high, y_low, y_high, z_window, places, z_places):
    return pl.pallas_call(
        brick_kernel,
        out_shape=jax.ShapeDtypeStruct((8, SLOTS), F32),
        in_specs=vmem_specs(8),
        out_specs=vmem_specs(1)[0],
        scratch_shapes=[
            pltpu.VMEM((2, CX + 2, 64, 128), F32),
            pltpu.VMEM((48, 128), F32),
        ],
        compiler_params=pltpu.CompilerParams(vmem_limit_bytes=VMEM_LIMIT),
        name="bricks",
    )(v, x_low, x_high, y_low, y_high, z_window, places, z_places)


def shift(value, axis, direction):
    count = lax.axis_size(axis)
    pairs = [(i, (i + direction) % count) for i in range(count)]
    return lax.ppermute(value, axis, pairs)


def place_tables(device_ids, live_count, targets):
    entries = jnp.arange(device_ids.shape[0], dtype=jnp.int32)
    is_live = entries < live_count
    earlier = entries[None, :] < entries[:, None]
    same_owner = targets[None, :] == targets[:, None]
    rank = jnp.sum((earlier & same_owner & is_live[None, :]).astype(jnp.int32), axis=1)
    columns = jnp.where(is_live, targets * 2 + rank, SLOTS)
    count = (CX // BRICK) * (CY // BRICK) * (CZ // BRICK)
    brick = jnp.arange(count, dtype=jnp.int32)
    slot = jnp.arange(SLOTS, dtype=jnp.int32)
    hits = (device_ids[:, None, None] == brick[None, :, None]) & (
        columns[:, None, None] == slot[None, None, :]
    )
    table = jnp.any(hits, axis=0).astype(F32)
    table = table.reshape(2, 3, 16, SLOTS)
    places = jnp.repeat(table.reshape(6, 16, SLOTS), 8, axis=1)
    z_places = [
        jnp.repeat(table[bx, :, end], BRICK, axis=0) for end in (0, 15) for bx in range(2)
    ]
    return places, jnp.stack(z_places, axis=0)


def exchange(faces):
    xlo, xhi, ylo, yhi, zlo, zhi = faces
    return (
        shift(xhi, "gx", 1), shift(xlo, "gx", -1),
        shift(yhi, "gy", 1), shift(ylo, "gy", -1),
        shift(zhi, "gz", 1), shift(zlo, "gz", -1),
    )


def per_device(phi_start, band_ids, band_count, owners):
    places, z_places = place_tables(
        band_ids.reshape(-1), band_count.reshape(()), owners.reshape(-1)
    )
    phi0, *faces = pack(phi_start)
    zlo0, zhi0 = faces[4:]
    v = phi0
    for _ in range(STEPS):
        v, *faces = step(phi0, zlo0, zhi0, v, faces[4], faces[5], exchange(faces))
    level_set = unpack(v)

    xlo, xhi, ylo, yhi, zlo, zhi = faces
    x_low, x_high = shift(xhi[2:3], "gx", 1), shift(xlo[0:1], "gx", -1)
    first = jnp.concatenate([x_low[:, 0], ylo[0], x_high[:, 0]], axis=0)
    last = jnp.concatenate([x_low[:, CY - 1], yhi[2], x_high[:, CY - 1]], axis=0)
    y_low, y_high = shift(last, "gy", 1), shift(first, "gy", -1)

    def plane(body, lane):
        middle = jnp.concatenate(
            [x_low[:, :, lane], body.reshape(CX, CY), x_high[:, :, lane]], axis=0
        )
        return jnp.concatenate([y_low[:, lane, None], middle, y_high[:, lane, None]], axis=1)

    bottom, above = plane(zlo[0], 0), plane(zlo[1], 128)
    below, top = plane(zhi[6], 127), plane(zhi[7], 255)
    under, over = shift(top, "gz", 1), shift(bottom, "gz", -1)
    z_window = jnp.stack([under, bottom, above, below, top, over], axis=0)
    record = bricks(v, x_low, x_high, y_low, y_high, z_window, places, z_places)
    totals = lax.all_to_all(record[:5], ("gx", "gy"), split_axis=1, concat_axis=1, tiled=True)
    return level_set, totals.reshape(1, 1, 1, 5, SLOTS)


def solution(mesh):
    placed = (
        P("gx", "gy", "gz"),
        P("gx", "gy", "gz", None),
        P("gx", "gy", "gz"),
        P("gx", "gy", "gz", None),
    )
    return jax.shard_map(
        per_device,
        mesh=mesh,
        in_specs=placed,
        out_specs=(P("gx", "gy", "gz"), P("gx", "gy", "gz", None, None)),
        check_vma=False,
    )
```

```python
import functools

import jax
import jax.numpy as jnp
from jax import lax
from jax.experimental import pallas as pl
from jax.experimental.pallas import tpu as pltpu
from jax.sharding import PartitionSpec as P

STEPS = 3
BRICK = 16
SLOTS = 64
CX, CY, CZ = 32, 48, 256
ROWS = CX * CY
YT = CY // 8
WENO_EPS = 1e-06
F32 = jnp.float32
VMEM_LIMIT = 24 * 1024 * 1024


def rcp(value):
    return pltpu.reciprocal(value, approx=True)


def smooth_weights(e_low, e_high, third):
    twice = third + third
    middle = e_low * e_high + (third * third * (4.0 / 3.0) + WENO_EPS)
    q_a = rcp(middle - e_low * twice)
    q_b = rcp(middle)
    q_c = rcp(middle + e_high * twice)
    return q_a * q_a, 6.0 * (q_b * q_b), q_c * q_c


def biased_parts(wa_next, wb, wc_prev, t_prev, t_here, t_next):
    x = wc_prev * (t_here - t_prev)
    y = wa_next * (t_next - t_here)
    both = x + y
    both = both + both
    total = (wa_next + wb) + wc_prev
    left = t_here + (both + y) * rcp(total + (wa_next + wa_next))
    right = t_here - (both + x) * rcp(total + (wc_prev + wc_prev))
    return left, right


def upwind_square(centre, left, right, sigma):
    return upwind_pair(centre - left, right - centre, sigma)


def upwind_pair(left, right_back, sigma):
    best = jnp.maximum(sigma * left, sigma * right_back)
    best = jnp.maximum(best, 0.0)
    return best * best


def sigma_of(value):
    return jnp.where(value > 0.0, F32(1.0), F32(-1.0))


def from_values(v_m, v_0, v_1, v_2):
    d_m, d_0, d_1 = v_0 - v_m, v_1 - v_0, v_2 - v_1
    e_0, e_1 = d_0 - d_m, d_1 - d_0
    return e_0, e_1, e_1 - e_0


def lane_down(part):
    return pltpu.roll(part, 1, 1)


def lane_up(part):
    return pltpu.roll(part, 127, 1)


def z_stage_weights(even, odd, even_down, odd_down, even_up, odd_up):
    v = {-2: even_down, -1: odd_down, 0: even, 1: odd, 2: even_up, 3: odd_up}
    d = {k: v[k + 1] - v[k] for k in range(-2, 3)}
    e = {k: d[k] - d[k - 1] for k in range(-1, 3)}
    t = {k: e[k + 1] - e[k] for k in range(-1, 2)}
    w_0 = smooth_weights(e[0], e[1], t[0])
    w_1 = smooth_weights(e[1], e[2], t[1])
    return (
        w_1[0], w_0[1], lane_down(w_1[2]), t[-1], t[0], t[1],
        lane_up(w_0[0]), w_1[1], w_0[2], lane_up(t[0]),
        3.0 * (d[-1] + d[0]), 3.0 * (d[0] + d[1]),
    )


def z_stage_parts(wa_0, wb_0, wc_0, t_m, t_0, t_1, wa_1, wb_1, wc_1, t_2, centre_0, centre_1):
    left_0, right_0 = biased_parts(wa_0, wb_0, wc_0, t_m, t_0, t_1)
    left_1, right_1 = biased_parts(wa_1, wb_1, wc_1, t_0, t_1, t_2)
    return centre_0, lane_down(left_1), right_0 - centre_0, centre_1 - left_0, right_1 - centre_1


def edge_column(window, u_ref, p_ref, u_row, p_row, sigma):
    def rows(start):
        return window[pl.ds(start, 8), :]

    e_0, e_1, t = from_values(rows(u_row - 1), rows(u_row), rows(u_row + 1), rows(u_row + 2))
    w_a, w_b, w_c = smooth_weights(e_0, e_1, t)
    for slot, part in enumerate((w_a, w_b, w_c, t)):
        u_ref[slot, pl.ds(u_row, 8), :] = part
    left, right = biased_parts(
        u_ref[0, pl.ds(p_row + 1, 8), :],
        u_ref[1, pl.ds(p_row, 8), :],
        u_ref[2, pl.ds(p_row - 1, 8), :],
        u_ref[3, pl.ds(p_row - 1, 8), :],
        u_ref[3, pl.ds(p_row, 8), :],
        u_ref[3, pl.ds(p_row + 1, 8), :],
    )
    p_ref[0, pl.ds(p_row, 8), :] = left
    p_ref[1, pl.ds(p_row, 8), :] = right
    centre = 3.0 * (rows(9) - rows(7))
    return upwind_square(
        centre, p_ref[0, pl.ds(7, 8), :], p_ref[1, pl.ds(8, 8), :], sigma
    )


def z_faces(source, zlo, zhi):
    for chunk in range(CX // 8):
        columns = slice(8 * CY * chunk, 8 * CY * (chunk + 1))
        for parity in range(2):
            part = source[8 * chunk : 8 * chunk + 8, :, 128 * parity : 128 * parity + 128]
            part = part.reshape(8 * CY, 128).T
            for k in range(4):
                zlo[2 * k + parity : 2 * k + parity + 1, columns] = part[k : k + 1]
                zhi[2 * k + parity : 2 * k + parity + 1, columns] = part[124 + k : 125 + k]


def y_faces(source, ylo, yhi, width):
    for x in range(CX):
        for k in range(width):
            ylo[k, x : x + 1, :] = source[x, k : k + 1, :]
            yhi[k, x : x + 1, :] = source[x, CY - width + k : CY - width + 1 + k, :]


def write_swap(parity, low, high, out_a, out_b):
    odd = parity == 1
    out_a[...] = jnp.where(odd, low, high)
    out_b[...] = jnp.where(odd, high, low)


def write_faces(parity, source, xa, xb, ya, yb, za, zb, yf, zf):
    y_faces(source, yf.at[0], yf.at[1], 3)
    write_swap(parity[1], yf[0], yf[1], ya, yb)
    write_swap(parity[0], source[0:3], source[CX - 3 : CX], xa, xb)
    z_faces(source, zf.at[0], zf.at[1])
    write_swap(parity[2], zf[0], zf[1], za, zb)


def low_high(parity, part_a, part_b):
    odd = parity == 1
    return jnp.where(odd, part_a, part_b), jnp.where(odd, part_b, part_a)


def pack_kernel(parity, phi, mixed, sigma, pace, xa, xb, ya, yb, za, zb, turned, yf, zf):
    for chunk in range(CX // 8):
        planes = slice(8 * chunk, 8 * chunk + 8)
        for half in range(2):
            part = phi[planes, :, 128 * half : 128 * half + 128]
            part = part.reshape(8 * CY, 128).T
            for c in range(3):
                turned[c, 128 * half : 128 * half + 128, :] = part[:, 128 * c : 128 * c + 128]
        for which in range(2):
            part = [turned[c, pl.ds(which, 128, stride=2), :].T for c in range(3)]
            part = jnp.concatenate(part, axis=0)
            mixed[planes, :, 128 * which : 128 * which + 128] = part.reshape(8, CY, 128)
    def signs(x, carry):
        value = mixed[x]
        sigma[x] = sigma_of(value)
        pace[x] = (0.05 * value) * lax.rsqrt(value * value + 1.0)
        return carry

    lax.fori_loop(0, CX, signs, 0)
    write_faces(parity, mixed, xa, xb, ya, yb, za, zb, yf, zf)


def unpack_kernel(mixed, out, turned):
    for chunk in range(CX // 8):
        planes = slice(8 * chunk, 8 * chunk + 8)
        for parity in range(2):
            part = mixed[planes, :, 128 * parity : 128 * parity + 128]
            part = part.reshape(8 * CY, 128).T
            for c in range(3):
                turned[c, pl.ds(parity, 128, stride=2), :] = part[:, 128 * c : 128 * c + 128]
        for half in range(2):
            part = [turned[c, 128 * half : 128 * half + 128, :].T for c in range(3)]
            part = jnp.concatenate(part, axis=0)
            out[planes, :, 128 * half : 128 * half + 128] = part.reshape(8, CY, 128)


def step_kernel(
    last,
    parity, sigma_in, pace, za0, zb0, v, za_own, zb_own, xa_in, xb_in, ya_in, yb_in, za_in, zb_in,
    out, xa, xb, ya, yb, za, zb,
    vs, summed, u_ref, p_ref, window, zu_ref, zp_ref, edges, fixes, yf, zf, xh,
    rolled, zs, zp, tots,
):
    def fill(x, carry):
        for zt in range(2):
            vs[zt, x, 8 : 8 + CY, :] = v[x, :, pl.ds(128 * zt, 128)]
        return carry

    lax.fori_loop(0, CX, fill, 0)
    yf[0], yf[1] = low_high(parity[1], ya_in[...], yb_in[...])
    for x in range(CX):
        for zt in range(2):
            lanes = slice(128 * zt, 128 * zt + 128)
            for k in range(3):
                vs[zt, x, 5 + k : 6 + k, :] = yf[0, k, x : x + 1, lanes]
                vs[zt, x, 8 + CY + k : 9 + CY + k, :] = yf[1, k, x : x + 1, lanes]
    xh[0], xh[1] = low_high(parity[0], xa_in[...], xb_in[...])

    z_low, z_high = low_high(parity[2], za_in[...], zb_in[...])
    zlo0, zhi0 = low_high(parity[2], za0[...], zb0[...])
    zlo_own, zhi_own = low_high(parity[2], za_own[...], zb_own[...])
    window[5:8, :] = z_low[5:8]
    window[8:16, :] = zlo_own
    fixed = edge_column(window, zu_ref, zp_ref, 6, 7, sigma_of(zlo0))
    for half, lane_at, cell_at in ((0, 0, 0), (0, 1, 2), (1, 0, 1)):
        edges[half, lane_at : lane_at + 1, :] = fixed[cell_at : cell_at + 1]
    window[8:16, :] = zhi_own
    window[16:19, :] = z_high[0:3]
    fixed = edge_column(window, zu_ref, zp_ref, 9, 8, sigma_of(zhi0))
    for half, lane_at, cell_at in ((0, 127, 6), (1, 126, 5), (1, 127, 7)):
        edges[half, lane_at : lane_at + 1, :] = fixed[cell_at : cell_at + 1]
    for half in range(2):
        fixes[half] = edges[half].T

    def x_pass(yt, carry):
        row = pl.multiple_of(8 * yt, 8)
        for zt in range(2):
            lanes = pl.ds(128 * zt, 128)

            def cell(x):
                if x < 0:
                    return xh[0, 3 + x, pl.ds(row, 8), lanes]
                if x >= CX:
                    return xh[1, x - CX, pl.ds(row, 8), lanes]
                return v[x, pl.ds(row, 8), lanes]

            d, e, t, weights, lefts, rights = {}, {}, {}, {}, {}, {}
            d[-3] = cell(-2) - cell(-3)
            d[-2] = cell(-1) - cell(-2)
            e[-2] = d[-2] - d[-3]
            for j in range(-2, CX + 1):
                d[j + 1] = cell(j + 2) - cell(j + 1)
                e[j + 1] = d[j + 1] - d[j]
                t[j] = e[j + 1] - e[j]
                weights[j] = smooth_weights(e[j], e[j + 1], t[j])
                p = j - 1
                if p >= -1:
                    lefts[p], rights[p] = biased_parts(
                        weights[p + 1][0], weights[p][1], weights[p - 1][2], t[p - 1], t[p], t[p + 1]
                    )
                if p >= 0:
                    sigma = sigma_in[p, pl.ds(row, 8), lanes]
                    centre = 3.0 * (d[p - 1] + d[p])
                    summed[zt, p, pl.ds(row, 8), :] = upwind_square(
                        centre, lefts[p - 1], rights[p], sigma
                    )
        return carry

    lax.fori_loop(0, YT, x_pass, 0)

    lane = lax.broadcasted_iota(jnp.int32, (8, 128), 1)
    fix_even = (lane < 2) | (lane == 127)
    fix_odd = (lane < 1) | (lane > 125)

    def y_weights(x, zt, k):
        start = 6 + 8 * k
        e_0, e_1, t = from_values(
            *[vs[zt, x, pl.ds(start + shift, 8), :] for shift in (-1, 0, 1, 2)]
        )
        w_a, w_b, w_c = smooth_weights(e_0, e_1, t)
        for slot, part in enumerate((w_a, w_b, w_c, t)):
            u_ref[zt, slot, pl.ds(8 * k, 8), :] = part

    def y_parts(zt, k):
        def read(slot, row):
            return u_ref[zt, slot, pl.ds(row, 8), :]

        row = 8 * k + 1
        left, right = biased_parts(
            read(0, row + 1), read(1, row), read(2, row - 1),
            read(3, row - 1), read(3, row), read(3, row + 1),
        )
        p_ref[zt, 0, pl.ds(8 * k, 8), :] = left
        p_ref[zt, 1, pl.ds(8 * k, 8), :] = right

    def tile(x, zt, k):
        return v[x, 8 * k : 8 * k + 8, 128 * zt : 128 * zt + 128]

    def sigma_at(x, zt, k):
        return sigma_in[x, 8 * k : 8 * k + 8, 128 * zt : 128 * zt + 128]

    def stage_0(x):
        for k in range(YT):
            rows = slice(8 * k, 8 * k + 8)
            for slot, part in enumerate((tile(x, 0, k), tile(x, 1, k))):
                rolled[slot, rows, :] = lane_down(part)
                rolled[2 + slot, rows, :] = lane_up(part)
        for zt in range(2):
            for k in range(YT + 1):
                y_weights(x, zt, k)

    def stage_1(x):
        for k in range(YT):
            rows = slice(8 * k, 8 * k + 8)
            parts = z_stage_weights(
                tile(x, 0, k), tile(x, 1, k), *[rolled[slot, rows, :] for slot in range(4)]
            )
            for slot, part in enumerate(parts):
                zs[slot, rows, :] = part
        for zt in range(2):
            for k in range(YT + 1):
                y_parts(zt, k)

    def stage_2(x):
        for k in range(YT):
            rows = slice(8 * k, 8 * k + 8)
            parts = z_stage_parts(*[zs[slot, rows, :] for slot in range(12)])
            for slot, part in enumerate(parts):
                zp[slot, rows, :] = part
        for zt in range(2):
            for k in range(YT):
                rows = slice(8 * k, 8 * k + 8)
                centre = 3.0 * (
                    vs[zt, x, 9 + 8 * k : 17 + 8 * k, :] - vs[zt, x, 7 + 8 * k : 15 + 8 * k, :]
                )
                tots[zt, rows, :] = summed[zt, x, rows, :] + upwind_square(
                    centre, p_ref[zt, 0, rows, :], p_ref[zt, 1, 8 * k + 1 : 8 * k + 9, :],
                    sigma_at(x, zt, k),
                )

    def stage_3(x):
        flat = pl.multiple_of(x * CY, 8)
        for k in range(YT):
            rows = slice(8 * k, 8 * k + 8)
            for zt in range(2):
                sigma = sigma_at(x, zt, k)
                if zt == 0:
                    along = upwind_pair(zp[0, rows, :] - zp[1, rows, :], zp[2, rows, :], sigma)
                    edge = fix_even
                else:
                    along = upwind_pair(zp[3, rows, :], zp[4, rows, :], sigma)
                    edge = fix_odd
                along = jnp.where(edge, fixes[zt, pl.ds(flat + 8 * k, 8), :], along)
                total = tots[zt, rows, :] + along
                root = total * lax.rsqrt(jnp.maximum(total, 1e-30))
                lanes = slice(128 * zt, 128 * zt + 128)
                out[x, rows, lanes] = v[x, rows, lanes] - pace[x, rows, lanes] * (root - 6.0)

    stages = (stage_3, stage_2, stage_1, stage_0)

    def run(at, low, high):
        for delay, stage in zip((3, 2, 1, 0), stages):
            if low <= delay <= high:
                stage(at - delay)

    def yz_pass(at, carry):
        run(at, 0, 3)
        return carry

    for at in range(3):
        run(at, 0, at)
    lax.fori_loop(3, CX, yz_pass, 0)
    for at in range(3):
        run(CX + at, at + 1, 3)
    if last:
        xa_out, xb_out = (out[CX - 1 : CX], out[0:1])
        write_swap(parity[0], xb_out, xa_out, xa, xb)
        y_faces(out, ya, yb, 1)
        z_faces(out, za, zb)
    else:
        write_faces(parity, out, xa, xb, ya, yb, za, zb, yf, zf)


def face_shapes(width):
    shapes = [(width, CY, CZ)] * 2 + [(width, CX, CZ)] * 2 + [(8, ROWS)] * 2
    return [jax.ShapeDtypeStruct(shape, F32) for shape in shapes]


BLOCK = jax.ShapeDtypeStruct((CX, CY, CZ), F32)
FACE_SCRATCH = [pltpu.VMEM((2, 3, CX, CZ), F32), pltpu.VMEM((2, 8, ROWS), F32)]


def vmem_specs(count):
    return [pl.BlockSpec(memory_space=pltpu.VMEM)] * count


def parity_specs(count):
    return [pl.BlockSpec(memory_space=pltpu.SMEM)] + vmem_specs(count)


def pack(parity, phi):
    return pl.pallas_call(
        pack_kernel,
        out_shape=[BLOCK] * 3 + face_shapes(3),
        in_specs=parity_specs(1),
        out_specs=vmem_specs(9),
        scratch_shapes=[pltpu.VMEM((3, CZ, 128), F32)] + FACE_SCRATCH,
        compiler_params=pltpu.CompilerParams(vmem_limit_bytes=VMEM_LIMIT),
        name="pack",
    )(parity, phi)


def unpack(mixed):
    return pl.pallas_call(
        unpack_kernel,
        out_shape=BLOCK,
        in_specs=vmem_specs(1),
        out_specs=vmem_specs(1)[0],
        scratch_shapes=[pltpu.VMEM((3, CZ, 128), F32)],
        compiler_params=pltpu.CompilerParams(vmem_limit_bytes=VMEM_LIMIT),
        name="unpack",
    )(mixed)


def step(parity, sigma_in, pace, za0, zb0, v, za_own, zb_own, halos, last):
    return pl.pallas_call(
        functools.partial(step_kernel, last),
        out_shape=[BLOCK] + face_shapes(1 if last else 3),
        in_specs=parity_specs(13),
        out_specs=vmem_specs(7),
        scratch_shapes=[
            pltpu.VMEM((2, CX, 64, 128), F32),
            pltpu.VMEM((2, CX, CY, 128), F32),
            pltpu.VMEM((2, 4, 64, 128), F32),
            pltpu.VMEM((2, 2, 64, 128), F32),
            pltpu.VMEM((24, ROWS), F32),
            pltpu.VMEM((4, 24, ROWS), F32),
            pltpu.VMEM((2, 24, ROWS), F32),
            pltpu.VMEM((2, 128, ROWS), F32),
            pltpu.VMEM((2, ROWS, 128), F32),
        ]
        + FACE_SCRATCH
        + [
            pltpu.VMEM((2, 3, CY, CZ), F32),
            pltpu.VMEM((4, CY, 128), F32),
            pltpu.VMEM((12, CY, 128), F32),
            pltpu.VMEM((5, CY, 128), F32),
            pltpu.VMEM((2, CY, 128), F32),
        ],
        compiler_params=pltpu.CompilerParams(vmem_limit_bytes=VMEM_LIMIT),
        name="step",
    )(parity, sigma_in, pace, za0, zb0, v, za_own, zb_own, *halos)


HALF_COS = [
    0.9999999991256178, -0.23370050635094053, 0.019968606689123116,
    -0.0008935362743290266, 2.3601076640059624e-05,
]
BAND_SQUARE = 1.5 * 1.5


def half_cosine(value):
    square = jnp.minimum(value * value, BAND_SQUARE)
    shape = F32(HALF_COS[4] / BAND_SQUARE**5)
    for k in (3, 2, 1, 0):
        shape = shape * square + F32(HALF_COS[k] / BAND_SQUARE ** (k + 1))
    return (BAND_SQUARE - square) * shape


def five_terms(centre, keep, dx, sx, dy, sy, dz, sz, dxy, dxz, dyz):
    twice = centre + centre
    xx, yy, zz = dx * dx, dy * dy, dz * dz
    squares = jnp.maximum(xx + yy + zz, 1.0)
    root = lax.rsqrt(squares)
    bend = (sx - twice) * (yy + zz) + (sy - twice) * (xx + zz) + (sz - twice) * (xx + yy)
    bend = bend - 0.5 * (dx * (dy * dxy + dz * dxz) + dy * dz * dyz)
    cosine = half_cosine(centre)
    spread = cosine * cosine
    if keep is not None:
        spread = jnp.where(keep, spread, 0.0)
    return (
        spread * (squares * root),
        spread * bend * (root * root),
        spread * dx,
        spread * dy,
        spread * dz,
    )


def brick_kernel(v, x_low, x_high, y_low, y_high, z_window, places, z_places, record, vs, stack):
    def fill(x, carry):
        for zt in range(2):
            vs[zt, x + 1, 8 : 8 + CY, :] = v[x, :, pl.ds(128 * zt, 128)]
        return carry

    lax.fori_loop(0, CX, fill, 0)
    for zt in range(2):
        lanes = slice(128 * zt, 128 * zt + 128)
        vs[zt, 0, 8 : 8 + CY, :] = x_low[0, :, lanes]
        vs[zt, CX + 1, 8 : 8 + CY, :] = x_high[0, :, lanes]
        for x in range(CX + 2):
            vs[zt, x, 7:8, :] = y_low[x : x + 1, lanes]
            vs[zt, x, 8 + CY : 9 + CY, :] = y_high[x : x + 1, lanes]

    lane = lax.broadcasted_iota(jnp.int32, (8, 128), 1)
    keeps = (lane != 0, lane != 127)

    def down(part):
        return pltpu.roll(part, 1, 1)

    def up(part):
        return pltpu.roll(part, 127, 1)

    def neighbours(pair):
        return ((down(pair[1]), pair[1]), (pair[0], up(pair[0])))

    def tile_terms(x, k):
        def read(zt, plane, shift):
            return vs[zt, plane, pl.ds(8 + 8 * k + shift, 8), :]

        two = range(2)
        centre = [read(zt, x + 1, 0) for zt in two]
        high = [read(zt, x + 2, 0) for zt in two]
        low = [read(zt, x, 0) for zt in two]
        dx = [high[zt] - low[zt] for zt in two]
        sx = [high[zt] + low[zt] for zt in two]
        right = [read(zt, x + 1, 1) for zt in two]
        left = [read(zt, x + 1, -1) for zt in two]
        dy = [right[zt] - left[zt] for zt in two]
        sy = [right[zt] + left[zt] for zt in two]
        dxy = [
            (read(zt, x + 2, 1) - read(zt, x, 1)) - (read(zt, x + 2, -1) - read(zt, x, -1))
            for zt in two
        ]
        around, dx_around, dy_around = neighbours(centre), neighbours(dx), neighbours(dy)
        results = []
        for zt in two:
            results.append(
                five_terms(
                    centre[zt], keeps[zt], dx[zt], sx[zt], dy[zt], sy[zt],
                    around[zt][1] - around[zt][0], around[zt][1] + around[zt][0],
                    dxy[zt],
                    dx_around[zt][1] - dx_around[zt][0],
                    dy_around[zt][1] - dy_around[zt][0],
                )
            )
        return [results[0][n] + results[1][n] for n in range(5)]

    zeros = jnp.zeros((8, 128), F32)
    for bx in range(2):

        def body(step_at, sums):
            sums = list(sums)
            for sub in range(2):
                x = BRICK * bx + 2 * step_at + sub
                for k in range(YT):
                    parts = tile_terms(x, k)
                    for n in range(5):
                        slot = 5 * (k // 2) + n
                        sums[slot] = sums[slot] + parts[n]
            return tuple(sums)

        sums = lax.fori_loop(0, BRICK // 2, body, (zeros,) * 15)
        for by in range(3):
            for n in range(5):
                row = 8 * (3 * bx + by) + n
                stack[row : row + 1, :] = jnp.sum(sums[5 * by + n], axis=0, keepdims=True)
            row = 8 * (3 * bx + by)
            stack[row + 5 : row + 8, :] = jnp.zeros((3, 128), F32)

    total = jnp.zeros((8, SLOTS), F32)
    for b in range(6):
        total = total + jnp.dot(
            stack[8 * b : 8 * b + 8, :], places[b],
            precision=lax.Precision.HIGHEST, preferred_element_type=F32,
        )
    for side in range(2):
        planes = [z_window[3 * side + k] for k in range(3)]

        def cut(plane, step_x, step_y):
            return planes[plane][1 + step_x : 33 + step_x, 1 + step_y : 49 + step_y]

        high, low = cut(1, 1, 0), cut(1, -1, 0)
        right, left = cut(1, 0, 1), cut(1, 0, -1)
        over, under = cut(2, 0, 0), cut(0, 0, 0)
        terms = five_terms(
            cut(1, 0, 0), None,
            high - low, high + low, right - left, right + left, over - under, over + under,
            (cut(1, 1, 1) - cut(1, -1, 1)) - (cut(1, 1, -1) - cut(1, -1, -1)),
            (cut(2, 1, 0) - cut(2, -1, 0)) - (cut(0, 1, 0) - cut(0, -1, 0)),
            (cut(2, 0, 1) - cut(2, 0, -1)) - (cut(0, 0, 1) - cut(0, 0, -1)),
        )
        for bx in range(2):
            rows = [jnp.sum(term[16 * bx : 16 * bx + 16], axis=0, keepdims=True) for term in terms]
            rows = jnp.concatenate(rows + [jnp.zeros((3, CY), F32)], axis=0)
            total = total + jnp.dot(
                rows, z_places[2 * side + bx],
                precision=lax.Precision.HIGHEST, preferred_element_type=F32,
            )
    scale = 2.0 / 3.0 / (BRICK * BRICK)
    row = lax.broadcasted_iota(jnp.int32, (8, SLOTS), 0)
    record[...] = total * jnp.where(row == 1, F32(scale), F32(0.5 * scale))


def bricks(v, x_low, x_high, y_low, y_high, z_window, places, z_places):
    return pl.pallas_call(
        brick_kernel,
        out_shape=jax.ShapeDtypeStruct((8, SLOTS), F32),
        in_specs=vmem_specs(8),
        out_specs=vmem_specs(1)[0],
        scratch_shapes=[
            pltpu.VMEM((2, CX + 2, 64, 128), F32),
            pltpu.VMEM((48, 128), F32),
        ],
        compiler_params=pltpu.CompilerParams(vmem_limit_bytes=VMEM_LIMIT),
        name="bricks",
    )(v, x_low, x_high, y_low, y_high, z_window, places, z_places)


def swap(value, axis, phase):
    count = lax.axis_size(axis)
    if phase == 0:
        pairs = [(i, i ^ 1) for i in range(count)]
    else:
        pairs = [(i, (i - 1 if i % 2 == 0 else i + 1) % count) for i in range(count)]
    return lax.ppermute(value, axis, pairs)


def place_tables(device_ids, live_count, targets):
    entries = jnp.arange(device_ids.shape[0], dtype=jnp.int32)
    is_live = entries < live_count
    earlier = entries[None, :] < entries[:, None]
    same_owner = targets[None, :] == targets[:, None]
    rank = jnp.sum((earlier & same_owner & is_live[None, :]).astype(jnp.int32), axis=1)
    columns = jnp.where(is_live, targets * 2 + rank, SLOTS)
    count = (CX // BRICK) * (CY // BRICK) * (CZ // BRICK)
    brick = jnp.arange(count, dtype=jnp.int32)
    slot = jnp.arange(SLOTS, dtype=jnp.int32)
    hits = (device_ids[:, None, None] == brick[None, :, None]) & (
        columns[:, None, None] == slot[None, None, :]
    )
    table = jnp.any(hits, axis=0).astype(F32)
    table = table.reshape(2, 3, 16, SLOTS)
    places = jnp.repeat(table.reshape(6, 16, SLOTS), 8, axis=1)
    z_places = [
        jnp.repeat(table[bx, :, end], BRICK, axis=0) for end in (0, 15) for bx in range(2)
    ]
    return places, jnp.stack(z_places, axis=0)


def exchange(faces):
    xa, xb, ya, yb, za, zb = faces
    yb = swap(yb, "gy", 1)
    ya = swap(ya, "gy", 0)
    zb = swap(zb, "gz", 1)
    za = swap(za, "gz", 0)
    xb = swap(xb, "gx", 1)
    xa = swap(xa, "gx", 0)
    return xa, xb, ya, yb, za, zb


def exchange_pair(low, high, axis, odd):
    part_b = swap(jnp.where(odd, high, low), axis, 1)
    part_a = swap(jnp.where(odd, low, high), axis, 0)
    return jnp.where(odd, part_a, part_b), jnp.where(odd, part_b, part_a)


def per_device(phi_start, band_ids, band_count, owners):
    parity = jnp.stack([lax.axis_index(name) % 2 for name in ("gx", "gy", "gz")])
    parity = parity.astype(jnp.int32)
    odd_x, odd_y, odd_z = [parity[k] == 1 for k in range(3)]
    places, z_places = place_tables(
        band_ids.reshape(-1), band_count.reshape(()), owners.reshape(-1)
    )
    v, sigma, pace, *faces = pack(parity, phi_start)
    za0, zb0 = faces[4:]
    for number in range(STEPS):
        v, *faces = step(
            parity, sigma, pace, za0, zb0, v, faces[4], faces[5], exchange(faces),
            number == STEPS - 1,
        )
    level_set = unpack(v)

    xa, xb, ylo, yhi, zlo, zhi = faces
    xb = swap(xb, "gx", 1)
    xa = swap(xa, "gx", 0)
    x_low, x_high = jnp.where(odd_x, xa, xb), jnp.where(odd_x, xb, xa)
    first = jnp.concatenate([x_low[:, 0], ylo[0], x_high[:, 0]], axis=0)
    last = jnp.concatenate([x_low[:, CY - 1], yhi[0], x_high[:, CY - 1]], axis=0)
    y_low, y_high = exchange_pair(first, last, "gy", odd_y)

    def plane(body, lane):
        middle = jnp.concatenate(
            [x_low[:, :, lane], body.reshape(CX, CY), x_high[:, :, lane]], axis=0
        )
        return jnp.concatenate([y_low[:, lane, None], middle, y_high[:, lane, None]], axis=1)

    bottom, above = plane(zlo[0], 0), plane(zlo[1], 128)
    below, top = plane(zhi[6], 127), plane(zhi[7], 255)
    under, over = exchange_pair(bottom, top, "gz", odd_z)
    z_window = jnp.stack([under, bottom, above, below, top, over], axis=0)
    record = bricks(v, x_low, x_high, y_low, y_high, z_window, places, z_places)
    totals = lax.all_to_all(record[:5], ("gx", "gy"), split_axis=1, concat_axis=1, tiled=True)
    return level_set, totals.reshape(1, 1, 1, 5, SLOTS)


def solution(mesh):
    placed = (
        P("gx", "gy", "gz"),
        P("gx", "gy", "gz", None),
        P("gx", "gy", "gz"),
        P("gx", "gy", "gz", None),
    )
    return jax.shard_map(
        per_device,
        mesh=mesh,
        in_specs=placed,
        out_specs=(P("gx", "gy", "gz"), P("gx", "gy", "gz", None, None)),
        check_vma=False,
    )
```

```python
import functools

import jax
import jax.numpy as jnp
from jax import lax
from jax.experimental import pallas as pl
from jax.experimental.pallas import tpu as pltpu
from jax.sharding import PartitionSpec as P

STEPS = 3
BRICK = 16
SLOTS = 64
CX, CY, CZ = 32, 48, 256
ROWS = CX * CY
YT = CY // 8
WENO_EPS = 1e-06
F32 = jnp.float32
VMEM_LIMIT = 16 * 1024 * 1024


def rcp(value):
    return pltpu.reciprocal(value, approx=True)


def smooth_weights(e_low, e_high, third):
    twice = third + third
    middle = e_low * e_high + (third * third * (4.0 / 3.0) + WENO_EPS)
    q_a = rcp(middle - e_low * twice)
    q_b = rcp(middle)
    q_c = rcp(middle + e_high * twice)
    return q_a * q_a, 6.0 * (q_b * q_b), q_c * q_c


def biased_parts(wa_next, wb, wc_prev, t_prev, t_here, t_next):
    x = wc_prev * (t_here - t_prev)
    y = wa_next * (t_next - t_here)
    both = x + y
    both = both + both
    total = (wa_next + wb) + wc_prev
    left = t_here + (both + y) * rcp(total + (wa_next + wa_next))
    right = t_here - (both + x) * rcp(total + (wc_prev + wc_prev))
    return left, right


def upwind_square(centre, left, right, sigma):
    return upwind_pair(centre - left, right - centre, sigma)


def upwind_pair(left, right_back, sigma):
    best = jnp.maximum(sigma * left, sigma * right_back)
    best = jnp.maximum(best, 0.0)
    return best * best


def sigma_of(value):
    return jnp.where(value > 0.0, F32(1.0), F32(-1.0))


def from_values(v_m, v_0, v_1, v_2):
    d_m, d_0, d_1 = v_0 - v_m, v_1 - v_0, v_2 - v_1
    e_0, e_1 = d_0 - d_m, d_1 - d_0
    return e_0, e_1, e_1 - e_0


def lane_down(part):
    return pltpu.roll(part, 1, 1)


def lane_up(part):
    return pltpu.roll(part, 127, 1)


def z_stage_weights(even, odd, even_down, odd_down, even_up, odd_up):
    v = {-2: even_down, -1: odd_down, 0: even, 1: odd, 2: even_up, 3: odd_up}
    d = {k: v[k + 1] - v[k] for k in range(-2, 3)}
    e = {k: d[k] - d[k - 1] for k in range(-1, 3)}
    t = {k: e[k + 1] - e[k] for k in range(-1, 2)}
    w_0 = smooth_weights(e[0], e[1], t[0])
    w_1 = smooth_weights(e[1], e[2], t[1])
    return (
        w_1[0], w_0[1], lane_down(w_1[2]), t[-1], t[0], t[1],
        lane_up(w_0[0]), w_1[1], w_0[2], lane_up(t[0]),
        3.0 * (d[-1] + d[0]), 3.0 * (d[0] + d[1]),
    )


def z_stage_parts(wa_0, wb_0, wc_0, t_m, t_0, t_1, wa_1, wb_1, wc_1, t_2, centre_0, centre_1):
    left_0, right_0 = biased_parts(wa_0, wb_0, wc_0, t_m, t_0, t_1)
    left_1, right_1 = biased_parts(wa_1, wb_1, wc_1, t_0, t_1, t_2)
    return centre_0, lane_down(left_1), right_0 - centre_0, centre_1 - left_0, right_1 - centre_1


def edge_column(window, u_ref, p_ref, u_row, p_row, sigma):
    def rows(start):
        return window[pl.ds(start, 8), :]

    e_0, e_1, t = from_values(rows(u_row - 1), rows(u_row), rows(u_row + 1), rows(u_row + 2))
    w_a, w_b, w_c = smooth_weights(e_0, e_1, t)
    for slot, part in enumerate((w_a, w_b, w_c, t)):
        u_ref[slot, pl.ds(u_row, 8), :] = part
    left, right = biased_parts(
        u_ref[0, pl.ds(p_row + 1, 8), :],
        u_ref[1, pl.ds(p_row, 8), :],
        u_ref[2, pl.ds(p_row - 1, 8), :],
        u_ref[3, pl.ds(p_row - 1, 8), :],
        u_ref[3, pl.ds(p_row, 8), :],
        u_ref[3, pl.ds(p_row + 1, 8), :],
    )
    p_ref[0, pl.ds(p_row, 8), :] = left
    p_ref[1, pl.ds(p_row, 8), :] = right
    centre = 3.0 * (rows(9) - rows(7))
    return upwind_square(
        centre, p_ref[0, pl.ds(7, 8), :], p_ref[1, pl.ds(8, 8), :], sigma
    )


def z_faces(source, zlo, zhi):
    for chunk in range(CX // 8):
        columns = slice(8 * CY * chunk, 8 * CY * (chunk + 1))
        for parity in range(2):
            part = source[8 * chunk : 8 * chunk + 8, :, 128 * parity : 128 * parity + 128]
            part = part.reshape(8 * CY, 128).T
            for k in range(4):
                zlo[2 * k + parity : 2 * k + parity + 1, columns] = part[k : k + 1]
                zhi[2 * k + parity : 2 * k + parity + 1, columns] = part[124 + k : 125 + k]


def y_faces(source, ylo, yhi, width):
    for x in range(CX):
        for k in range(width):
            ylo[k, x : x + 1, :] = source[x, k : k + 1, :]
            yhi[k, x : x + 1, :] = source[x, CY - width + k : CY - width + 1 + k, :]


def write_swap(parity, low, high, out_a, out_b):
    odd = parity == 1
    out_a[...] = jnp.where(odd, low, high)
    out_b[...] = jnp.where(odd, high, low)


def write_faces(parity, source, xa, xb, ya, yb, za, zb, yf, zf):
    y_faces(source, yf.at[0], yf.at[1], 3)
    write_swap(parity[1], yf[0], yf[1], ya, yb)
    write_swap(parity[0], source[0:3], source[CX - 3 : CX], xa, xb)
    z_faces(source, zf.at[0], zf.at[1])
    write_swap(parity[2], zf[0], zf[1], za, zb)


def low_high(parity, part_a, part_b):
    odd = parity == 1
    return jnp.where(odd, part_a, part_b), jnp.where(odd, part_b, part_a)


def pack_kernel(parity, phi, mixed, sigma, pace, xa, xb, ya, yb, za, zb, turned, yf, zf):
    for chunk in range(CX // 8):
        planes = slice(8 * chunk, 8 * chunk + 8)
        for half in range(2):
            part = phi[planes, :, 128 * half : 128 * half + 128]
            part = part.reshape(8 * CY, 128).T
            for c in range(3):
                turned[c, 128 * half : 128 * half + 128, :] = part[:, 128 * c : 128 * c + 128]
        for which in range(2):
            part = [turned[c, pl.ds(which, 128, stride=2), :].T for c in range(3)]
            part = jnp.concatenate(part, axis=0)
            mixed[planes, :, 128 * which : 128 * which + 128] = part.reshape(8, CY, 128)
    def signs(x, carry):
        value = mixed[x]
        sigma[x] = sigma_of(value)
        pace[x] = (0.05 * value) * lax.rsqrt(value * value + 1.0)
        return carry

    lax.fori_loop(0, CX, signs, 0)
    write_faces(parity, mixed, xa, xb, ya, yb, za, zb, yf, zf)


def unpack_kernel(mixed, out, turned):
    for chunk in range(CX // 8):
        planes = slice(8 * chunk, 8 * chunk + 8)
        for parity in range(2):
            part = mixed[planes, :, 128 * parity : 128 * parity + 128]
            part = part.reshape(8 * CY, 128).T
            for c in range(3):
                turned[c, pl.ds(parity, 128, stride=2), :] = part[:, 128 * c : 128 * c + 128]
        for half in range(2):
            part = [turned[c, 128 * half : 128 * half + 128, :].T for c in range(3)]
            part = jnp.concatenate(part, axis=0)
            out[planes, :, 128 * half : 128 * half + 128] = part.reshape(8, CY, 128)


def step_kernel(
    last,
    parity, sigma_in, pace, za0, zb0, v, za_own, zb_own, xa_in, xb_in, ya_in, yb_in, za_in, zb_in,
    *refs,
):
    faces = 6 if last else 7
    step_body(last, parity, sigma_in, pace, za0, zb0, v, za_own, zb_own, xa_in, xb_in, ya_in,
              yb_in, za_in, zb_in, refs[:faces], *refs[faces:])


def step_body(
    last,
    parity, sigma_in, pace, za0, zb0, v, za_own, zb_own, xa_in, xb_in, ya_in, yb_in, za_in, zb_in,
    outs,
    vs, summed, u_ref, p_ref, window, zu_ref, zp_ref, edges, fixes, yf, zf, xh,
    rolled, zs, zp, tots,
):
    out = outs[0]

    def fill(x, carry):
        for zt in range(2):
            vs[zt, x, 8 : 8 + CY, :] = v[x, :, pl.ds(128 * zt, 128)]
        return carry

    lax.fori_loop(0, CX, fill, 0)
    yf[0], yf[1] = low_high(parity[1], ya_in[...], yb_in[...])
    for x in range(CX):
        for zt in range(2):
            lanes = slice(128 * zt, 128 * zt + 128)
            for k in range(3):
                vs[zt, x, 5 + k : 6 + k, :] = yf[0, k, x : x + 1, lanes]
                vs[zt, x, 8 + CY + k : 9 + CY + k, :] = yf[1, k, x : x + 1, lanes]
    xh[0], xh[1] = low_high(parity[0], xa_in[...], xb_in[...])

    z_low, z_high = low_high(parity[2], za_in[...], zb_in[...])
    zlo0, zhi0 = low_high(parity[2], za0[...], zb0[...])
    zlo_own, zhi_own = low_high(parity[2], za_own[...], zb_own[...])
    window[5:8, :] = z_low[5:8]
    window[8:16, :] = zlo_own
    fixed = edge_column(window, zu_ref, zp_ref, 6, 7, sigma_of(zlo0))
    for half, lane_at, cell_at in ((0, 0, 0), (0, 1, 2), (1, 0, 1)):
        edges[half, lane_at : lane_at + 1, :] = fixed[cell_at : cell_at + 1]
    window[8:16, :] = zhi_own
    window[16:19, :] = z_high[0:3]
    fixed = edge_column(window, zu_ref, zp_ref, 9, 8, sigma_of(zhi0))
    for half, lane_at, cell_at in ((0, 127, 6), (1, 126, 5), (1, 127, 7)):
        edges[half, lane_at : lane_at + 1, :] = fixed[cell_at : cell_at + 1]
    for half in range(2):
        fixes[half] = edges[half].T

    def x_pass(yt, carry):
        row = pl.multiple_of(8 * yt, 8)
        for zt in range(2):
            lanes = pl.ds(128 * zt, 128)

            def cell(x):
                if x < 0:
                    return xh[0, 3 + x, pl.ds(row, 8), lanes]
                if x >= CX:
                    return xh[1, x - CX, pl.ds(row, 8), lanes]
                return v[x, pl.ds(row, 8), lanes]

            d, e, t, weights, lefts, rights = {}, {}, {}, {}, {}, {}
            d[-3] = cell(-2) - cell(-3)
            d[-2] = cell(-1) - cell(-2)
            e[-2] = d[-2] - d[-3]
            for j in range(-2, CX + 1):
                d[j + 1] = cell(j + 2) - cell(j + 1)
                e[j + 1] = d[j + 1] - d[j]
                t[j] = e[j + 1] - e[j]
                weights[j] = smooth_weights(e[j], e[j + 1], t[j])
                p = j - 1
                if p >= -1:
                    lefts[p], rights[p] = biased_parts(
                        weights[p + 1][0], weights[p][1], weights[p - 1][2], t[p - 1], t[p], t[p + 1]
                    )
                if p >= 0:
                    sigma = sigma_in[p, pl.ds(row, 8), lanes]
                    centre = 3.0 * (d[p - 1] + d[p])
                    summed[zt, p, pl.ds(row, 8), :] = upwind_square(
                        centre, lefts[p - 1], rights[p], sigma
                    )
        return carry

    lax.fori_loop(0, YT, x_pass, 0)

    lane = lax.broadcasted_iota(jnp.int32, (8, 128), 1)
    fix_even = (lane < 2) | (lane == 127)
    fix_odd = (lane < 1) | (lane > 125)

    def y_weights(x, zt, k):
        start = 6 + 8 * k
        e_0, e_1, t = from_values(
            *[vs[zt, x, pl.ds(start + shift, 8), :] for shift in (-1, 0, 1, 2)]
        )
        w_a, w_b, w_c = smooth_weights(e_0, e_1, t)
        for slot, part in enumerate((w_a, w_b, w_c, t)):
            u_ref[zt, slot, pl.ds(8 * k, 8), :] = part

    def y_parts(zt, k):
        def read(slot, row):
            return u_ref[zt, slot, pl.ds(row, 8), :]

        row = 8 * k + 1
        left, right = biased_parts(
            read(0, row + 1), read(1, row), read(2, row - 1),
            read(3, row - 1), read(3, row), read(3, row + 1),
        )
        p_ref[zt, 0, pl.ds(8 * k, 8), :] = left
        p_ref[zt, 1, pl.ds(8 * k, 8), :] = right

    def tile(x, zt, k):
        return v[x, 8 * k : 8 * k + 8, 128 * zt : 128 * zt + 128]

    def sigma_at(x, zt, k):
        return sigma_in[x, 8 * k : 8 * k + 8, 128 * zt : 128 * zt + 128]

    def stage_0(x):
        for k in range(YT):
            rows = slice(8 * k, 8 * k + 8)
            for slot, part in enumerate((tile(x, 0, k), tile(x, 1, k))):
                rolled[slot, rows, :] = lane_down(part)
                rolled[2 + slot, rows, :] = lane_up(part)
        for zt in range(2):
            for k in range(YT + 1):
                y_weights(x, zt, k)

    def stage_1(x):
        for k in range(YT):
            rows = slice(8 * k, 8 * k + 8)
            parts = z_stage_weights(
                tile(x, 0, k), tile(x, 1, k), *[rolled[slot, rows, :] for slot in range(4)]
            )
            for slot, part in enumerate(parts):
                zs[slot, rows, :] = part
        for zt in range(2):
            for k in range(YT + 1):
                y_parts(zt, k)

    def stage_2(x):
        for k in range(YT):
            rows = slice(8 * k, 8 * k + 8)
            parts = z_stage_parts(*[zs[slot, rows, :] for slot in range(12)])
            for slot, part in enumerate(parts):
                zp[slot, rows, :] = part
        for zt in range(2):
            for k in range(YT):
                rows = slice(8 * k, 8 * k + 8)
                centre = 3.0 * (
                    vs[zt, x, 9 + 8 * k : 17 + 8 * k, :] - vs[zt, x, 7 + 8 * k : 15 + 8 * k, :]
                )
                tots[zt, rows, :] = summed[zt, x, rows, :] + upwind_square(
                    centre, p_ref[zt, 0, rows, :], p_ref[zt, 1, 8 * k + 1 : 8 * k + 9, :],
                    sigma_at(x, zt, k),
                )

    def stage_3(x):
        flat = pl.multiple_of(x * CY, 8)
        for k in range(YT):
            rows = slice(8 * k, 8 * k + 8)
            for zt in range(2):
                sigma = sigma_at(x, zt, k)
                if zt == 0:
                    along = upwind_pair(zp[0, rows, :] - zp[1, rows, :], zp[2, rows, :], sigma)
                    edge = fix_even
                else:
                    along = upwind_pair(zp[3, rows, :], zp[4, rows, :], sigma)
                    edge = fix_odd
                along = jnp.where(edge, fixes[zt, pl.ds(flat + 8 * k, 8), :], along)
                total = tots[zt, rows, :] + along
                root = total * lax.rsqrt(jnp.maximum(total, 1e-30))
                lanes = slice(128 * zt, 128 * zt + 128)
                out[x, rows, lanes] = v[x, rows, lanes] - pace[x, rows, lanes] * (root - 6.0)

    stages = (stage_3, stage_2, stage_1, stage_0)

    def run(at, low, high):
        for delay, stage in zip((3, 2, 1, 0), stages):
            if low <= delay <= high:
                stage(at - delay)

    def yz_pass(at, carry):
        run(at, 0, 3)
        return carry

    for at in range(3):
        run(at, 0, at)
    lax.fori_loop(3, CX, yz_pass, 0)
    for at in range(3):
        run(CX + at, at + 1, 3)
    if last:
        xa, xb, ylo, yhi, planes = outs[1:]
        write_swap(parity[0], out[0:1], out[CX - 1 : CX], xa, xb)
        y_faces(out, ylo, yhi, 1)
        planes[...] = jnp.zeros((4, CX, 128), F32)
        for chunk in range(CX // 8):
            for half in range(2):
                part = out[8 * chunk : 8 * chunk + 8, :, 128 * half : 128 * half + 128]
                part = part.reshape(8 * CY, 128).T
                for x in range(8):
                    lanes = slice(CY * x, CY * x + CY)
                    at = slice(8 * chunk + x, 8 * chunk + x + 1)
                    planes[half, at, 0:CY] = part[0:1, lanes]
                    planes[2 + half, at, 0:CY] = part[127:128, lanes]
    else:
        write_faces(parity, out, *outs[1:], yf, zf)


def rows_kernel(parity, xa, xb, ylo, yhi, ya, yb, ext):
    x_low, x_high = low_high(parity[0], xa[0], xb[0])
    for side, (source, row) in enumerate(((ylo, 0), (yhi, CY - 1))):
        ext[side, 0:1, :] = x_low[row : row + 1]
        ext[side, 1 : CX + 1, :] = source[0]
        ext[side, CX + 1 : CX + 2, :] = x_high[row : row + 1]
    write_swap(parity[1], ext[0], ext[1], ya, yb)


def planes_kernel(parity, xa, xb, ya, yb, own, planes, za, zb):
    x_sides = low_high(parity[0], xa[0], xb[0])
    y_low, y_high = low_high(parity[1], ya[...], yb[...])
    planes[...] = jnp.zeros((4, 40, 128), F32)
    for q in range(4):
        planes[q, 1 : CX + 1, :] = own[q]
    for side in range(2):
        row = (CX + 1) * side
        for half in range(2):
            turned = x_sides[side][:, 128 * half : 128 * half + 128].T
            planes[half, row : row + 1, 0:CY] = turned[0:1]
            planes[2 + half, row : row + 1, 0:CY] = turned[127:128]
    lane = lax.broadcasted_iota(jnp.int32, (CX + 2, 128), 1)
    for q in range(4):
        lanes = slice(128 * (q % 2), 128 * (q % 2) + 128)
        start = 0 if q < 2 else 127
        low = y_low[:, lanes]
        if start != 127:
            low = pltpu.roll(low, 127 - start, 1)
        high = pltpu.roll(y_high[:, lanes], (CY - start) % 128, 1)
        planes[q, 0 : CX + 2, :] = jnp.where(
            lane == 127, low, jnp.where(lane == CY, high, planes[q, 0 : CX + 2, :])
        )
    write_swap(parity[2], planes[0], planes[3], za, zb)


def face_shapes(width):
    shapes = [(width, CY, CZ)] * 2 + [(width, CX, CZ)] * 2
    shapes += [(8, ROWS)] * 2 if width == 3 else [(4, CX, 128)]
    return [jax.ShapeDtypeStruct(shape, F32) for shape in shapes]


def row_faces(parity, xa, xb, ylo, yhi):
    return pl.pallas_call(
        rows_kernel,
        out_shape=[jax.ShapeDtypeStruct((CX + 2, CZ), F32)] * 2,
        in_specs=parity_specs(4),
        out_specs=vmem_specs(2),
        scratch_shapes=[pltpu.VMEM((2, CX + 2, CZ), F32)],
        compiler_params=pltpu.CompilerParams(vmem_limit_bytes=VMEM_LIMIT),
        name="row_faces",
    )(parity, xa, xb, ylo, yhi)


def plane_faces(parity, xa, xb, ya, yb, own):
    return pl.pallas_call(
        planes_kernel,
        out_shape=[jax.ShapeDtypeStruct(shape, F32) for shape in ((4, 40, 128), (40, 128), (40, 128))],
        in_specs=parity_specs(5),
        out_specs=vmem_specs(3),
        compiler_params=pltpu.CompilerParams(vmem_limit_bytes=VMEM_LIMIT),
        name="plane_faces",
    )(parity, xa, xb, ya, yb, own)


BLOCK = jax.ShapeDtypeStruct((CX, CY, CZ), F32)
FACE_SCRATCH = [pltpu.VMEM((2, 3, CX, CZ), F32), pltpu.VMEM((2, 8, ROWS), F32)]


def vmem_specs(count):
    return [pl.BlockSpec(memory_space=pltpu.VMEM)] * count


def parity_specs(count):
    return [pl.BlockSpec(memory_space=pltpu.SMEM)] + vmem_specs(count)


def pack(parity, phi):
    return pl.pallas_call(
        pack_kernel,
        out_shape=[BLOCK] * 3 + face_shapes(3),
        in_specs=parity_specs(1),
        out_specs=vmem_specs(9),
        scratch_shapes=[pltpu.VMEM((3, CZ, 128), F32)] + FACE_SCRATCH,
        compiler_params=pltpu.CompilerParams(vmem_limit_bytes=VMEM_LIMIT),
        name="pack",
    )(parity, phi)


def unpack(mixed):
    return pl.pallas_call(
        unpack_kernel,
        out_shape=BLOCK,
        in_specs=vmem_specs(1),
        out_specs=vmem_specs(1)[0],
        scratch_shapes=[pltpu.VMEM((3, CZ, 128), F32)],
        compiler_params=pltpu.CompilerParams(vmem_limit_bytes=VMEM_LIMIT),
        name="unpack",
    )(mixed)


def step(parity, sigma_in, pace, za0, zb0, v, za_own, zb_own, halos, last):
    return pl.pallas_call(
        functools.partial(step_kernel, last),
        out_shape=[BLOCK] + face_shapes(1 if last else 3),
        in_specs=parity_specs(13),
        out_specs=vmem_specs(6 if last else 7),
        scratch_shapes=[
            pltpu.VMEM((2, CX, 64, 128), F32),
            pltpu.VMEM((2, CX, CY, 128), F32),
            pltpu.VMEM((2, 4, 64, 128), F32),
            pltpu.VMEM((2, 2, 64, 128), F32),
            pltpu.VMEM((24, ROWS), F32),
            pltpu.VMEM((4, 24, ROWS), F32),
            pltpu.VMEM((2, 24, ROWS), F32),
            pltpu.VMEM((2, 128, ROWS), F32),
            pltpu.VMEM((2, ROWS, 128), F32),
        ]
        + FACE_SCRATCH
        + [
            pltpu.VMEM((2, 3, CY, CZ), F32),
            pltpu.VMEM((4, CY, 128), F32),
            pltpu.VMEM((12, CY, 128), F32),
            pltpu.VMEM((5, CY, 128), F32),
            pltpu.VMEM((2, CY, 128), F32),
        ],
        compiler_params=pltpu.CompilerParams(vmem_limit_bytes=VMEM_LIMIT),
        name="step",
    )(parity, sigma_in, pace, za0, zb0, v, za_own, zb_own, *halos)


HALF_COS = [
    0.9999999991256178, -0.23370050635094053, 0.019968606689123116,
    -0.0008935362743290266, 2.3601076640059624e-05,
]
BAND_SQUARE = 1.5 * 1.5


def half_cosine(value):
    square = jnp.minimum(value * value, BAND_SQUARE)
    shape = F32(HALF_COS[4] / BAND_SQUARE**5)
    for k in (3, 2, 1, 0):
        shape = shape * square + F32(HALF_COS[k] / BAND_SQUARE ** (k + 1))
    return (BAND_SQUARE - square) * shape


def five_terms(centre, keep, dx, sx, dy, sy, dz, sz, dxy, dxz, dyz):
    twice = centre + centre
    xx, yy, zz = dx * dx, dy * dy, dz * dz
    squares = jnp.maximum(xx + yy + zz, 1.0)
    root = lax.rsqrt(squares)
    bend = (sx - twice) * (yy + zz) + (sy - twice) * (xx + zz) + (sz - twice) * (xx + yy)
    bend = bend - 0.5 * (dx * (dy * dxy + dz * dxz) + dy * dz * dyz)
    cosine = half_cosine(centre)
    spread = cosine * cosine
    if keep is not None:
        spread = jnp.where(keep, spread, 0.0)
    return (
        spread * (squares * root),
        spread * bend * (root * root),
        spread * dx,
        spread * dy,
        spread * dz,
    )


def brick_tables(ids, targets, live_count):
    entry = lax.broadcasted_iota(jnp.int32, (1, SLOTS), 1)
    live = entry < live_count
    row = lax.broadcasted_iota(jnp.int32, (SLOTS, SLOTS), 0)
    column = lax.broadcasted_iota(jnp.int32, (SLOTS, SLOTS), 1)
    owner = targets.astype(F32)
    down = jnp.sum(jnp.where(row == column, owner, 0.0), axis=1, keepdims=True)
    earlier = (row < column) & (row < live_count) & (down == owner)
    rank = jnp.sum(earlier.astype(F32), axis=0, keepdims=True)
    slot = jnp.where(live, 2.0 * owner + rank, F32(SLOTS))
    to_slot = (slot == row.astype(F32)).astype(F32)

    def finder(count, brick_of):
        at = lax.broadcasted_iota(jnp.int32, (count, SLOTS), 0)
        return (ids == brick_of(at)).astype(F32)

    return to_slot, finder


def exact_dot(left, right, dims=(((1,), (0,)), ((), ()))):
    return lax.dot_general(
        left, right, dims, precision=lax.Precision.HIGHEST, preferred_element_type=F32
    )


def brick_kernel(
    parity, count, v, xa, xb, ya, yb, za, zb, planes, ids, targets, record, vs, stack
):
    x_low, x_high = low_high(parity[0], xa[...], xb[...])
    y_low, y_high = low_high(parity[1], ya[...], yb[...])
    under, over = low_high(parity[2], za[...], zb[...])
    def fill(x, carry):
        for zt in range(2):
            vs[zt, x + 1, 8 : 8 + CY, :] = v[x, :, pl.ds(128 * zt, 128)]
        return carry

    lax.fori_loop(0, CX, fill, 0)
    for zt in range(2):
        lanes = slice(128 * zt, 128 * zt + 128)
        vs[zt, 0, 8 : 8 + CY, :] = x_low[0, :, lanes]
        vs[zt, CX + 1, 8 : 8 + CY, :] = x_high[0, :, lanes]
        for x in range(CX + 2):
            vs[zt, x, 7:8, :] = y_low[x : x + 1, lanes]
            vs[zt, x, 8 + CY : 9 + CY, :] = y_high[x : x + 1, lanes]

    lane = lax.broadcasted_iota(jnp.int32, (8, 128), 1)
    keeps = (lane != 0, lane != 127)

    def down(part):
        return pltpu.roll(part, 1, 1)

    def up(part):
        return pltpu.roll(part, 127, 1)

    def neighbours(pair):
        return ((down(pair[1]), pair[1]), (pair[0], up(pair[0])))

    def tile_terms(x, k):
        def read(zt, plane, shift):
            return vs[zt, plane, pl.ds(8 + 8 * k + shift, 8), :]

        two = range(2)
        centre = [read(zt, x + 1, 0) for zt in two]
        high = [read(zt, x + 2, 0) for zt in two]
        low = [read(zt, x, 0) for zt in two]
        dx = [high[zt] - low[zt] for zt in two]
        sx = [high[zt] + low[zt] for zt in two]
        right = [read(zt, x + 1, 1) for zt in two]
        left = [read(zt, x + 1, -1) for zt in two]
        dy = [right[zt] - left[zt] for zt in two]
        sy = [right[zt] + left[zt] for zt in two]
        dxy = [
            (read(zt, x + 2, 1) - read(zt, x, 1)) - (read(zt, x + 2, -1) - read(zt, x, -1))
            for zt in two
        ]
        around, dx_around, dy_around = neighbours(centre), neighbours(dx), neighbours(dy)
        results = []
        for zt in two:
            results.append(
                five_terms(
                    centre[zt], keeps[zt], dx[zt], sx[zt], dy[zt], sy[zt],
                    around[zt][1] - around[zt][0], around[zt][1] + around[zt][0],
                    dxy[zt],
                    dx_around[zt][1] - dx_around[zt][0],
                    dy_around[zt][1] - dy_around[zt][0],
                )
            )
        return [results[0][n] + results[1][n] for n in range(5)]

    zeros = jnp.zeros((8, 128), F32)
    for bx in range(2):

        def body(step_at, sums):
            sums = list(sums)
            for sub in range(2):
                x = BRICK * bx + 2 * step_at + sub
                for k in range(YT):
                    parts = tile_terms(x, k)
                    for n in range(5):
                        slot = 5 * (k // 2) + n
                        sums[slot] = sums[slot] + parts[n]
            return tuple(sums)

        sums = lax.fori_loop(0, BRICK // 2, body, (zeros,) * 15)
        for by in range(3):
            for n in range(5):
                row = 8 * (3 * bx + by) + n
                stack[row : row + 1, :] = jnp.sum(sums[5 * by + n], axis=0, keepdims=True)
            row = 8 * (3 * bx + by)
            stack[row + 5 : row + 8, :] = jnp.zeros((3, 128), F32)

    to_slot, finder = brick_tables(ids[...], targets[...], count[0])
    found = jnp.zeros((8, SLOTS), F32)
    for b in range(6):
        found = found + exact_dot(
            stack[8 * b : 8 * b + 8, :], finder(128, lambda at: 16 * b + at // 8)
        )
    for side in range(2):
        window = (under, planes[0], planes[1]) if side == 0 else (planes[2], planes[3], over)

        def cut(plane, step_x, step_y):
            part = window[plane][1 + step_x : 33 + step_x]
            return pltpu.roll(part, (-step_y) % 128, 1) if step_y else part

        high, low = cut(1, 1, 0), cut(1, -1, 0)
        right, left = cut(1, 0, 1), cut(1, 0, -1)
        above, below = cut(2, 0, 0), cut(0, 0, 0)
        terms = five_terms(
            cut(1, 0, 0), None,
            high - low, high + low, right - left, right + left, above - below, above + below,
            (cut(1, 1, 1) - cut(1, -1, 1)) - (cut(1, 1, -1) - cut(1, -1, -1)),
            (cut(2, 1, 0) - cut(2, -1, 0)) - (cut(0, 1, 0) - cut(0, -1, 0)),
            (cut(2, 0, 1) - cut(2, 0, -1)) - (cut(0, 0, 1) - cut(0, 0, -1)),
        )
        for bx in range(2):
            rows = [jnp.sum(term[16 * bx : 16 * bx + 16], axis=0, keepdims=True) for term in terms]
            rows = jnp.concatenate(rows + [jnp.zeros((3, 128), F32)], axis=0)
            found = found + exact_dot(
                rows,
                finder(
                    128,
                    lambda at: jnp.where(at < CY, 48 * bx + 16 * (at // 16) + 15 * side, -1),
                ),
            )
    total = exact_dot(found, to_slot, (((1,), (1,)), ((), ())))
    scale = 2.0 / 3.0 / (BRICK * BRICK)
    row = lax.broadcasted_iota(jnp.int32, (8, SLOTS), 0)
    record[...] = total * jnp.where(row == 1, F32(scale), F32(0.5 * scale))


def bricks(parity, count, v, halos, planes, ids, targets):
    return pl.pallas_call(
        brick_kernel,
        out_shape=jax.ShapeDtypeStruct((8, SLOTS), F32),
        in_specs=[pl.BlockSpec(memory_space=pltpu.SMEM)] * 2 + vmem_specs(10),
        out_specs=vmem_specs(1)[0],
        scratch_shapes=[
            pltpu.VMEM((2, CX + 2, 64, 128), F32),
            pltpu.VMEM((48, 128), F32),
        ],
        compiler_params=pltpu.CompilerParams(vmem_limit_bytes=VMEM_LIMIT),
        name="bricks",
    )(parity, count, v, *halos, planes, ids, targets)


def swap(value, axis, phase):
    count = lax.axis_size(axis)
    if phase == 0:
        pairs = [(i, i ^ 1) for i in range(count)]
    else:
        pairs = [(i, (i - 1 if i % 2 == 0 else i + 1) % count) for i in range(count)]
    return lax.ppermute(value, axis, pairs)


def exchange(faces):
    xa, xb, ya, yb, za, zb = faces
    yb = swap(yb, "gy", 1)
    ya = swap(ya, "gy", 0)
    zb = swap(zb, "gz", 1)
    za = swap(za, "gz", 0)
    xb = swap(xb, "gx", 1)
    xa = swap(xa, "gx", 0)
    return xa, xb, ya, yb, za, zb


def per_device(phi_start, band_ids, band_count, owners):
    parity = jnp.stack([lax.axis_index(name) % 2 for name in ("gx", "gy", "gz")])
    parity = parity.astype(jnp.int32)
    v, sigma, pace, *faces = pack(parity, phi_start)
    za0, zb0 = faces[4:]
    for number in range(STEPS):
        v, *faces = step(
            parity, sigma, pace, za0, zb0, v, faces[4], faces[5], exchange(faces),
            number == STEPS - 1,
        )
    level_set = unpack(v)

    xa, xb, ylo, yhi, own = faces
    xb = swap(xb, "gx", 1)
    xa = swap(xa, "gx", 0)
    ya, yb = row_faces(parity, xa, xb, ylo, yhi)
    yb = swap(yb, "gy", 1)
    ya = swap(ya, "gy", 0)
    planes, za, zb = plane_faces(parity, xa, xb, ya, yb, own)
    zb = swap(zb, "gz", 1)
    za = swap(za, "gz", 0)
    record = bricks(
        parity, band_count.reshape(1), v, (xa, xb, ya, yb, za, zb), planes,
        band_ids.reshape(1, SLOTS), owners.reshape(1, SLOTS),
    )
    totals = lax.all_to_all(record[:5], ("gx", "gy"), split_axis=1, concat_axis=1, tiled=True)
    return level_set, totals.reshape(1, 1, 1, 5, SLOTS)


def solution(mesh):
    placed = (
        P("gx", "gy", "gz"),
        P("gx", "gy", "gz", None),
        P("gx", "gy", "gz"),
        P("gx", "gy", "gz", None),
    )
    return jax.shard_map(
        per_device,
        mesh=mesh,
        in_specs=placed,
        out_specs=(P("gx", "gy", "gz"), P("gx", "gy", "gz", None, None)),
        check_vma=False,
    )
```

```python
import functools

import jax
import jax.numpy as jnp
from jax import lax
from jax.experimental import pallas as pl
from jax.experimental.pallas import tpu as pltpu
from jax.sharding import PartitionSpec as P

STEPS = 3
BRICK = 16
SLOTS = 64
CX, CY, CZ = 32, 48, 256
ROWS = CX * CY
YT = CY // 8
WENO_EPS = 1e-06
F32 = jnp.float32
VMEM_LIMIT = 16 * 1024 * 1024


def rcp(value):
    return pltpu.reciprocal(value, approx=True)


def smooth_weights(e_low, e_high, third):
    twice = third + third
    middle = e_low * e_high + (third * third * (4.0 / 3.0) + WENO_EPS)
    q_a = rcp(middle - e_low * twice)
    q_b = rcp(middle)
    q_c = rcp(middle + e_high * twice)
    return q_a * q_a, 6.0 * (q_b * q_b), q_c * q_c


def biased_parts(wa_next, wb, wc_prev, t_prev, t_here, t_next):
    x = wc_prev * (t_here - t_prev)
    y = wa_next * (t_next - t_here)
    both = x + y
    both = both + both
    total = (wa_next + wb) + wc_prev
    left = t_here + (both + y) * rcp(total + (wa_next + wa_next))
    right = t_here - (both + x) * rcp(total + (wc_prev + wc_prev))
    return left, right


def upwind_square(centre, left, right, sigma):
    return upwind_pair(centre - left, right - centre, sigma)


def upwind_pair(left, right_back, sigma):
    best = jnp.maximum(sigma * left, sigma * right_back)
    best = jnp.maximum(best, 0.0)
    return best * best


def sigma_of(value):
    return jnp.where(value > 0.0, F32(1.0), F32(-1.0))


def from_values(v_m, v_0, v_1, v_2):
    d_m, d_0, d_1 = v_0 - v_m, v_1 - v_0, v_2 - v_1
    e_0, e_1 = d_0 - d_m, d_1 - d_0
    return e_0, e_1, e_1 - e_0


def lane_down(part):
    return pltpu.roll(part, 1, 1)


def lane_up(part):
    return pltpu.roll(part, 127, 1)


def z_stage_weights(even, odd, even_down, odd_down, even_up, odd_up):
    v = {-2: even_down, -1: odd_down, 0: even, 1: odd, 2: even_up, 3: odd_up}
    d = {k: v[k + 1] - v[k] for k in range(-2, 3)}
    e = {k: d[k] - d[k - 1] for k in range(-1, 3)}
    t = {k: e[k + 1] - e[k] for k in range(-1, 2)}
    w_0 = smooth_weights(e[0], e[1], t[0])
    w_1 = smooth_weights(e[1], e[2], t[1])
    return (
        w_1[0], w_0[1], lane_down(w_1[2]), t[-1], t[0], t[1],
        lane_up(w_0[0]), w_1[1], w_0[2], lane_up(t[0]),
        3.0 * (d[-1] + d[0]), 3.0 * (d[0] + d[1]),
    )


def z_stage_parts(wa_0, wb_0, wc_0, t_m, t_0, t_1, wa_1, wb_1, wc_1, t_2, centre_0, centre_1):
    left_0, right_0 = biased_parts(wa_0, wb_0, wc_0, t_m, t_0, t_1)
    left_1, right_1 = biased_parts(wa_1, wb_1, wc_1, t_0, t_1, t_2)
    return centre_0, lane_down(left_1), right_0 - centre_0, centre_1 - left_0, right_1 - centre_1


def edge_column(window, u_ref, p_ref, u_row, p_row, sigma):
    def rows(start):
        return window[pl.ds(start, 8), :]

    e_0, e_1, t = from_values(rows(u_row - 1), rows(u_row), rows(u_row + 1), rows(u_row + 2))
    w_a, w_b, w_c = smooth_weights(e_0, e_1, t)
    for slot, part in enumerate((w_a, w_b, w_c, t)):
        u_ref[slot, pl.ds(u_row, 8), :] = part
    left, right = biased_parts(
        u_ref[0, pl.ds(p_row + 1, 8), :],
        u_ref[1, pl.ds(p_row, 8), :],
        u_ref[2, pl.ds(p_row - 1, 8), :],
        u_ref[3, pl.ds(p_row - 1, 8), :],
        u_ref[3, pl.ds(p_row, 8), :],
        u_ref[3, pl.ds(p_row + 1, 8), :],
    )
    p_ref[0, pl.ds(p_row, 8), :] = left
    p_ref[1, pl.ds(p_row, 8), :] = right
    centre = 3.0 * (rows(9) - rows(7))
    return upwind_square(
        centre, p_ref[0, pl.ds(7, 8), :], p_ref[1, pl.ds(8, 8), :], sigma
    )


def z_faces(source, zlo, zhi):
    for chunk in range(CX // 8):
        columns = slice(8 * CY * chunk, 8 * CY * (chunk + 1))
        for parity in range(2):
            part = source[8 * chunk : 8 * chunk + 8, :, 128 * parity : 128 * parity + 128]
            part = part.reshape(8 * CY, 128).T
            for k in range(4):
                zlo[2 * k + parity : 2 * k + parity + 1, columns] = part[k : k + 1]
                zhi[2 * k + parity : 2 * k + parity + 1, columns] = part[124 + k : 125 + k]


def y_faces(source, ylo, yhi, width):
    for x in range(CX):
        for k in range(width):
            ylo[k, x : x + 1, :] = source[x, k : k + 1, :]
            yhi[k, x : x + 1, :] = source[x, CY - width + k : CY - width + 1 + k, :]


def write_swap(parity, low, high, out_a, out_b):
    odd = parity == 1
    out_a[...] = jnp.where(odd, low, high)
    out_b[...] = jnp.where(odd, high, low)


def write_faces(parity, source, xa, xb, ya, yb, za, zb, yf, zf):
    y_faces(source, yf.at[0], yf.at[1], 3)
    write_swap(parity[1], yf[0], yf[1], ya, yb)
    write_swap(parity[0], source[0:3], source[CX - 3 : CX], xa, xb)
    z_faces(source, zf.at[0], zf.at[1])
    write_swap(parity[2], zf[0], zf[1], za, zb)


def low_high(parity, part_a, part_b):
    odd = parity == 1
    return jnp.where(odd, part_a, part_b), jnp.where(odd, part_b, part_a)


def pack_kernel(parity, phi, mixed, sigma, pace, xa, xb, ya, yb, za, zb, turned, yf, zf):
    for chunk in range(CX // 8):
        planes = slice(8 * chunk, 8 * chunk + 8)
        for half in range(2):
            part = phi[planes, :, 128 * half : 128 * half + 128]
            part = part.reshape(8 * CY, 128).T
            for c in range(3):
                turned[c, 128 * half : 128 * half + 128, :] = part[:, 128 * c : 128 * c + 128]
        for which in range(2):
            part = [turned[c, pl.ds(which, 128, stride=2), :].T for c in range(3)]
            part = jnp.concatenate(part, axis=0)
            mixed[planes, :, 128 * which : 128 * which + 128] = part.reshape(8, CY, 128)
    def signs(x, carry):
        value = mixed[x]
        sigma[x] = sigma_of(value)
        pace[x] = (0.05 * value) * lax.rsqrt(value * value + 1.0)
        return carry

    lax.fori_loop(0, CX, signs, 0)
    write_faces(parity, mixed, xa, xb, ya, yb, za, zb, yf, zf)


def unpack_kernel(mixed, out, turned):
    for chunk in range(CX // 8):
        planes = slice(8 * chunk, 8 * chunk + 8)
        for parity in range(2):
            part = mixed[planes, :, 128 * parity : 128 * parity + 128]
            part = part.reshape(8 * CY, 128).T
            for c in range(3):
                turned[c, pl.ds(parity, 128, stride=2), :] = part[:, 128 * c : 128 * c + 128]
        for half in range(2):
            part = [turned[c, 128 * half : 128 * half + 128, :].T for c in range(3)]
            part = jnp.concatenate(part, axis=0)
            out[planes, :, 128 * half : 128 * half + 128] = part.reshape(8, CY, 128)


def step_kernel(
    last,
    parity, sigma_in, pace, za0, zb0, v, za_own, zb_own, xa_in, xb_in, ya_in, yb_in, za_in, zb_in,
    *refs,
):
    faces = 6 if last else 7
    step_body(last, parity, sigma_in, pace, za0, zb0, v, za_own, zb_own, xa_in, xb_in, ya_in,
              yb_in, za_in, zb_in, refs[:faces], *refs[faces:])


def step_body(
    last,
    parity, sigma_in, pace, za0, zb0, v, za_own, zb_own, xa_in, xb_in, ya_in, yb_in, za_in, zb_in,
    outs,
    vs, summed, u_ref, p_ref, window, zu_ref, zp_ref, edges, fixes, yf, zf, xh,
    rolled, zs, zp, tots,
):
    out = outs[0]

    def fill(x, carry):
        for zt in range(2):
            vs[zt, x, 8 : 8 + CY, :] = v[x, :, pl.ds(128 * zt, 128)]
        return carry

    lax.fori_loop(0, CX, fill, 0)
    yf[0], yf[1] = low_high(parity[1], ya_in[...], yb_in[...])
    for x in range(CX):
        for zt in range(2):
            lanes = slice(128 * zt, 128 * zt + 128)
            for k in range(3):
                vs[zt, x, 5 + k : 6 + k, :] = yf[0, k, x : x + 1, lanes]
                vs[zt, x, 8 + CY + k : 9 + CY + k, :] = yf[1, k, x : x + 1, lanes]
    xh[0], xh[1] = low_high(parity[0], xa_in[...], xb_in[...])

    z_low, z_high = low_high(parity[2], za_in[...], zb_in[...])
    zlo0, zhi0 = low_high(parity[2], za0[...], zb0[...])
    zlo_own, zhi_own = low_high(parity[2], za_own[...], zb_own[...])
    window[5:8, :] = z_low[5:8]
    window[8:16, :] = zlo_own
    fixed = edge_column(window, zu_ref, zp_ref, 6, 7, sigma_of(zlo0))
    for half, lane_at, cell_at in ((0, 0, 0), (0, 1, 2), (1, 0, 1)):
        edges[half, lane_at : lane_at + 1, :] = fixed[cell_at : cell_at + 1]
    window[8:16, :] = zhi_own
    window[16:19, :] = z_high[0:3]
    fixed = edge_column(window, zu_ref, zp_ref, 9, 8, sigma_of(zhi0))
    for half, lane_at, cell_at in ((0, 127, 6), (1, 126, 5), (1, 127, 7)):
        edges[half, lane_at : lane_at + 1, :] = fixed[cell_at : cell_at + 1]
    for half in range(2):
        fixes[half] = edges[half].T

    def x_pass(yt, carry):
        row = pl.multiple_of(8 * yt, 8)
        for zt in range(2):
            lanes = pl.ds(128 * zt, 128)

            def cell(x):
                if x < 0:
                    return xh[0, 3 + x, pl.ds(row, 8), lanes]
                if x >= CX:
                    return xh[1, x - CX, pl.ds(row, 8), lanes]
                return v[x, pl.ds(row, 8), lanes]

            d, e, t, weights, lefts, rights = {}, {}, {}, {}, {}, {}
            d[-3] = cell(-2) - cell(-3)
            d[-2] = cell(-1) - cell(-2)
            e[-2] = d[-2] - d[-3]
            for j in range(-2, CX + 1):
                d[j + 1] = cell(j + 2) - cell(j + 1)
                e[j + 1] = d[j + 1] - d[j]
                t[j] = e[j + 1] - e[j]
                weights[j] = smooth_weights(e[j], e[j + 1], t[j])
                p = j - 1
                if p >= -1:
                    lefts[p], rights[p] = biased_parts(
                        weights[p + 1][0], weights[p][1], weights[p - 1][2], t[p - 1], t[p], t[p + 1]
                    )
                if p >= 0:
                    sigma = sigma_in[p, pl.ds(row, 8), lanes]
                    centre = 3.0 * (d[p - 1] + d[p])
                    summed[zt, p, pl.ds(row, 8), :] = upwind_square(
                        centre, lefts[p - 1], rights[p], sigma
                    )
        return carry

    lax.fori_loop(0, YT, x_pass, 0)

    lane = lax.broadcasted_iota(jnp.int32, (8, 128), 1)
    fix_even = (lane < 2) | (lane == 127)
    fix_odd = (lane < 1) | (lane > 125)

    def y_weights(x, zt, k):
        start = 6 + 8 * k
        e_0, e_1, t = from_values(
            *[vs[zt, x, pl.ds(start + shift, 8), :] for shift in (-1, 0, 1, 2)]
        )
        w_a, w_b, w_c = smooth_weights(e_0, e_1, t)
        for slot, part in enumerate((w_a, w_b, w_c, t)):
            u_ref[zt, slot, pl.ds(8 * k, 8), :] = part

    def y_parts(zt, k):
        def read(slot, row):
            return u_ref[zt, slot, pl.ds(row, 8), :]

        row = 8 * k + 1
        left, right = biased_parts(
            read(0, row + 1), read(1, row), read(2, row - 1),
            read(3, row - 1), read(3, row), read(3, row + 1),
        )
        p_ref[zt, 0, pl.ds(8 * k, 8), :] = left
        p_ref[zt, 1, pl.ds(8 * k, 8), :] = right

    def tile(x, zt, k):
        return v[x, 8 * k : 8 * k + 8, 128 * zt : 128 * zt + 128]

    def sigma_at(x, zt, k):
        return sigma_in[x, 8 * k : 8 * k + 8, 128 * zt : 128 * zt + 128]

    def stage_0(x):
        for k in range(YT):
            rows = slice(8 * k, 8 * k + 8)
            for slot, part in enumerate((tile(x, 0, k), tile(x, 1, k))):
                rolled[slot, rows, :] = lane_down(part)
                rolled[2 + slot, rows, :] = lane_up(part)
        for zt in range(2):
            for k in range(YT + 1):
                y_weights(x, zt, k)

    def stage_1(x):
        for k in range(YT):
            rows = slice(8 * k, 8 * k + 8)
            parts = z_stage_weights(
                tile(x, 0, k), tile(x, 1, k), *[rolled[slot, rows, :] for slot in range(4)]
            )
            for slot, part in enumerate(parts):
                zs[slot, rows, :] = part
        for zt in range(2):
            for k in range(YT + 1):
                y_parts(zt, k)

    def stage_2(x):
        for k in range(YT):
            rows = slice(8 * k, 8 * k + 8)
            parts = z_stage_parts(*[zs[slot, rows, :] for slot in range(12)])
            for slot, part in enumerate(parts):
                zp[slot, rows, :] = part
        for zt in range(2):
            for k in range(YT):
                rows = slice(8 * k, 8 * k + 8)
                centre = 3.0 * (
                    vs[zt, x, 9 + 8 * k : 17 + 8 * k, :] - vs[zt, x, 7 + 8 * k : 15 + 8 * k, :]
                )
                tots[zt, rows, :] = summed[zt, x, rows, :] + upwind_square(
                    centre, p_ref[zt, 0, rows, :], p_ref[zt, 1, 8 * k + 1 : 8 * k + 9, :],
                    sigma_at(x, zt, k),
                )

    def stage_3(x):
        flat = pl.multiple_of(x * CY, 8)
        for k in range(YT):
            rows = slice(8 * k, 8 * k + 8)
            for zt in range(2):
                sigma = sigma_at(x, zt, k)
                if zt == 0:
                    along = upwind_pair(zp[0, rows, :] - zp[1, rows, :], zp[2, rows, :], sigma)
                    edge = fix_even
                else:
                    along = upwind_pair(zp[3, rows, :], zp[4, rows, :], sigma)
                    edge = fix_odd
                along = jnp.where(edge, fixes[zt, pl.ds(flat + 8 * k, 8), :], along)
                total = tots[zt, rows, :] + along
                root = total * lax.rsqrt(jnp.maximum(total, 1e-30))
                lanes = slice(128 * zt, 128 * zt + 128)
                out[x, rows, lanes] = v[x, rows, lanes] - pace[x, rows, lanes] * (root - 6.0)

    stages = (stage_3, stage_2, stage_1, stage_0)

    def run(at, low, high):
        for delay, stage in zip((3, 2, 1, 0), stages):
            if low <= delay <= high:
                stage(at - delay)

    def yz_pass(at, carry):
        run(at, 0, 3)
        return carry

    for at in range(3):
        run(at, 0, at)
    lax.fori_loop(3, CX, yz_pass, 0)
    for at in range(3):
        run(CX + at, at + 1, 3)
    if last:
        xa, xb, ylo, yhi, planes = outs[1:]
        write_swap(parity[0], out[0:1], out[CX - 1 : CX], xa, xb)
        y_faces(out, ylo, yhi, 2)
        planes[...] = jnp.zeros((4, CX, 128), F32)
        for chunk in range(CX // 8):
            for half in range(2):
                part = out[8 * chunk : 8 * chunk + 8, :, 128 * half : 128 * half + 128]
                part = part.reshape(8 * CY, 128).T
                for x in range(8):
                    lanes = slice(CY * x, CY * x + CY)
                    at = slice(8 * chunk + x, 8 * chunk + x + 1)
                    planes[half, at, 0:CY] = part[0:1, lanes]
                    planes[2 + half, at, 0:CY] = part[127:128, lanes]
    else:
        write_faces(parity, out, *outs[1:], yf, zf)


def rows_kernel(parity, xa, xb, ylo, yhi, ya, yb, y_rows):
    x_low, x_high = low_high(parity[0], xa[0], xb[0])
    for at, (source, layer, row) in enumerate(
        ((ylo, 0, 0), (ylo, 1, 1), (yhi, 0, CY - 2), (yhi, 1, CY - 1))
    ):
        y_rows[at, 0:1, :] = x_low[row : row + 1]
        y_rows[at, 1 : CX + 1, :] = source[layer]
        y_rows[at, CX + 1 : CX + 2, :] = x_high[row : row + 1]
    write_swap(parity[1], y_rows[0], y_rows[3], ya, yb)


def planes_kernel(parity, xa, xb, ya, yb, own, planes, za, zb):
    x_sides = low_high(parity[0], xa[0], xb[0])
    y_low, y_high = low_high(parity[1], ya[...], yb[...])
    planes[...] = jnp.zeros((4, 40, 128), F32)
    for q in range(4):
        planes[q, 1 : CX + 1, :] = own[q]
    for side in range(2):
        row = (CX + 1) * side
        for half in range(2):
            turned = x_sides[side][:, 128 * half : 128 * half + 128].T
            planes[half, row : row + 1, 0:CY] = turned[0:1]
            planes[2 + half, row : row + 1, 0:CY] = turned[127:128]
    lane = lax.broadcasted_iota(jnp.int32, (CX + 2, 128), 1)
    for q in range(4):
        lanes = slice(128 * (q % 2), 128 * (q % 2) + 128)
        start = 0 if q < 2 else 127
        low = y_low[:, lanes]
        if start != 127:
            low = pltpu.roll(low, 127 - start, 1)
        high = pltpu.roll(y_high[:, lanes], (CY - start) % 128, 1)
        planes[q, 0 : CX + 2, :] = jnp.where(
            lane == 127, low, jnp.where(lane == CY, high, planes[q, 0 : CX + 2, :])
        )
    write_swap(parity[2], planes[0], planes[3], za, zb)


def face_shapes(width):
    shapes = [(width, CY, CZ)] * 2 + [(max(width, 2), CX, CZ)] * 2
    shapes += [(8, ROWS)] * 2 if width == 3 else [(4, CX, 128)]
    return [jax.ShapeDtypeStruct(shape, F32) for shape in shapes]


def row_faces(parity, xa, xb, ylo, yhi):
    return pl.pallas_call(
        rows_kernel,
        out_shape=[jax.ShapeDtypeStruct((CX + 2, CZ), F32)] * 2
        + [jax.ShapeDtypeStruct((4, CX + 2, CZ), F32)],
        in_specs=parity_specs(4),
        out_specs=vmem_specs(3),
        compiler_params=pltpu.CompilerParams(vmem_limit_bytes=VMEM_LIMIT),
        name="row_faces",
    )(parity, xa, xb, ylo, yhi)


def plane_faces(parity, xa, xb, ya, yb, own):
    return pl.pallas_call(
        planes_kernel,
        out_shape=[jax.ShapeDtypeStruct(shape, F32) for shape in ((4, 40, 128), (40, 128), (40, 128))],
        in_specs=parity_specs(5),
        out_specs=vmem_specs(3),
        compiler_params=pltpu.CompilerParams(vmem_limit_bytes=VMEM_LIMIT),
        name="plane_faces",
    )(parity, xa, xb, ya, yb, own)


BLOCK = jax.ShapeDtypeStruct((CX, CY, CZ), F32)
FACE_SCRATCH = [pltpu.VMEM((2, 3, CX, CZ), F32), pltpu.VMEM((2, 8, ROWS), F32)]


def vmem_specs(count):
    return [pl.BlockSpec(memory_space=pltpu.VMEM)] * count


def parity_specs(count):
    return [pl.BlockSpec(memory_space=pltpu.SMEM)] + vmem_specs(count)


def pack(parity, phi):
    return pl.pallas_call(
        pack_kernel,
        out_shape=[BLOCK] * 3 + face_shapes(3),
        in_specs=parity_specs(1),
        out_specs=vmem_specs(9),
        scratch_shapes=[pltpu.VMEM((3, CZ, 128), F32)] + FACE_SCRATCH,
        compiler_params=pltpu.CompilerParams(vmem_limit_bytes=VMEM_LIMIT),
        name="pack",
    )(parity, phi)


def unpack(mixed):
    return pl.pallas_call(
        unpack_kernel,
        out_shape=BLOCK,
        in_specs=vmem_specs(1),
        out_specs=vmem_specs(1)[0],
        scratch_shapes=[pltpu.VMEM((3, CZ, 128), F32)],
        compiler_params=pltpu.CompilerParams(vmem_limit_bytes=VMEM_LIMIT),
        name="unpack",
    )(mixed)


def step(parity, sigma_in, pace, za0, zb0, v, za_own, zb_own, halos, last):
    return pl.pallas_call(
        functools.partial(step_kernel, last),
        out_shape=[BLOCK] + face_shapes(1 if last else 3),
        in_specs=parity_specs(13),
        out_specs=vmem_specs(6 if last else 7),
        scratch_shapes=[
            pltpu.VMEM((2, CX, 64, 128), F32),
            pltpu.VMEM((2, CX, CY, 128), F32),
            pltpu.VMEM((2, 4, 64, 128), F32),
            pltpu.VMEM((2, 2, 64, 128), F32),
            pltpu.VMEM((24, ROWS), F32),
            pltpu.VMEM((4, 24, ROWS), F32),
            pltpu.VMEM((2, 24, ROWS), F32),
            pltpu.VMEM((2, 128, ROWS), F32),
            pltpu.VMEM((2, ROWS, 128), F32),
        ]
        + FACE_SCRATCH
        + [
            pltpu.VMEM((2, 3, CY, CZ), F32),
            pltpu.VMEM((4, CY, 128), F32),
            pltpu.VMEM((12, CY, 128), F32),
            pltpu.VMEM((5, CY, 128), F32),
            pltpu.VMEM((2, CY, 128), F32),
        ],
        compiler_params=pltpu.CompilerParams(vmem_limit_bytes=VMEM_LIMIT),
        name="step",
    )(parity, sigma_in, pace, za0, zb0, v, za_own, zb_own, *halos)


HALF_COS = [
    0.9999999991256178, -0.23370050635094053, 0.019968606689123116,
    -0.0008935362743290266, 2.3601076640059624e-05,
]
BAND_SQUARE = 1.5 * 1.5


def half_cosine(value):
    square = jnp.minimum(value * value, BAND_SQUARE)
    shape = F32(HALF_COS[4] / BAND_SQUARE**5)
    for k in (3, 2, 1, 0):
        shape = shape * square + F32(HALF_COS[k] / BAND_SQUARE ** (k + 1))
    return (BAND_SQUARE - square) * shape


def five_terms(centre, keep, dx, sx, dy, sy, dz, sz, dxy, dxz, dyz):
    twice = centre + centre
    xx, yy, zz = dx * dx, dy * dy, dz * dz
    squares = jnp.maximum(xx + yy + zz, 1.0)
    root = lax.rsqrt(squares)
    bend = (sx - twice) * (yy + zz) + (sy - twice) * (xx + zz) + (sz - twice) * (xx + yy)
    bend = bend - 0.5 * (dx * (dy * dxy + dz * dxz) + dy * dz * dyz)
    cosine = half_cosine(centre)
    spread = cosine * cosine
    if keep is not None:
        spread = jnp.where(keep, spread, 0.0)
    return (
        spread * (squares * root),
        spread * bend * (root * root),
        spread * dx,
        spread * dy,
        spread * dz,
    )


def brick_tables(ids, targets, live_count):
    entry = lax.broadcasted_iota(jnp.int32, (1, SLOTS), 1)
    live = entry < live_count
    row = lax.broadcasted_iota(jnp.int32, (SLOTS, SLOTS), 0)
    column = lax.broadcasted_iota(jnp.int32, (SLOTS, SLOTS), 1)
    owner = targets.astype(F32)
    down = jnp.sum(jnp.where(row == column, owner, 0.0), axis=1, keepdims=True)
    earlier = (row < column) & (row < live_count) & (down == owner)
    rank = jnp.sum(earlier.astype(F32), axis=0, keepdims=True)
    slot = jnp.where(live, 2.0 * owner + rank, F32(SLOTS))
    to_slot = (slot == row.astype(F32)).astype(F32)

    def finder(count, brick_of):
        at = lax.broadcasted_iota(jnp.int32, (count, SLOTS), 0)
        return (ids == brick_of(at)).astype(F32)

    return to_slot, finder


def exact_dot(left, right, dims=(((1,), (0,)), ((), ()))):
    return lax.dot_general(
        left, right, dims, precision=lax.Precision.HIGHEST, preferred_element_type=F32
    )


def neighbours(pair):
    return ((lane_down(pair[1]), pair[1]), (pair[0], lane_up(pair[0])))


def pair_terms(grid, keeps):
    two = range(2)

    def diff(first, second):
        return [grid[first][half] - grid[second][half] for half in two]

    def summed(first, second):
        return [grid[first][half] + grid[second][half] for half in two]

    dx, sx = diff((1, 0), (-1, 0)), summed((1, 0), (-1, 0))
    dy, sy = diff((0, 1), (0, -1)), summed((0, 1), (0, -1))
    over, under = diff((1, 1), (-1, 1)), diff((1, -1), (-1, -1))
    around, dx_around, dy_around = neighbours(grid[0, 0]), neighbours(dx), neighbours(dy)
    results = []
    for half in two:
        results.append(
            five_terms(
                grid[0, 0][half], keeps[half], dx[half], sx[half], dy[half], sy[half],
                around[half][1] - around[half][0], around[half][1] + around[half][0],
                over[half] - under[half],
                dx_around[half][1] - dx_around[half][0],
                dy_around[half][1] - dy_around[half][0],
            )
        )
    return [results[0][n] + results[1][n] for n in range(5)]


STAR = [(0, 0), (1, 0), (-1, 0), (0, 1), (0, -1), (1, 1), (1, -1), (-1, 1), (-1, -1)]


def tile_terms(vs, plane, k, keeps):
    grid = {
        (sx, sy): [vs[half, plane + sx, pl.ds(8 + 8 * k + sy, 8), :] for half in range(2)]
        for sx, sy in STAR
    }
    return pair_terms(grid, keeps)


def z_keeps(rows):
    lane = lax.broadcasted_iota(jnp.int32, (rows, 128), 1)
    return [lane != 0, lane != 127]


def inner_kernel(v, stack, vs):
    def fill(x, carry):
        for half in range(2):
            vs[half, x, 8 : 8 + CY, :] = v[x, :, pl.ds(128 * half, 128)]
            vs[half, x, 7:8, :] = jnp.zeros((1, 128), F32)
            vs[half, x, 8 + CY : 9 + CY, :] = jnp.zeros((1, 128), F32)
        return carry

    lax.fori_loop(0, CX, fill, 0)
    keeps = z_keeps(8)
    row = lax.broadcasted_iota(jnp.int32, (8, 128), 0)
    first = [keep & (row != 0) for keep in keeps]
    last = [keep & (row != 7) for keep in keeps]
    zeros = jnp.zeros((8, 128), F32)
    for bx in range(2):

        def body(step_at, sums):
            sums = list(sums)
            for sub in range(3):
                x = BRICK * bx + (1 - bx) + 3 * step_at + sub
                for k in range(YT):
                    parts = tile_terms(vs, x, k, first if k == 0 else last if k == 5 else keeps)
                    for n in range(5):
                        slot = 5 * (k // 2) + n
                        sums[slot] = sums[slot] + parts[n]
            return tuple(sums)

        sums = lax.fori_loop(0, 5, body, (zeros,) * 15)
        for by in range(3):
            row_at = 8 * (3 * bx + by)
            for n in range(5):
                total = jnp.sum(sums[5 * by + n], axis=0, keepdims=True)
                stack[row_at + n : row_at + n + 1, :] = total
            stack[row_at + 5 : row_at + 8, :] = jnp.zeros((3, 128), F32)


def edge_kernel(
    parity, count, inner, v, xa, xb, ya, yb, za, zb, y_rows, planes, ids, targets, record,
    vs, stack,
):
    x_sides = low_high(parity[0], xa[0], xb[0])
    y_sides = low_high(parity[1], ya[...], yb[...])
    under, over = low_high(parity[2], za[...], zb[...])
    stack[...] = inner[...]

    def add(b, n, row):
        stack[8 * b + n : 8 * b + n + 1, :] += row

    keeps = z_keeps(8)
    for side in range(2):
        for half in range(2):
            lanes = slice(128 * half, 128 * half + 128)
            for at in range(3):
                x = at - 1 if side == 0 else CX - 2 + at
                if 0 <= x < CX:
                    vs[half, at, 8 : 8 + CY, :] = v[x, :, lanes]
                else:
                    vs[half, at, 8 : 8 + CY, :] = x_sides[side][:, lanes]
                vs[half, at, 7:8, :] = y_sides[0][x + 1 : x + 2, lanes]
                vs[half, at, 8 + CY : 9 + CY, :] = y_sides[1][x + 1 : x + 2, lanes]
        for by in range(3):
            parts = [tile_terms(vs, 1, 2 * by + sub, keeps) for sub in range(2)]
            for n in range(5):
                add(3 * side + by, n, jnp.sum(parts[0][n] + parts[1][n], axis=0, keepdims=True))

    keeps = z_keeps(16)
    row = lax.broadcasted_iota(jnp.int32, (16, 128), 0)
    for side in range(2):
        if side == 0:
            rows = (y_sides[0], y_rows[0], y_rows[1])
        else:
            rows = (y_rows[2], y_rows[3], y_sides[1])
        for bx in range(2):
            grid = {
                (sx, sy): [
                    rows[1 + sy][1 + 16 * bx + sx : 17 + 16 * bx + sx, 128 * half : 128 * half + 128]
                    for half in range(2)
                ]
                for sx, sy in STAR
            }
            inside = row != (0 if bx == 0 else 15)
            parts = pair_terms(grid, [keep & inside for keep in keeps])
            for n in range(5):
                add(3 * bx + 2 * side, n, jnp.sum(parts[n], axis=0, keepdims=True))

    to_slot, finder = brick_tables(ids[...], targets[...], count[0])
    found = jnp.zeros((8, SLOTS), F32)
    for b in range(6):
        found = found + exact_dot(
            stack[8 * b : 8 * b + 8, :], finder(128, lambda at: 16 * b + at // 8)
        )
    for side in range(2):
        window = (under, planes[0], planes[1]) if side == 0 else (planes[2], planes[3], over)

        def cut(plane, step_x, step_y):
            part = window[plane][1 + step_x : 33 + step_x]
            return pltpu.roll(part, (-step_y) % 128, 1) if step_y else part

        high, low = cut(1, 1, 0), cut(1, -1, 0)
        right, left = cut(1, 0, 1), cut(1, 0, -1)
        above, below = cut(2, 0, 0), cut(0, 0, 0)
        terms = five_terms(
            cut(1, 0, 0), None,
            high - low, high + low, right - left, right + left, above - below, above + below,
            (cut(1, 1, 1) - cut(1, -1, 1)) - (cut(1, 1, -1) - cut(1, -1, -1)),
            (cut(2, 1, 0) - cut(2, -1, 0)) - (cut(0, 1, 0) - cut(0, -1, 0)),
            (cut(2, 0, 1) - cut(2, 0, -1)) - (cut(0, 0, 1) - cut(0, 0, -1)),
        )
        for bx in range(2):
            rows = [jnp.sum(term[16 * bx : 16 * bx + 16], axis=0, keepdims=True) for term in terms]
            rows = jnp.concatenate(rows + [jnp.zeros((3, 128), F32)], axis=0)
            found = found + exact_dot(
                rows,
                finder(
                    128,
                    lambda at: jnp.where(at < CY, 48 * bx + 16 * (at // 16) + 15 * side, -1),
                ),
            )
    total = exact_dot(found, to_slot, (((1,), (1,)), ((), ())))
    scale = 2.0 / 3.0 / (BRICK * BRICK)
    row = lax.broadcasted_iota(jnp.int32, (8, SLOTS), 0)
    record[...] = total * jnp.where(row == 1, F32(scale), F32(0.5 * scale))


def inner_bricks(v):
    return pl.pallas_call(
        inner_kernel,
        out_shape=jax.ShapeDtypeStruct((48, 128), F32),
        in_specs=vmem_specs(1),
        out_specs=vmem_specs(1)[0],
        scratch_shapes=[pltpu.VMEM((2, CX, 64, 128), F32)],
        compiler_params=pltpu.CompilerParams(vmem_limit_bytes=VMEM_LIMIT),
        cost_estimate=pl.CostEstimate(flops=20000000, bytes_accessed=6000000, transcendentals=400000),
        name="inner_bricks",
    )(v)


def edge_bricks(parity, count, inner, v, halos, y_rows, planes, ids, targets):
    return pl.pallas_call(
        edge_kernel,
        out_shape=jax.ShapeDtypeStruct((8, SLOTS), F32),
        in_specs=[pl.BlockSpec(memory_space=pltpu.SMEM)] * 2 + vmem_specs(12),
        out_specs=vmem_specs(1)[0],
        scratch_shapes=[
            pltpu.VMEM((2, 3, 64, 128), F32),
            pltpu.VMEM((48, 128), F32),
        ],
        compiler_params=pltpu.CompilerParams(vmem_limit_bytes=VMEM_LIMIT),
        name="edge_bricks",
    )(parity, count, inner, v, *halos, y_rows, planes, ids, targets)


def swap(value, axis, phase):
    count = lax.axis_size(axis)
    if phase == 0:
        pairs = [(i, i ^ 1) for i in range(count)]
    else:
        pairs = [(i, (i - 1 if i % 2 == 0 else i + 1) % count) for i in range(count)]
    return lax.ppermute(value, axis, pairs)


def exchange(faces):
    xa, xb, ya, yb, za, zb = faces
    zb = swap(zb, "gz", 1)
    yb = swap(yb, "gy", 1)
    ya = swap(ya, "gy", 0)
    za = swap(za, "gz", 0)
    xb = swap(xb, "gx", 1)
    xa = swap(xa, "gx", 0)
    return xa, xb, ya, yb, za, zb


def per_device(phi_start, band_ids, band_count, owners):
    parity = jnp.stack([lax.axis_index(name) % 2 for name in ("gx", "gy", "gz")])
    parity = parity.astype(jnp.int32)
    v, sigma, pace, *faces = pack(parity, phi_start)
    za0, zb0 = faces[4:]
    for number in range(STEPS):
        v, *faces = step(
            parity, sigma, pace, za0, zb0, v, faces[4], faces[5], exchange(faces),
            number == STEPS - 1,
        )
    level_set = unpack(v)

    xa, xb, ylo, yhi, own = faces
    xb = swap(xb, "gx", 1)
    xa = swap(xa, "gx", 0)
    ya, yb, y_rows = row_faces(parity, xa, xb, ylo, yhi)
    inner = inner_bricks(v)
    yb = swap(yb, "gy", 1)
    ya = swap(ya, "gy", 0)
    ya, yb, inner = lax.optimization_barrier((ya, yb, inner))
    planes, za, zb = plane_faces(parity, xa, xb, ya, yb, own)
    zb = swap(zb, "gz", 1)
    za = swap(za, "gz", 0)
    record = edge_bricks(
        parity, band_count.reshape(1), inner, v, (xa, xb, ya, yb, za, zb), y_rows, planes,
        band_ids.reshape(1, SLOTS), owners.reshape(1, SLOTS),
    )
    totals = lax.all_to_all(record[:5], ("gx", "gy"), split_axis=1, concat_axis=1, tiled=True)
    return level_set, totals.reshape(1, 1, 1, 5, SLOTS)


def solution(mesh):
    placed = (
        P("gx", "gy", "gz"),
        P("gx", "gy", "gz", None),
        P("gx", "gy", "gz"),
        P("gx", "gy", "gz", None),
    )
    return jax.shard_map(
        per_device,
        mesh=mesh,
        in_specs=placed,
        out_specs=(P("gx", "gy", "gz"), P("gx", "gy", "gz", None, None)),
        check_vma=False,
    )
```

```python
import functools

import jax
import jax.numpy as jnp
from jax import lax
from jax.experimental import pallas as pl
from jax.experimental.pallas import tpu as pltpu
from jax.sharding import PartitionSpec as P

STEPS = 3
BRICK = 16
SLOTS = 64
Z_SENT = 32
PEERS = 32
CX, CY, CZ = 32, 48, 256
ROWS = CX * CY
YT = CY // 8
WENO_EPS = 1e-06
F32 = jnp.float32
VMEM_LIMIT = 16 * 1024 * 1024


def rcp(value):
    return pltpu.reciprocal(value, approx=True)


def smooth_weights(e_low, e_high, third):
    twice = third + third
    middle = e_low * e_high + (third * third * (4.0 / 3.0) + WENO_EPS)
    q_a = rcp(middle - e_low * twice)
    q_b = rcp(middle)
    q_c = rcp(middle + e_high * twice)
    return q_a * q_a, 6.0 * (q_b * q_b), q_c * q_c


def biased_parts(wa_next, wb, wc_prev, t_prev, t_here, t_next):
    x = wc_prev * (t_here - t_prev)
    y = wa_next * (t_next - t_here)
    both = x + y
    both = both + both
    total = (wa_next + wb) + wc_prev
    left = t_here + (both + y) * rcp(total + (wa_next + wa_next))
    right = t_here - (both + x) * rcp(total + (wc_prev + wc_prev))
    return left, right


def upwind_square(centre, left, right, sigma):
    return upwind_pair(centre - left, right - centre, sigma)


def upwind_pair(left, right_back, sigma):
    best = jnp.maximum(sigma * left, sigma * right_back)
    best = jnp.maximum(best, 0.0)
    return best * best


def sigma_of(value):
    return jnp.where(value > 0.0, F32(1.0), F32(-1.0))


def from_values(v_m, v_0, v_1, v_2):
    d_m, d_0, d_1 = v_0 - v_m, v_1 - v_0, v_2 - v_1
    e_0, e_1 = d_0 - d_m, d_1 - d_0
    return e_0, e_1, e_1 - e_0


def lane_down(part):
    return pltpu.roll(part, 1, 1)


def lane_up(part):
    return pltpu.roll(part, 127, 1)


def z_stage_weights(even, odd, even_down, odd_down, even_up, odd_up):
    v = {-2: even_down, -1: odd_down, 0: even, 1: odd, 2: even_up, 3: odd_up}
    d = {k: v[k + 1] - v[k] for k in range(-2, 3)}
    e = {k: d[k] - d[k - 1] for k in range(-1, 3)}
    t = {k: e[k + 1] - e[k] for k in range(-1, 2)}
    w_0 = smooth_weights(e[0], e[1], t[0])
    w_1 = smooth_weights(e[1], e[2], t[1])
    return (
        w_1[0], w_0[1], lane_down(w_1[2]), t[-1], t[0], t[1],
        lane_up(w_0[0]), w_1[1], w_0[2], lane_up(t[0]),
        3.0 * (d[-1] + d[0]), 3.0 * (d[0] + d[1]),
    )


def z_stage_parts(wa_0, wb_0, wc_0, t_m, t_0, t_1, wa_1, wb_1, wc_1, t_2, centre_0, centre_1):
    left_0, right_0 = biased_parts(wa_0, wb_0, wc_0, t_m, t_0, t_1)
    left_1, right_1 = biased_parts(wa_1, wb_1, wc_1, t_0, t_1, t_2)
    return centre_0, lane_down(left_1), right_0 - centre_0, centre_1 - left_0, right_1 - centre_1


def edge_column(window, u_ref, p_ref, u_row, p_row, sigma):
    def rows(start):
        return window[pl.ds(start, 8), :]

    e_0, e_1, t = from_values(rows(u_row - 1), rows(u_row), rows(u_row + 1), rows(u_row + 2))
    w_a, w_b, w_c = smooth_weights(e_0, e_1, t)
    for slot, part in enumerate((w_a, w_b, w_c, t)):
        u_ref[slot, pl.ds(u_row, 8), :] = part
    left, right = biased_parts(
        u_ref[0, pl.ds(p_row + 1, 8), :],
        u_ref[1, pl.ds(p_row, 8), :],
        u_ref[2, pl.ds(p_row - 1, 8), :],
        u_ref[3, pl.ds(p_row - 1, 8), :],
        u_ref[3, pl.ds(p_row, 8), :],
        u_ref[3, pl.ds(p_row + 1, 8), :],
    )
    p_ref[0, pl.ds(p_row, 8), :] = left
    p_ref[1, pl.ds(p_row, 8), :] = right
    centre = 3.0 * (rows(9) - rows(7))
    return upwind_square(
        centre, p_ref[0, pl.ds(7, 8), :], p_ref[1, pl.ds(8, 8), :], sigma
    )


def z_faces(source, zlo, zhi):
    for chunk in range(CX // 8):
        columns = slice(8 * CY * chunk, 8 * CY * (chunk + 1))
        for parity in range(2):
            part = source[8 * chunk : 8 * chunk + 8, :, 128 * parity : 128 * parity + 128]
            part = part.reshape(8 * CY, 128).T
            for k in range(4):
                zlo[2 * k + parity : 2 * k + parity + 1, columns] = part[k : k + 1]
                zhi[2 * k + parity : 2 * k + parity + 1, columns] = part[124 + k : 125 + k]


def y_faces(source, ylo, yhi, width):
    for x in range(CX):
        for k in range(width):
            ylo[k, x : x + 1, :] = source[x, k : k + 1, :]
            yhi[k, x : x + 1, :] = source[x, CY - width + k : CY - width + 1 + k, :]


def write_swap(parity, low, high, out_a, out_b):
    odd = parity == 1
    out_a[...] = jnp.where(odd, low, high)
    if out_b.shape == out_a.shape:
        out_b[...] = jnp.where(odd, high, low)
    else:
        out_b[...] = jnp.zeros(out_b.shape, F32)
        out_b[0:8] = jnp.where(odd, high, low)


def side_faces_kernel(with_signs, parity, source, *refs):
    xa, xb, ya, yb = refs[:4]
    yf = refs[-1]
    y_faces(source, yf.at[0], yf.at[1], 3)
    write_swap(parity[1], yf[0], yf[1], ya, yb)
    write_swap(parity[0], source[0:3], source[CX - 3 : CX], xa, xb)
    if with_signs:
        sigma, pace = refs[4:6]

        def signs(x, carry):
            value = source[x]
            sigma[x] = sigma_of(value)
            pace[x] = (0.05 * value) * lax.rsqrt(value * value + 1.0)
            return carry

        lax.fori_loop(0, CX, signs, 0)


def write_z_faces(parity, source, za, zb, zf):
    z_faces(source, zf.at[0], zf.at[1])
    write_swap(parity[2], zf[0], zf[1], za, zb)


def low_high(parity, part_a, part_b):
    odd = parity == 1
    return jnp.where(odd, part_a, part_b), jnp.where(odd, part_b, part_a)


def pack_kernel(parity, phi, mixed, za, zb, turned, zf):
    for chunk in range(CX // 8):
        planes = slice(8 * chunk, 8 * chunk + 8)
        for half in range(2):
            part = phi[planes, :, 128 * half : 128 * half + 128]
            part = part.reshape(8 * CY, 128).T
            for c in range(3):
                turned[c, 128 * half : 128 * half + 128, :] = part[:, 128 * c : 128 * c + 128]
        for which in range(2):
            part = [turned[c, pl.ds(which, 128, stride=2), :].T for c in range(3)]
            part = jnp.concatenate(part, axis=0)
            mixed[planes, :, 128 * which : 128 * which + 128] = part.reshape(8, CY, 128)
    write_z_faces(parity, mixed, za, zb, zf)


def unpack_kernel(mixed, out, turned):
    for chunk in range(CX // 8):
        planes = slice(8 * chunk, 8 * chunk + 8)
        for parity in range(2):
            part = mixed[planes, :, 128 * parity : 128 * parity + 128]
            part = part.reshape(8 * CY, 128).T
            for c in range(3):
                turned[c, pl.ds(parity, 128, stride=2), :] = part[:, 128 * c : 128 * c + 128]
        for half in range(2):
            part = [turned[c, 128 * half : 128 * half + 128, :].T for c in range(3)]
            part = jnp.concatenate(part, axis=0)
            out[planes, :, 128 * half : 128 * half + 128] = part.reshape(8, CY, 128)


def step_kernel(
    last,
    parity, sigma_in, pace, za0, zb0, v, za_own, zb_own, xa_in, xb_in, ya_in, yb_in, za_in, zb_in,
    *refs,
):
    faces = 6 if last else 3
    step_body(last, parity, sigma_in, pace, za0, zb0, v, za_own, zb_own, xa_in, xb_in, ya_in,
              yb_in, za_in, zb_in, refs[:faces], *refs[faces:])


def step_body(
    last,
    parity, sigma_in, pace, za0, zb0, v, za_own, zb_own, xa_in, xb_in, ya_in, yb_in, za_in, zb_in,
    outs,
    vs, summed, u_ref, p_ref, window, zu_ref, zp_ref, edges, fixes, yf, zf, xh,
    rolled, zs, zp, tots,
):
    out = outs[0]

    def fill(x, carry):
        for zt in range(2):
            vs[zt, x, 8 : 8 + CY, :] = v[x, :, pl.ds(128 * zt, 128)]
        return carry

    lax.fori_loop(0, CX, fill, 0)
    yf[0], yf[1] = low_high(parity[1], ya_in[...], yb_in[...])
    for x in range(CX):
        for zt in range(2):
            lanes = slice(128 * zt, 128 * zt + 128)
            for k in range(3):
                vs[zt, x, 5 + k : 6 + k, :] = yf[0, k, x : x + 1, lanes]
                vs[zt, x, 8 + CY + k : 9 + CY + k, :] = yf[1, k, x : x + 1, lanes]
    xh[0], xh[1] = low_high(parity[0], xa_in[...], xb_in[...])

    z_low, z_high = low_high(parity[2], za_in[...], zb_in[0:8])
    zlo0, zhi0 = low_high(parity[2], za0[...], zb0[0:8])
    zlo_own, zhi_own = low_high(parity[2], za_own[...], zb_own[0:8])
    window[5:8, :] = z_low[5:8]
    window[8:16, :] = zlo_own
    fixed = edge_column(window, zu_ref, zp_ref, 6, 7, sigma_of(zlo0))
    for half, lane_at, cell_at in ((0, 0, 0), (0, 1, 2), (1, 0, 1)):
        edges[half, lane_at : lane_at + 1, :] = fixed[cell_at : cell_at + 1]
    window[8:16, :] = zhi_own
    window[16:19, :] = z_high[0:3]
    fixed = edge_column(window, zu_ref, zp_ref, 9, 8, sigma_of(zhi0))
    for half, lane_at, cell_at in ((0, 127, 6), (1, 126, 5), (1, 127, 7)):
        edges[half, lane_at : lane_at + 1, :] = fixed[cell_at : cell_at + 1]
    for half in range(2):
        fixes[half] = edges[half].T

    def x_pass(yt, carry):
        row = pl.multiple_of(8 * yt, 8)
        for zt in range(2):
            lanes = pl.ds(128 * zt, 128)

            def cell(x):
                if x < 0:
                    return xh[0, 3 + x, pl.ds(row, 8), lanes]
                if x >= CX:
                    return xh[1, x - CX, pl.ds(row, 8), lanes]
                return v[x, pl.ds(row, 8), lanes]

            d, e, t, weights, lefts, rights = {}, {}, {}, {}, {}, {}
            d[-3] = cell(-2) - cell(-3)
            d[-2] = cell(-1) - cell(-2)
            e[-2] = d[-2] - d[-3]
            for j in range(-2, CX + 1):
                d[j + 1] = cell(j + 2) - cell(j + 1)
                e[j + 1] = d[j + 1] - d[j]
                t[j] = e[j + 1] - e[j]
                weights[j] = smooth_weights(e[j], e[j + 1], t[j])
                p = j - 1
                if p >= -1:
                    lefts[p], rights[p] = biased_parts(
                        weights[p + 1][0], weights[p][1], weights[p - 1][2], t[p - 1], t[p], t[p + 1]
                    )
                if p >= 0:
                    sigma = sigma_in[p, pl.ds(row, 8), lanes]
                    centre = 3.0 * (d[p - 1] + d[p])
                    summed[zt, p, pl.ds(row, 8), :] = upwind_square(
                        centre, lefts[p - 1], rights[p], sigma
                    )
        return carry

    lax.fori_loop(0, YT, x_pass, 0)

    lane = lax.broadcasted_iota(jnp.int32, (8, 128), 1)
    fix_even = (lane < 2) | (lane == 127)
    fix_odd = (lane < 1) | (lane > 125)

    def y_weights(x, zt, k):
        start = 6 + 8 * k
        e_0, e_1, t = from_values(
            *[vs[zt, x, pl.ds(start + shift, 8), :] for shift in (-1, 0, 1, 2)]
        )
        w_a, w_b, w_c = smooth_weights(e_0, e_1, t)
        for slot, part in enumerate((w_a, w_b, w_c, t)):
            u_ref[zt, slot, pl.ds(8 * k, 8), :] = part

    def y_parts(zt, k):
        def read(slot, row):
            return u_ref[zt, slot, pl.ds(row, 8), :]

        row = 8 * k + 1
        left, right = biased_parts(
            read(0, row + 1), read(1, row), read(2, row - 1),
            read(3, row - 1), read(3, row), read(3, row + 1),
        )
        p_ref[zt, 0, pl.ds(8 * k, 8), :] = left
        p_ref[zt, 1, pl.ds(8 * k, 8), :] = right

    def tile(x, zt, k):
        return v[x, 8 * k : 8 * k + 8, 128 * zt : 128 * zt + 128]

    def sigma_at(x, zt, k):
        return sigma_in[x, 8 * k : 8 * k + 8, 128 * zt : 128 * zt + 128]

    def stage_0(x):
        for k in range(YT):
            rows = slice(8 * k, 8 * k + 8)
            for slot, part in enumerate((tile(x, 0, k), tile(x, 1, k))):
                rolled[slot, rows, :] = lane_down(part)
                rolled[2 + slot, rows, :] = lane_up(part)
        for zt in range(2):
            for k in range(YT + 1):
                y_weights(x, zt, k)

    def stage_1(x):
        for k in range(YT):
            rows = slice(8 * k, 8 * k + 8)
            parts = z_stage_weights(
                tile(x, 0, k), tile(x, 1, k), *[rolled[slot, rows, :] for slot in range(4)]
            )
            for slot, part in enumerate(parts):
                zs[slot, rows, :] = part
        for zt in range(2):
            for k in range(YT + 1):
                y_parts(zt, k)

    def stage_2(x):
        for k in range(YT):
            rows = slice(8 * k, 8 * k + 8)
            parts = z_stage_parts(*[zs[slot, rows, :] for slot in range(12)])
            for slot, part in enumerate(parts):
                zp[slot, rows, :] = part
        for zt in range(2):
            for k in range(YT):
                rows = slice(8 * k, 8 * k + 8)
                centre = 3.0 * (
                    vs[zt, x, 9 + 8 * k : 17 + 8 * k, :] - vs[zt, x, 7 + 8 * k : 15 + 8 * k, :]
                )
                tots[zt, rows, :] = summed[zt, x, rows, :] + upwind_square(
                    centre, p_ref[zt, 0, rows, :], p_ref[zt, 1, 8 * k + 1 : 8 * k + 9, :],
                    sigma_at(x, zt, k),
                )

    def stage_3(x):
        flat = pl.multiple_of(x * CY, 8)
        for k in range(YT):
            rows = slice(8 * k, 8 * k + 8)
            for zt in range(2):
                sigma = sigma_at(x, zt, k)
                if zt == 0:
                    along = upwind_pair(zp[0, rows, :] - zp[1, rows, :], zp[2, rows, :], sigma)
                    edge = fix_even
                else:
                    along = upwind_pair(zp[3, rows, :], zp[4, rows, :], sigma)
                    edge = fix_odd
                along = jnp.where(edge, fixes[zt, pl.ds(flat + 8 * k, 8), :], along)
                total = tots[zt, rows, :] + along
                root = total * lax.rsqrt(jnp.maximum(total, 1e-30))
                lanes = slice(128 * zt, 128 * zt + 128)
                out[x, rows, lanes] = v[x, rows, lanes] - pace[x, rows, lanes] * (root - 6.0)

    stages = (stage_3, stage_2, stage_1, stage_0)

    def run(at, low, high):
        for delay, stage in zip((3, 2, 1, 0), stages):
            if low <= delay <= high:
                stage(at - delay)

    def yz_pass(at, carry):
        run(at, 0, 3)
        return carry

    for at in range(3):
        run(at, 0, at)
    lax.fori_loop(3, CX, yz_pass, 0)
    for at in range(3):
        run(CX + at, at + 1, 3)
    if last:
        xa, xb, ylo, yhi, planes = outs[1:]
        write_swap(parity[0], out[0:1], out[CX - 1 : CX], xa, xb)
        y_faces(out, ylo, yhi, 2)
        planes[...] = jnp.zeros((4, CX, 128), F32)
        for chunk in range(CX // 8):
            for half in range(2):
                part = out[8 * chunk : 8 * chunk + 8, :, 128 * half : 128 * half + 128]
                part = part.reshape(8 * CY, 128).T
                for x in range(8):
                    lanes = slice(CY * x, CY * x + CY)
                    at = slice(8 * chunk + x, 8 * chunk + x + 1)
                    planes[half, at, 0:CY] = part[0:1, lanes]
                    planes[2 + half, at, 0:CY] = part[127:128, lanes]
    else:
        write_z_faces(parity, out, *outs[1:], zf)


def rows_kernel(parity, xa, xb, ylo, yhi, ya, yb, y_rows):
    x_low, x_high = low_high(parity[0], xa[0], xb[0])
    for at, (source, layer, row) in enumerate(
        ((ylo, 0, 0), (ylo, 1, 1), (yhi, 0, CY - 2), (yhi, 1, CY - 1))
    ):
        y_rows[at, 0:1, :] = x_low[row : row + 1]
        y_rows[at, 1 : CX + 1, :] = source[layer]
        y_rows[at, CX + 1 : CX + 2, :] = x_high[row : row + 1]
    write_swap(parity[1], y_rows[0], y_rows[3], ya, yb)


def planes_kernel(parity, xa, xb, ya, yb, own, planes, za, zb):
    x_sides = low_high(parity[0], xa[0], xb[0])
    y_low, y_high = low_high(parity[1], ya[...], yb[...])
    planes[...] = jnp.zeros((4, 40, 128), F32)
    for q in range(4):
        planes[q, 1 : CX + 1, :] = own[q]
    for side in range(2):
        row = (CX + 1) * side
        for half in range(2):
            turned = x_sides[side][:, 128 * half : 128 * half + 128].T
            planes[half, row : row + 1, 0:CY] = turned[0:1]
            planes[2 + half, row : row + 1, 0:CY] = turned[127:128]
    lane = lax.broadcasted_iota(jnp.int32, (CX + 2, 128), 1)
    for q in range(4):
        lanes = slice(128 * (q % 2), 128 * (q % 2) + 128)
        start = 0 if q < 2 else 127
        low = y_low[:, lanes]
        if start != 127:
            low = pltpu.roll(low, 127 - start, 1)
        high = pltpu.roll(y_high[:, lanes], (CY - start) % 128, 1)
        planes[q, 0 : CX + 2, :] = jnp.where(
            lane == 127, low, jnp.where(lane == CY, high, planes[q, 0 : CX + 2, :])
        )
    write_swap(parity[2], planes[0], planes[3], za, zb)


def face_shapes(width):
    shapes = [(width, CY, CZ)] * 2 + [(max(width, 2), CX, CZ)] * 2
    shapes += [(8, ROWS)] * 2 if width == 3 else [(4, CX, 128)]
    return [jax.ShapeDtypeStruct(shape, F32) for shape in shapes]


def row_faces(parity, xa, xb, ylo, yhi):
    return pl.pallas_call(
        rows_kernel,
        out_shape=[jax.ShapeDtypeStruct((CX + 2, CZ), F32)] * 2
        + [jax.ShapeDtypeStruct((4, CX + 2, CZ), F32)],
        in_specs=parity_specs(4),
        out_specs=vmem_specs(3),
        compiler_params=pltpu.CompilerParams(vmem_limit_bytes=VMEM_LIMIT),
        name="row_faces",
    )(parity, xa, xb, ylo, yhi)


def plane_faces(parity, xa, xb, ya, yb, own):
    return pl.pallas_call(
        planes_kernel,
        out_shape=[jax.ShapeDtypeStruct(shape, F32) for shape in ((4, 40, 128), (40, 128), (40, 128))],
        in_specs=parity_specs(5),
        out_specs=vmem_specs(3),
        compiler_params=pltpu.CompilerParams(vmem_limit_bytes=VMEM_LIMIT),
        name="plane_faces",
    )(parity, xa, xb, ya, yb, own)


BLOCK = jax.ShapeDtypeStruct((CX, CY, CZ), F32)
FACE_SCRATCH = [pltpu.VMEM((2, 3, CX, CZ), F32), pltpu.VMEM((2, 8, ROWS), F32)]


def vmem_specs(count):
    return [pl.BlockSpec(memory_space=pltpu.VMEM)] * count


def parity_specs(count):
    return [pl.BlockSpec(memory_space=pltpu.SMEM)] + vmem_specs(count)


Z_FACE = jax.ShapeDtypeStruct((8, ROWS), F32)
Z_LONG = jax.ShapeDtypeStruct((Z_SENT, ROWS), F32)


def pack(parity, phi):
    return pl.pallas_call(
        pack_kernel,
        out_shape=[BLOCK, Z_FACE, Z_LONG],
        in_specs=parity_specs(1),
        out_specs=vmem_specs(3),
        scratch_shapes=[pltpu.VMEM((3, CZ, 128), F32), pltpu.VMEM((2, 8, ROWS), F32)],
        compiler_params=pltpu.CompilerParams(vmem_limit_bytes=VMEM_LIMIT),
        name="pack",
    )(parity, phi)


def side_faces(parity, source, with_signs):
    shapes = face_shapes(3)[:4] + [BLOCK] * (2 if with_signs else 0)
    return pl.pallas_call(
        functools.partial(side_faces_kernel, with_signs),
        out_shape=shapes,
        in_specs=parity_specs(1),
        out_specs=vmem_specs(len(shapes)),
        scratch_shapes=[pltpu.VMEM((2, 3, CX, CZ), F32)],
        compiler_params=pltpu.CompilerParams(vmem_limit_bytes=VMEM_LIMIT),
        cost_estimate=pl.CostEstimate(flops=20000000, bytes_accessed=6000000, transcendentals=400000),
        name="side_faces",
    )(parity, source)


def unpack(mixed):
    return pl.pallas_call(
        unpack_kernel,
        out_shape=BLOCK,
        in_specs=vmem_specs(1),
        out_specs=vmem_specs(1)[0],
        scratch_shapes=[pltpu.VMEM((3, CZ, 128), F32)],
        compiler_params=pltpu.CompilerParams(vmem_limit_bytes=VMEM_LIMIT),
        name="unpack",
    )(mixed)


def step(parity, sigma_in, pace, za0, zb0, v, za_own, zb_own, halos, last):
    return pl.pallas_call(
        functools.partial(step_kernel, last),
        out_shape=[BLOCK] + (face_shapes(1) if last else [Z_FACE, Z_LONG]),
        in_specs=parity_specs(13),
        out_specs=vmem_specs(6 if last else 3),
        scratch_shapes=[
            pltpu.VMEM((2, CX, 64, 128), F32),
            pltpu.VMEM((2, CX, CY, 128), F32),
            pltpu.VMEM((2, 4, 64, 128), F32),
            pltpu.VMEM((2, 2, 64, 128), F32),
            pltpu.VMEM((24, ROWS), F32),
            pltpu.VMEM((4, 24, ROWS), F32),
            pltpu.VMEM((2, 24, ROWS), F32),
            pltpu.VMEM((2, 128, ROWS), F32),
            pltpu.VMEM((2, ROWS, 128), F32),
        ]
        + FACE_SCRATCH
        + [
            pltpu.VMEM((2, 3, CY, CZ), F32),
            pltpu.VMEM((4, CY, 128), F32),
            pltpu.VMEM((12, CY, 128), F32),
            pltpu.VMEM((5, CY, 128), F32),
            pltpu.VMEM((2, CY, 128), F32),
        ],
        compiler_params=pltpu.CompilerParams(vmem_limit_bytes=VMEM_LIMIT),
        name="step",
    )(parity, sigma_in, pace, za0, zb0, v, za_own, zb_own, *halos)


HALF_COS = [
    0.9999999991256178, -0.23370050635094053, 0.019968606689123116,
    -0.0008935362743290266, 2.3601076640059624e-05,
]
BAND_SQUARE = 1.5 * 1.5


def half_cosine(value):
    square = jnp.minimum(value * value, BAND_SQUARE)
    shape = F32(HALF_COS[4] / BAND_SQUARE**5)
    for k in (3, 2, 1, 0):
        shape = shape * square + F32(HALF_COS[k] / BAND_SQUARE ** (k + 1))
    return (BAND_SQUARE - square) * shape


def five_terms(centre, keep, dx, sx, dy, sy, dz, sz, dxy, dxz, dyz):
    twice = centre + centre
    xx, yy, zz = dx * dx, dy * dy, dz * dz
    squares = jnp.maximum(xx + yy + zz, 1.0)
    root = lax.rsqrt(squares)
    bend = (sx - twice) * (yy + zz) + (sy - twice) * (xx + zz) + (sz - twice) * (xx + yy)
    bend = bend - 0.5 * (dx * (dy * dxy + dz * dxz) + dy * dz * dyz)
    cosine = half_cosine(centre)
    spread = cosine * cosine
    if keep is not None:
        spread = jnp.where(keep, spread, 0.0)
    return (
        spread * (squares * root),
        spread * bend * (root * root),
        spread * dx,
        spread * dy,
        spread * dz,
    )


def brick_tables(ids, targets, live_count):
    entry = lax.broadcasted_iota(jnp.int32, (1, SLOTS), 1)
    live = entry < live_count
    row = lax.broadcasted_iota(jnp.int32, (SLOTS, SLOTS), 0)
    column = lax.broadcasted_iota(jnp.int32, (SLOTS, SLOTS), 1)
    owner = targets.astype(F32)
    down = jnp.sum(jnp.where(row == column, owner, 0.0), axis=1, keepdims=True)
    earlier = (row < column) & (row < live_count) & (down == owner)
    rank = jnp.sum(earlier.astype(F32), axis=0, keepdims=True)
    owner_at = jnp.where(live, owner, F32(SLOTS))
    peers = lax.broadcasted_iota(jnp.int32, (PEERS, SLOTS), 0).astype(F32)
    to_slot = [((owner_at == peers) & (rank == F32(c))).astype(F32) for c in range(2)]

    def finder(count, brick_of):
        at = lax.broadcasted_iota(jnp.int32, (count, SLOTS), 0)
        return (ids == brick_of(at)).astype(F32)

    return to_slot, finder


def exact_dot(left, right, dims=(((1,), (0,)), ((), ()))):
    return lax.dot_general(
        left, right, dims, precision=lax.Precision.HIGHEST, preferred_element_type=F32
    )


def neighbours(pair):
    return ((lane_down(pair[1]), pair[1]), (pair[0], lane_up(pair[0])))


def pair_terms(grid, keeps):
    two = range(2)

    def diff(first, second):
        return [grid[first][half] - grid[second][half] for half in two]

    def summed(first, second):
        return [grid[first][half] + grid[second][half] for half in two]

    dx, sx = diff((1, 0), (-1, 0)), summed((1, 0), (-1, 0))
    dy, sy = diff((0, 1), (0, -1)), summed((0, 1), (0, -1))
    over, under = diff((1, 1), (-1, 1)), diff((1, -1), (-1, -1))
    around, dx_around, dy_around = neighbours(grid[0, 0]), neighbours(dx), neighbours(dy)
    results = []
    for half in two:
        results.append(
            five_terms(
                grid[0, 0][half], keeps[half], dx[half], sx[half], dy[half], sy[half],
                around[half][1] - around[half][0], around[half][1] + around[half][0],
                over[half] - under[half],
                dx_around[half][1] - dx_around[half][0],
                dy_around[half][1] - dy_around[half][0],
            )
        )
    return [results[0][n] + results[1][n] for n in range(5)]


STAR = [(0, 0), (1, 0), (-1, 0), (0, 1), (0, -1), (1, 1), (1, -1), (-1, 1), (-1, -1)]


def tile_terms(vs, plane, k, keeps):
    grid = {
        (sx, sy): [vs[half, plane + sx, pl.ds(8 + 8 * k + sy, 8), :] for half in range(2)]
        for sx, sy in STAR
    }
    return pair_terms(grid, keeps)


def z_keeps(rows):
    lane = lax.broadcasted_iota(jnp.int32, (rows, 128), 1)
    return [lane != 0, lane != 127]


def inner_kernel(v, stack, vs):
    def fill(x, carry):
        for half in range(2):
            vs[half, x, 8 : 8 + CY, :] = v[x, :, pl.ds(128 * half, 128)]
            vs[half, x, 7:8, :] = jnp.zeros((1, 128), F32)
            vs[half, x, 8 + CY : 9 + CY, :] = jnp.zeros((1, 128), F32)
        return carry

    lax.fori_loop(0, CX, fill, 0)
    keeps = z_keeps(8)
    row = lax.broadcasted_iota(jnp.int32, (8, 128), 0)
    first = [keep & (row != 0) for keep in keeps]
    last = [keep & (row != 7) for keep in keeps]
    zeros = jnp.zeros((8, 128), F32)
    for bx in range(2):

        def body(step_at, sums):
            sums = list(sums)
            for sub in range(3):
                x = BRICK * bx + (1 - bx) + 3 * step_at + sub
                for k in range(YT):
                    parts = tile_terms(vs, x, k, first if k == 0 else last if k == 5 else keeps)
                    for n in range(5):
                        slot = 5 * (k // 2) + n
                        sums[slot] = sums[slot] + parts[n]
            return tuple(sums)

        sums = lax.fori_loop(0, 5, body, (zeros,) * 15)
        for by in range(3):
            row_at = 8 * (3 * bx + by)
            for n in range(5):
                total = jnp.sum(sums[5 * by + n], axis=0, keepdims=True)
                stack[row_at + n : row_at + n + 1, :] = total
            stack[row_at + 5 : row_at + 8, :] = jnp.zeros((3, 128), F32)


def edge_kernel(
    parity, count, inner, v, xa, xb, ya, yb, za, zb, y_rows, planes, ids, targets, record,
    vs, stack,
):
    x_sides = low_high(parity[0], xa[0], xb[0])
    y_sides = low_high(parity[1], ya[...], yb[...])
    under, over = low_high(parity[2], za[...], zb[...])
    stack[...] = inner[...]

    def add(b, n, row):
        stack[8 * b + n : 8 * b + n + 1, :] += row

    keeps = z_keeps(8)
    for side in range(2):
        for half in range(2):
            lanes = slice(128 * half, 128 * half + 128)
            for at in range(3):
                x = at - 1 if side == 0 else CX - 2 + at
                if 0 <= x < CX:
                    vs[half, at, 8 : 8 + CY, :] = v[x, :, lanes]
                else:
                    vs[half, at, 8 : 8 + CY, :] = x_sides[side][:, lanes]
                vs[half, at, 7:8, :] = y_sides[0][x + 1 : x + 2, lanes]
                vs[half, at, 8 + CY : 9 + CY, :] = y_sides[1][x + 1 : x + 2, lanes]
        for by in range(3):
            parts = [tile_terms(vs, 1, 2 * by + sub, keeps) for sub in range(2)]
            for n in range(5):
                add(3 * side + by, n, jnp.sum(parts[0][n] + parts[1][n], axis=0, keepdims=True))

    keeps = z_keeps(16)
    row = lax.broadcasted_iota(jnp.int32, (16, 128), 0)
    for side in range(2):
        if side == 0:
            rows = (y_sides[0], y_rows[0], y_rows[1])
        else:
            rows = (y_rows[2], y_rows[3], y_sides[1])
        for bx in range(2):
            grid = {
                (sx, sy): [
                    rows[1 + sy][1 + 16 * bx + sx : 17 + 16 * bx + sx, 128 * half : 128 * half + 128]
                    for half in range(2)
                ]
                for sx, sy in STAR
            }
            inside = row != (0 if bx == 0 else 15)
            parts = pair_terms(grid, [keep & inside for keep in keeps])
            for n in range(5):
                add(3 * bx + 2 * side, n, jnp.sum(parts[n], axis=0, keepdims=True))

    to_slot, finder = brick_tables(ids[...], targets[...], count[0])
    found = jnp.zeros((8, SLOTS), F32)
    for b in range(6):
        found = found + exact_dot(
            stack[8 * b : 8 * b + 8, :], finder(128, lambda at: 16 * b + at // 8)
        )
    for side in range(2):
        window = (under, planes[0], planes[1]) if side == 0 else (planes[2], planes[3], over)

        def cut(plane, step_x, step_y):
            part = window[plane][1 + step_x : 33 + step_x]
            return pltpu.roll(part, (-step_y) % 128, 1) if step_y else part

        high, low = cut(1, 1, 0), cut(1, -1, 0)
        right, left = cut(1, 0, 1), cut(1, 0, -1)
        above, below = cut(2, 0, 0), cut(0, 0, 0)
        terms = five_terms(
            cut(1, 0, 0), None,
            high - low, high + low, right - left, right + left, above - below, above + below,
            (cut(1, 1, 1) - cut(1, -1, 1)) - (cut(1, 1, -1) - cut(1, -1, -1)),
            (cut(2, 1, 0) - cut(2, -1, 0)) - (cut(0, 1, 0) - cut(0, -1, 0)),
            (cut(2, 0, 1) - cut(2, 0, -1)) - (cut(0, 0, 1) - cut(0, 0, -1)),
        )
        for bx in range(2):
            rows = [jnp.sum(term[16 * bx : 16 * bx + 16], axis=0, keepdims=True) for term in terms]
            rows = jnp.concatenate(rows + [jnp.zeros((3, 128), F32)], axis=0)
            found = found + exact_dot(
                rows,
                finder(
                    128,
                    lambda at: jnp.where(at < CY, 48 * bx + 16 * (at // 16) + 15 * side, -1),
                ),
            )
    scale = 2.0 / 3.0 / (BRICK * BRICK)
    row = lax.broadcasted_iota(jnp.int32, (8, SLOTS), 0)
    found = found * jnp.where(row == 1, F32(scale), F32(0.5 * scale))
    for c in range(2):
        record[:, 8 * c : 8 * c + 8] = exact_dot(to_slot[c], found, (((1,), (1,)), ((), ())))


def arrange_kernel(received, out):
    source = lax.broadcasted_iota(jnp.int32, (PEERS, SLOTS), 0)
    slot = lax.broadcasted_iota(jnp.int32, (PEERS, SLOTS), 1)
    total = jnp.zeros((8, SLOTS), F32)
    for c in range(2):
        total = total + exact_dot(
            received[:, 8 * c : 8 * c + 8], (slot == 2 * source + c).astype(F32),
            (((0,), (0,)), ((), ())),
        )
    out[...] = total[0:5]


def arrange(received):
    return pl.pallas_call(
        arrange_kernel,
        out_shape=jax.ShapeDtypeStruct((5, SLOTS), F32),
        in_specs=vmem_specs(1),
        out_specs=vmem_specs(1)[0],
        compiler_params=pltpu.CompilerParams(vmem_limit_bytes=VMEM_LIMIT),
        name="arrange",
    )(received)


def inner_bricks(v):
    return pl.pallas_call(
        inner_kernel,
        out_shape=jax.ShapeDtypeStruct((48, 128), F32),
        in_specs=vmem_specs(1),
        out_specs=vmem_specs(1)[0],
        scratch_shapes=[pltpu.VMEM((2, CX, 64, 128), F32)],
        compiler_params=pltpu.CompilerParams(vmem_limit_bytes=VMEM_LIMIT),
        cost_estimate=pl.CostEstimate(flops=20000000, bytes_accessed=6000000, transcendentals=400000),
        name="inner_bricks",
    )(v)


def edge_bricks(parity, count, inner, v, halos, y_rows, planes, ids, targets):
    return pl.pallas_call(
        edge_kernel,
        out_shape=jax.ShapeDtypeStruct((PEERS, 16), F32),
        in_specs=[pl.BlockSpec(memory_space=pltpu.SMEM)] * 2 + vmem_specs(12),
        out_specs=vmem_specs(1)[0],
        scratch_shapes=[
            pltpu.VMEM((2, 3, 64, 128), F32),
            pltpu.VMEM((48, 128), F32),
        ],
        compiler_params=pltpu.CompilerParams(vmem_limit_bytes=VMEM_LIMIT),
        name="edge_bricks",
    )(parity, count, inner, v, *halos, y_rows, planes, ids, targets)


def swap(value, axis, phase):
    count = lax.axis_size(axis)
    if phase == 0:
        pairs = [(i, i ^ 1) for i in range(count)]
    else:
        pairs = [(i, (i - 1 if i % 2 == 0 else i + 1) % count) for i in range(count)]
    return lax.ppermute(value, axis, pairs)


def exchange(v, za, zb, parity, with_signs):
    zb = swap(zb, "gz", 1)
    za = swap(za, "gz", 0)
    xa, xb, ya, yb, *signs = side_faces(parity, v, with_signs)
    yb = swap(yb, "gy", 1)
    ya = swap(ya, "gy", 0)
    xb = swap(xb, "gx", 1)
    xa = swap(xa, "gx", 0)
    return (xa, xb, ya, yb, za, zb), signs


def per_device(phi_start, band_ids, band_count, owners):
    parity = jnp.stack([lax.axis_index(name) % 2 for name in ("gx", "gy", "gz")])
    parity = parity.astype(jnp.int32)
    v, za0, zb0 = pack(parity, phi_start)
    halos, (sigma, pace) = exchange(v, za0, zb0, parity, True)
    za, zb = za0, zb0
    for number in range(STEPS - 1):
        v, za, zb = step(parity, sigma, pace, za0, zb0, v, za, zb, halos, False)
        halos, _ = exchange(v, za, zb, parity, False)
    v, *faces = step(parity, sigma, pace, za0, zb0, v, za, zb, halos, True)
    level_set = unpack(v)

    xa, xb, ylo, yhi, own = faces
    xb = swap(xb, "gx", 1)
    xa = swap(xa, "gx", 0)
    ya, yb, y_rows = row_faces(parity, xa, xb, ylo, yhi)
    inner = inner_bricks(v)
    yb = swap(yb, "gy", 1)
    ya = swap(ya, "gy", 0)
    ya, yb, inner = lax.optimization_barrier((ya, yb, inner))
    planes, za, zb = plane_faces(parity, xa, xb, ya, yb, own)
    zb = swap(zb, "gz", 1)
    za = swap(za, "gz", 0)
    record = edge_bricks(
        parity, band_count.reshape(1), inner, v, (xa, xb, ya, yb, za, zb), y_rows, planes,
        band_ids.reshape(1, SLOTS), owners.reshape(1, SLOTS),
    )
    received = lax.all_to_all(record, ("gx", "gy"), split_axis=0, concat_axis=0, tiled=True)
    return level_set, arrange(received).reshape(1, 1, 1, 5, SLOTS)


def solution(mesh):
    placed = (
        P("gx", "gy", "gz"),
        P("gx", "gy", "gz", None),
        P("gx", "gy", "gz"),
        P("gx", "gy", "gz", None),
    )
    return jax.shard_map(
        per_device,
        mesh=mesh,
        in_specs=placed,
        out_specs=(P("gx", "gy", "gz"), P("gx", "gy", "gz", None, None)),
        check_vma=False,
    )
```

```python
import functools

import jax
import jax.numpy as jnp
from jax import lax
from jax.experimental import pallas as pl
from jax.experimental.pallas import tpu as pltpu
from jax.sharding import PartitionSpec as P

STEPS = 3
BRICK = 16
SLOTS = 64
PEERS = 32
CX, CY, CZ = 32, 48, 256
ROWS = CX * CY
YT = CY // 8
WENO_EPS = 1e-06
F32 = jnp.float32
VMEM_LIMIT = 16 * 1024 * 1024


def rcp(value):
    return pltpu.reciprocal(value, approx=True)


def smooth_weights(e_low, e_high, third):
    twice = third + third
    middle = e_low * e_high + (third * third * (4.0 / 3.0) + WENO_EPS)
    q_a = rcp(middle - e_low * twice)
    q_b = rcp(middle)
    q_c = rcp(middle + e_high * twice)
    return q_a * q_a, 6.0 * (q_b * q_b), q_c * q_c


def biased_parts(wa_next, wb, wc_prev, t_prev, t_here, t_next):
    x = wc_prev * (t_here - t_prev)
    y = wa_next * (t_next - t_here)
    both = x + y
    both = both + both
    total = (wa_next + wb) + wc_prev
    left = t_here + (both + y) * rcp(total + (wa_next + wa_next))
    right = t_here - (both + x) * rcp(total + (wc_prev + wc_prev))
    return left, right


def upwind_square(centre, left, right, sigma):
    return upwind_pair(centre - left, right - centre, sigma)


def upwind_pair(left, right_back, sigma):
    best = jnp.maximum(sigma * left, sigma * right_back)
    best = jnp.maximum(best, 0.0)
    return best * best


def sigma_of(value):
    return jnp.where(value > 0.0, F32(1.0), F32(-1.0))


def from_values(v_m, v_0, v_1, v_2):
    d_m, d_0, d_1 = v_0 - v_m, v_1 - v_0, v_2 - v_1
    e_0, e_1 = d_0 - d_m, d_1 - d_0
    return e_0, e_1, e_1 - e_0


def lane_down(part):
    return pltpu.roll(part, 1, 1)


def lane_up(part):
    return pltpu.roll(part, 127, 1)


def z_stage_weights(even, odd, even_down, odd_down, even_up, odd_up):
    v = {-2: even_down, -1: odd_down, 0: even, 1: odd, 2: even_up, 3: odd_up}
    d = {k: v[k + 1] - v[k] for k in range(-2, 3)}
    e = {k: d[k] - d[k - 1] for k in range(-1, 3)}
    t = {k: e[k + 1] - e[k] for k in range(-1, 2)}
    w_0 = smooth_weights(e[0], e[1], t[0])
    w_1 = smooth_weights(e[1], e[2], t[1])
    return (
        w_1[0], w_0[1], lane_down(w_1[2]), t[-1], t[0], t[1],
        lane_up(w_0[0]), w_1[1], w_0[2], lane_up(t[0]),
        3.0 * (d[-1] + d[0]), 3.0 * (d[0] + d[1]),
    )


def z_stage_parts(wa_0, wb_0, wc_0, t_m, t_0, t_1, wa_1, wb_1, wc_1, t_2, centre_0, centre_1):
    left_0, right_0 = biased_parts(wa_0, wb_0, wc_0, t_m, t_0, t_1)
    left_1, right_1 = biased_parts(wa_1, wb_1, wc_1, t_0, t_1, t_2)
    return centre_0, lane_down(left_1), right_0 - centre_0, centre_1 - left_0, right_1 - centre_1


def edge_column(window, u_ref, p_ref, u_row, p_row, sigma):
    def rows(start):
        return window[pl.ds(start, 8), :]

    e_0, e_1, t = from_values(rows(u_row - 1), rows(u_row), rows(u_row + 1), rows(u_row + 2))
    w_a, w_b, w_c = smooth_weights(e_0, e_1, t)
    for slot, part in enumerate((w_a, w_b, w_c, t)):
        u_ref[slot, pl.ds(u_row, 8), :] = part
    left, right = biased_parts(
        u_ref[0, pl.ds(p_row + 1, 8), :],
        u_ref[1, pl.ds(p_row, 8), :],
        u_ref[2, pl.ds(p_row - 1, 8), :],
        u_ref[3, pl.ds(p_row - 1, 8), :],
        u_ref[3, pl.ds(p_row, 8), :],
        u_ref[3, pl.ds(p_row + 1, 8), :],
    )
    p_ref[0, pl.ds(p_row, 8), :] = left
    p_ref[1, pl.ds(p_row, 8), :] = right
    centre = 3.0 * (rows(9) - rows(7))
    return upwind_square(
        centre, p_ref[0, pl.ds(7, 8), :], p_ref[1, pl.ds(8, 8), :], sigma
    )


def z_faces(source, zlo, zhi):
    for chunk in range(CX // 8):
        columns = slice(8 * CY * chunk, 8 * CY * (chunk + 1))
        for parity in range(2):
            part = source[8 * chunk : 8 * chunk + 8, :, 128 * parity : 128 * parity + 128]
            part = part.reshape(8 * CY, 128).T
            for k in range(4):
                zlo[2 * k + parity : 2 * k + parity + 1, columns] = part[k : k + 1]
                zhi[2 * k + parity : 2 * k + parity + 1, columns] = part[124 + k : 125 + k]


def y_faces(source, ylo, yhi, width):
    for x in range(CX):
        for k in range(width):
            ylo[k, x : x + 1, :] = source[x, k : k + 1, :]
            yhi[k, x : x + 1, :] = source[x, CY - width + k : CY - width + 1 + k, :]


def write_swap(parity, low, high, out_a, out_b):
    odd = parity == 1
    out_a[...] = jnp.where(odd, low, high)
    out_b[...] = jnp.where(odd, high, low)


def write_faces(parity, source, xa, xb, ya, yb, za, zb, yf, zf):
    y_faces(source, yf.at[0], yf.at[1], 3)
    write_swap(parity[1], yf[0], yf[1], ya, yb)
    write_swap(parity[0], source[0:3], source[CX - 3 : CX], xa, xb)
    z_faces(source, zf.at[0], zf.at[1])
    write_swap(parity[2], zf[0], zf[1], za, zb)


def low_high(parity, part_a, part_b):
    odd = parity == 1
    return jnp.where(odd, part_a, part_b), jnp.where(odd, part_b, part_a)


def pack_kernel(parity, phi, mixed, sigma, pace, xa, xb, ya, yb, za, zb, turned, yf, zf):
    for chunk in range(CX // 8):
        planes = slice(8 * chunk, 8 * chunk + 8)
        for half in range(2):
            part = phi[planes, :, 128 * half : 128 * half + 128]
            part = part.reshape(8 * CY, 128).T
            for c in range(3):
                turned[c, 128 * half : 128 * half + 128, :] = part[:, 128 * c : 128 * c + 128]
        for which in range(2):
            part = [turned[c, pl.ds(which, 128, stride=2), :].T for c in range(3)]
            part = jnp.concatenate(part, axis=0)
            mixed[planes, :, 128 * which : 128 * which + 128] = part.reshape(8, CY, 128)
    def signs(x, carry):
        value = mixed[x]
        sigma[x] = sigma_of(value)
        pace[x] = (0.05 * value) * lax.rsqrt(value * value + 1.0)
        return carry

    lax.fori_loop(0, CX, signs, 0)
    write_faces(parity, mixed, xa, xb, ya, yb, za, zb, yf, zf)


def unpack_kernel(mixed, out, turned):
    for chunk in range(CX // 8):
        planes = slice(8 * chunk, 8 * chunk + 8)
        for parity in range(2):
            part = mixed[planes, :, 128 * parity : 128 * parity + 128]
            part = part.reshape(8 * CY, 128).T
            for c in range(3):
                turned[c, pl.ds(parity, 128, stride=2), :] = part[:, 128 * c : 128 * c + 128]
        for half in range(2):
            part = [turned[c, 128 * half : 128 * half + 128, :].T for c in range(3)]
            part = jnp.concatenate(part, axis=0)
            out[planes, :, 128 * half : 128 * half + 128] = part.reshape(8, CY, 128)


def x_kernel(parity, sigma_in, v, xa_in, xb_in, summed, xh):
    xh[0], xh[1] = low_high(parity[0], xa_in[...], xb_in[...])

    def x_pass(yt, carry):
        row = pl.multiple_of(8 * yt, 8)
        for zt in range(2):
            lanes = pl.ds(128 * zt, 128)

            def cell(x):
                if x < 0:
                    return xh[0, 3 + x, pl.ds(row, 8), lanes]
                if x >= CX:
                    return xh[1, x - CX, pl.ds(row, 8), lanes]
                return v[x, pl.ds(row, 8), lanes]

            d, e, t, weights, lefts, rights = {}, {}, {}, {}, {}, {}
            d[-3] = cell(-2) - cell(-3)
            d[-2] = cell(-1) - cell(-2)
            e[-2] = d[-2] - d[-3]
            for j in range(-2, CX + 1):
                d[j + 1] = cell(j + 2) - cell(j + 1)
                e[j + 1] = d[j + 1] - d[j]
                t[j] = e[j + 1] - e[j]
                weights[j] = smooth_weights(e[j], e[j + 1], t[j])
                p = j - 1
                if p >= -1:
                    lefts[p], rights[p] = biased_parts(
                        weights[p + 1][0], weights[p][1], weights[p - 1][2], t[p - 1], t[p], t[p + 1]
                    )
                if p >= 0:
                    sigma = sigma_in[p, pl.ds(row, 8), lanes]
                    centre = 3.0 * (d[p - 1] + d[p])
                    summed[zt, p, pl.ds(row, 8), :] = upwind_square(
                        centre, lefts[p - 1], rights[p], sigma
                    )
        return carry

    lax.fori_loop(0, YT, x_pass, 0)


def step_kernel(
    last,
    parity, sigma_in, pace, za0, zb0, v, za_own, zb_own, summed, ya_in, yb_in, za_in, zb_in,
    *refs,
):
    faces = 6 if last else 7
    step_body(last, parity, sigma_in, pace, za0, zb0, v, za_own, zb_own, summed, ya_in,
              yb_in, za_in, zb_in, refs[:faces], *refs[faces:])


def step_body(
    last,
    parity, sigma_in, pace, za0, zb0, v, za_own, zb_own, summed, ya_in, yb_in, za_in, zb_in,
    outs,
    vs, u_ref, p_ref, window, zu_ref, zp_ref, edges, fixes, yf, zf,
    rolled, zs, zp, tots,
):
    out = outs[0]

    def fill(x, carry):
        for zt in range(2):
            vs[zt, x, 8 : 8 + CY, :] = v[x, :, pl.ds(128 * zt, 128)]
        return carry

    lax.fori_loop(0, CX, fill, 0)
    yf[0], yf[1] = low_high(parity[1], ya_in[...], yb_in[...])
    for x in range(CX):
        for zt in range(2):
            lanes = slice(128 * zt, 128 * zt + 128)
            for k in range(3):
                vs[zt, x, 5 + k : 6 + k, :] = yf[0, k, x : x + 1, lanes]
                vs[zt, x, 8 + CY + k : 9 + CY + k, :] = yf[1, k, x : x + 1, lanes]

    z_low, z_high = low_high(parity[2], za_in[...], zb_in[...])
    zlo0, zhi0 = low_high(parity[2], za0[...], zb0[...])
    zlo_own, zhi_own = low_high(parity[2], za_own[...], zb_own[...])
    window[5:8, :] = z_low[5:8]
    window[8:16, :] = zlo_own
    fixed = edge_column(window, zu_ref, zp_ref, 6, 7, sigma_of(zlo0))
    for half, lane_at, cell_at in ((0, 0, 0), (0, 1, 2), (1, 0, 1)):
        edges[half, lane_at : lane_at + 1, :] = fixed[cell_at : cell_at + 1]
    window[8:16, :] = zhi_own
    window[16:19, :] = z_high[0:3]
    fixed = edge_column(window, zu_ref, zp_ref, 9, 8, sigma_of(zhi0))
    for half, lane_at, cell_at in ((0, 127, 6), (1, 126, 5), (1, 127, 7)):
        edges[half, lane_at : lane_at + 1, :] = fixed[cell_at : cell_at + 1]
    for half in range(2):
        fixes[half] = edges[half].T

    lane = lax.broadcasted_iota(jnp.int32, (8, 128), 1)
    fix_even = (lane < 2) | (lane == 127)
    fix_odd = (lane < 1) | (lane > 125)

    def y_weights(x, zt, k):
        start = 6 + 8 * k
        e_0, e_1, t = from_values(
            *[vs[zt, x, pl.ds(start + shift, 8), :] for shift in (-1, 0, 1, 2)]
        )
        w_a, w_b, w_c = smooth_weights(e_0, e_1, t)
        for slot, part in enumerate((w_a, w_b, w_c, t)):
            u_ref[zt, slot, pl.ds(8 * k, 8), :] = part

    def y_parts(zt, k):
        def read(slot, row):
            return u_ref[zt, slot, pl.ds(row, 8), :]

        row = 8 * k + 1
        left, right = biased_parts(
            read(0, row + 1), read(1, row), read(2, row - 1),
            read(3, row - 1), read(3, row), read(3, row + 1),
        )
        p_ref[zt, 0, pl.ds(8 * k, 8), :] = left
        p_ref[zt, 1, pl.ds(8 * k, 8), :] = right

    def tile(x, zt, k):
        return v[x, 8 * k : 8 * k + 8, 128 * zt : 128 * zt + 128]

    def sigma_at(x, zt, k):
        return sigma_in[x, 8 * k : 8 * k + 8, 128 * zt : 128 * zt + 128]

    def stage_0(x):
        for k in range(YT):
            rows = slice(8 * k, 8 * k + 8)
            for slot, part in enumerate((tile(x, 0, k), tile(x, 1, k))):
                rolled[slot, rows, :] = lane_down(part)
                rolled[2 + slot, rows, :] = lane_up(part)
        for zt in range(2):
            for k in range(YT + 1):
                y_weights(x, zt, k)

    def stage_1(x):
        for k in range(YT):
            rows = slice(8 * k, 8 * k + 8)
            parts = z_stage_weights(
                tile(x, 0, k), tile(x, 1, k), *[rolled[slot, rows, :] for slot in range(4)]
            )
            for slot, part in enumerate(parts):
                zs[slot, rows, :] = part
        for zt in range(2):
            for k in range(YT + 1):
                y_parts(zt, k)

    def stage_2(x):
        for k in range(YT):
            rows = slice(8 * k, 8 * k + 8)
            parts = z_stage_parts(*[zs[slot, rows, :] for slot in range(12)])
            for slot, part in enumerate(parts):
                zp[slot, rows, :] = part
        for zt in range(2):
            for k in range(YT):
                rows = slice(8 * k, 8 * k + 8)
                centre = 3.0 * (
                    vs[zt, x, 9 + 8 * k : 17 + 8 * k, :] - vs[zt, x, 7 + 8 * k : 15 + 8 * k, :]
                )
                tots[zt, rows, :] = summed[zt, x, rows, :] + upwind_square(
                    centre, p_ref[zt, 0, rows, :], p_ref[zt, 1, 8 * k + 1 : 8 * k + 9, :],
                    sigma_at(x, zt, k),
                )

    def stage_3(x):
        flat = pl.multiple_of(x * CY, 8)
        for k in range(YT):
            rows = slice(8 * k, 8 * k + 8)
            for zt in range(2):
                sigma = sigma_at(x, zt, k)
                if zt == 0:
                    along = upwind_pair(zp[0, rows, :] - zp[1, rows, :], zp[2, rows, :], sigma)
                    edge = fix_even
                else:
                    along = upwind_pair(zp[3, rows, :], zp[4, rows, :], sigma)
                    edge = fix_odd
                along = jnp.where(edge, fixes[zt, pl.ds(flat + 8 * k, 8), :], along)
                total = tots[zt, rows, :] + along
                root = total * lax.rsqrt(jnp.maximum(total, 1e-30))
                lanes = slice(128 * zt, 128 * zt + 128)
                out[x, rows, lanes] = v[x, rows, lanes] - pace[x, rows, lanes] * (root - 6.0)

    stages = (stage_3, stage_2, stage_1, stage_0)

    def run(at, low, high):
        for delay, stage in zip((3, 2, 1, 0), stages):
            if low <= delay <= high:
                stage(at - delay)

    def yz_pass(at, carry):
        run(at, 0, 3)
        return carry

    for at in range(3):
        run(at, 0, at)
    lax.fori_loop(3, CX, yz_pass, 0)
    for at in range(3):
        run(CX + at, at + 1, 3)
    if last:
        xa, xb, ylo, yhi, planes = outs[1:]
        write_swap(parity[0], out[0:1], out[CX - 1 : CX], xa, xb)
        y_faces(out, ylo, yhi, 2)
        planes[...] = jnp.zeros((4, CX, 128), F32)
        for chunk in range(CX // 8):
            for half in range(2):
                part = out[8 * chunk : 8 * chunk + 8, :, 128 * half : 128 * half + 128]
                part = part.reshape(8 * CY, 128).T
                for x in range(8):
                    lanes = slice(CY * x, CY * x + CY)
                    at = slice(8 * chunk + x, 8 * chunk + x + 1)
                    planes[half, at, 0:CY] = part[0:1, lanes]
                    planes[2 + half, at, 0:CY] = part[127:128, lanes]
    else:
        write_faces(parity, out, *outs[1:], yf, zf)


def rows_kernel(parity, xa, xb, ylo, yhi, ya, yb, y_rows):
    x_low, x_high = low_high(parity[0], xa[0], xb[0])
    for at, (source, layer, row) in enumerate(
        ((ylo, 0, 0), (ylo, 1, 1), (yhi, 0, CY - 2), (yhi, 1, CY - 1))
    ):
        y_rows[at, 0:1, :] = x_low[row : row + 1]
        y_rows[at, 1 : CX + 1, :] = source[layer]
        y_rows[at, CX + 1 : CX + 2, :] = x_high[row : row + 1]
    write_swap(parity[1], y_rows[0], y_rows[3], ya, yb)


def planes_kernel(parity, xa, xb, ya, yb, own, planes, za, zb):
    x_sides = low_high(parity[0], xa[0], xb[0])
    y_low, y_high = low_high(parity[1], ya[...], yb[...])
    planes[...] = jnp.zeros((4, 40, 128), F32)
    for q in range(4):
        planes[q, 1 : CX + 1, :] = own[q]
    for side in range(2):
        row = (CX + 1) * side
        for half in range(2):
            turned = x_sides[side][:, 128 * half : 128 * half + 128].T
            planes[half, row : row + 1, 0:CY] = turned[0:1]
            planes[2 + half, row : row + 1, 0:CY] = turned[127:128]
    lane = lax.broadcasted_iota(jnp.int32, (CX + 2, 128), 1)
    for q in range(4):
        lanes = slice(128 * (q % 2), 128 * (q % 2) + 128)
        start = 0 if q < 2 else 127
        low = y_low[:, lanes]
        if start != 127:
            low = pltpu.roll(low, 127 - start, 1)
        high = pltpu.roll(y_high[:, lanes], (CY - start) % 128, 1)
        planes[q, 0 : CX + 2, :] = jnp.where(
            lane == 127, low, jnp.where(lane == CY, high, planes[q, 0 : CX + 2, :])
        )
    write_swap(parity[2], planes[0], planes[3], za, zb)


def face_shapes(width):
    shapes = [(width, CY, CZ)] * 2 + [(max(width, 2), CX, CZ)] * 2
    shapes += [(8, ROWS)] * 2 if width == 3 else [(4, CX, 128)]
    return [jax.ShapeDtypeStruct(shape, F32) for shape in shapes]


def row_faces(parity, xa, xb, ylo, yhi):
    return pl.pallas_call(
        rows_kernel,
        out_shape=[jax.ShapeDtypeStruct((CX + 2, CZ), F32)] * 2
        + [jax.ShapeDtypeStruct((4, CX + 2, CZ), F32)],
        in_specs=parity_specs(4),
        out_specs=vmem_specs(3),
        compiler_params=pltpu.CompilerParams(vmem_limit_bytes=VMEM_LIMIT),
        name="row_faces",
    )(parity, xa, xb, ylo, yhi)


def plane_faces(parity, xa, xb, ya, yb, own):
    return pl.pallas_call(
        planes_kernel,
        out_shape=[jax.ShapeDtypeStruct(shape, F32) for shape in ((4, 40, 128), (40, 128), (40, 128))],
        in_specs=parity_specs(5),
        out_specs=vmem_specs(3),
        compiler_params=pltpu.CompilerParams(vmem_limit_bytes=VMEM_LIMIT),
        name="plane_faces",
    )(parity, xa, xb, ya, yb, own)


BLOCK = jax.ShapeDtypeStruct((CX, CY, CZ), F32)
FACE_SCRATCH = [pltpu.VMEM((2, 3, CX, CZ), F32), pltpu.VMEM((2, 8, ROWS), F32)]


def vmem_specs(count):
    return [pl.BlockSpec(memory_space=pltpu.VMEM)] * count


def parity_specs(count):
    return [pl.BlockSpec(memory_space=pltpu.SMEM)] + vmem_specs(count)


def pack(parity, phi):
    return pl.pallas_call(
        pack_kernel,
        out_shape=[BLOCK] * 3 + face_shapes(3),
        in_specs=parity_specs(1),
        out_specs=vmem_specs(9),
        scratch_shapes=[pltpu.VMEM((3, CZ, 128), F32)] + FACE_SCRATCH,
        compiler_params=pltpu.CompilerParams(vmem_limit_bytes=VMEM_LIMIT),
        name="pack",
    )(parity, phi)


def unpack(mixed):
    return pl.pallas_call(
        unpack_kernel,
        out_shape=BLOCK,
        in_specs=vmem_specs(1),
        out_specs=vmem_specs(1)[0],
        scratch_shapes=[pltpu.VMEM((3, CZ, 128), F32)],
        compiler_params=pltpu.CompilerParams(vmem_limit_bytes=VMEM_LIMIT),
        name="unpack",
    )(mixed)


def x_sums(parity, sigma, v, xa, xb):
    return pl.pallas_call(
        x_kernel,
        out_shape=jax.ShapeDtypeStruct((2, CX, CY, 128), F32),
        in_specs=parity_specs(4),
        out_specs=vmem_specs(1)[0],
        scratch_shapes=[pltpu.VMEM((2, 3, CY, CZ), F32)],
        compiler_params=pltpu.CompilerParams(vmem_limit_bytes=VMEM_LIMIT),
        cost_estimate=pl.CostEstimate(flops=20000000, bytes_accessed=6000000, transcendentals=400000),
        name="x_sums",
    )(parity, sigma, v, xa, xb)


def step(parity, sigma_in, pace, za0, zb0, v, za_own, zb_own, halos, last):
    xa, xb, *others = halos
    summed = x_sums(parity, sigma_in, v, xa, xb)
    return pl.pallas_call(
        functools.partial(step_kernel, last),
        out_shape=[BLOCK] + face_shapes(1 if last else 3),
        in_specs=parity_specs(12),
        out_specs=vmem_specs(6 if last else 7),
        scratch_shapes=[
            pltpu.VMEM((2, CX, 64, 128), F32),
            pltpu.VMEM((2, 4, 64, 128), F32),
            pltpu.VMEM((2, 2, 64, 128), F32),
            pltpu.VMEM((24, ROWS), F32),
            pltpu.VMEM((4, 24, ROWS), F32),
            pltpu.VMEM((2, 24, ROWS), F32),
            pltpu.VMEM((2, 128, ROWS), F32),
            pltpu.VMEM((2, ROWS, 128), F32),
        ]
        + FACE_SCRATCH
        + [
            pltpu.VMEM((4, CY, 128), F32),
            pltpu.VMEM((12, CY, 128), F32),
            pltpu.VMEM((5, CY, 128), F32),
            pltpu.VMEM((2, CY, 128), F32),
        ],
        compiler_params=pltpu.CompilerParams(vmem_limit_bytes=VMEM_LIMIT),
        name="step",
    )(parity, sigma_in, pace, za0, zb0, v, za_own, zb_own, summed, *others)


HALF_COS = [
    0.9999999991256178, -0.23370050635094053, 0.019968606689123116,
    -0.0008935362743290266, 2.3601076640059624e-05,
]
BAND_SQUARE = 1.5 * 1.5


def half_cosine(value):
    square = jnp.minimum(value * value, BAND_SQUARE)
    shape = F32(HALF_COS[4] / BAND_SQUARE**5)
    for k in (3, 2, 1, 0):
        shape = shape * square + F32(HALF_COS[k] / BAND_SQUARE ** (k + 1))
    return (BAND_SQUARE - square) * shape


def five_terms(centre, keep, dx, sx, dy, sy, dz, sz, dxy, dxz, dyz):
    twice = centre + centre
    xx, yy, zz = dx * dx, dy * dy, dz * dz
    squares = jnp.maximum(xx + yy + zz, 1.0)
    root = lax.rsqrt(squares)
    bend = (sx - twice) * (yy + zz) + (sy - twice) * (xx + zz) + (sz - twice) * (xx + yy)
    bend = bend - 0.5 * (dx * (dy * dxy + dz * dxz) + dy * dz * dyz)
    cosine = half_cosine(centre)
    spread = cosine * cosine
    if keep is not None:
        spread = jnp.where(keep, spread, 0.0)
    return (
        spread * (squares * root),
        spread * bend * (root * root),
        spread * dx,
        spread * dy,
        spread * dz,
    )


def brick_tables(ids, targets, live_count):
    entry = lax.broadcasted_iota(jnp.int32, (1, SLOTS), 1)
    live = entry < live_count
    row = lax.broadcasted_iota(jnp.int32, (SLOTS, SLOTS), 0)
    column = lax.broadcasted_iota(jnp.int32, (SLOTS, SLOTS), 1)
    owner = targets.astype(F32)
    down = jnp.sum(jnp.where(row == column, owner, 0.0), axis=1, keepdims=True)
    earlier = (row < column) & (row < live_count) & (down == owner)
    rank = jnp.sum(earlier.astype(F32), axis=0, keepdims=True)
    owner_at = jnp.where(live, owner, F32(SLOTS))
    peers = lax.broadcasted_iota(jnp.int32, (PEERS, SLOTS), 0).astype(F32)
    to_slot = [((owner_at == peers) & (rank == F32(c))).astype(F32) for c in range(2)]

    def finder(count, brick_of):
        at = lax.broadcasted_iota(jnp.int32, (count, SLOTS), 0)
        return (ids == brick_of(at)).astype(F32)

    return to_slot, finder


def exact_dot(left, right, dims=(((1,), (0,)), ((), ()))):
    return lax.dot_general(
        left, right, dims, precision=lax.Precision.HIGHEST, preferred_element_type=F32
    )


def neighbours(pair):
    return ((lane_down(pair[1]), pair[1]), (pair[0], lane_up(pair[0])))


def pair_terms(grid, keeps):
    two = range(2)

    def diff(first, second):
        return [grid[first][half] - grid[second][half] for half in two]

    def summed(first, second):
        return [grid[first][half] + grid[second][half] for half in two]

    dx, sx = diff((1, 0), (-1, 0)), summed((1, 0), (-1, 0))
    dy, sy = diff((0, 1), (0, -1)), summed((0, 1), (0, -1))
    over, under = diff((1, 1), (-1, 1)), diff((1, -1), (-1, -1))
    around, dx_around, dy_around = neighbours(grid[0, 0]), neighbours(dx), neighbours(dy)
    results = []
    for half in two:
        results.append(
            five_terms(
                grid[0, 0][half], keeps[half], dx[half], sx[half], dy[half], sy[half],
                around[half][1] - around[half][0], around[half][1] + around[half][0],
                over[half] - under[half],
                dx_around[half][1] - dx_around[half][0],
                dy_around[half][1] - dy_around[half][0],
            )
        )
    return [results[0][n] + results[1][n] for n in range(5)]


STAR = [(0, 0), (1, 0), (-1, 0), (0, 1), (0, -1), (1, 1), (1, -1), (-1, 1), (-1, -1)]


def tile_terms(vs, plane, k, keeps):
    grid = {
        (sx, sy): [vs[half, plane + sx, pl.ds(8 + 8 * k + sy, 8), :] for half in range(2)]
        for sx, sy in STAR
    }
    return pair_terms(grid, keeps)


def z_keeps(rows):
    lane = lax.broadcasted_iota(jnp.int32, (rows, 128), 1)
    return [lane != 0, lane != 127]


def inner_kernel(v, stack, vs):
    def fill(x, carry):
        for half in range(2):
            vs[half, x, 8 : 8 + CY, :] = v[x, :, pl.ds(128 * half, 128)]
            vs[half, x, 7:8, :] = jnp.zeros((1, 128), F32)
            vs[half, x, 8 + CY : 9 + CY, :] = jnp.zeros((1, 128), F32)
        return carry

    lax.fori_loop(0, CX, fill, 0)
    keeps = z_keeps(8)
    row = lax.broadcasted_iota(jnp.int32, (8, 128), 0)
    first = [keep & (row != 0) for keep in keeps]
    last = [keep & (row != 7) for keep in keeps]
    zeros = jnp.zeros((8, 128), F32)
    for bx in range(2):

        def body(step_at, sums):
            sums = list(sums)
            for sub in range(3):
                x = BRICK * bx + (1 - bx) + 3 * step_at + sub
                for k in range(YT):
                    parts = tile_terms(vs, x, k, first if k == 0 else last if k == 5 else keeps)
                    for n in range(5):
                        slot = 5 * (k // 2) + n
                        sums[slot] = sums[slot] + parts[n]
            return tuple(sums)

        sums = lax.fori_loop(0, 5, body, (zeros,) * 15)
        for by in range(3):
            row_at = 8 * (3 * bx + by)
            for n in range(5):
                total = jnp.sum(sums[5 * by + n], axis=0, keepdims=True)
                stack[row_at + n : row_at + n + 1, :] = total
            stack[row_at + 5 : row_at + 8, :] = jnp.zeros((3, 128), F32)


def edge_kernel(
    parity, count, inner, v, xa, xb, ya, yb, za, zb, y_rows, planes, ids, targets, record,
    vs, stack,
):
    x_sides = low_high(parity[0], xa[0], xb[0])
    y_sides = low_high(parity[1], ya[...], yb[...])
    under, over = low_high(parity[2], za[...], zb[...])
    stack[...] = inner[...]

    def add(b, n, row):
        stack[8 * b + n : 8 * b + n + 1, :] += row

    keeps = z_keeps(8)
    for side in range(2):
        for half in range(2):
            lanes = slice(128 * half, 128 * half + 128)
            for at in range(3):
                x = at - 1 if side == 0 else CX - 2 + at
                if 0 <= x < CX:
                    vs[half, at, 8 : 8 + CY, :] = v[x, :, lanes]
                else:
                    vs[half, at, 8 : 8 + CY, :] = x_sides[side][:, lanes]
                vs[half, at, 7:8, :] = y_sides[0][x + 1 : x + 2, lanes]
                vs[half, at, 8 + CY : 9 + CY, :] = y_sides[1][x + 1 : x + 2, lanes]
        for by in range(3):
            parts = [tile_terms(vs, 1, 2 * by + sub, keeps) for sub in range(2)]
            for n in range(5):
                add(3 * side + by, n, jnp.sum(parts[0][n] + parts[1][n], axis=0, keepdims=True))

    keeps = z_keeps(16)
    row = lax.broadcasted_iota(jnp.int32, (16, 128), 0)
    for side in range(2):
        if side == 0:
            rows = (y_sides[0], y_rows[0], y_rows[1])
        else:
            rows = (y_rows[2], y_rows[3], y_sides[1])
        for bx in range(2):
            grid = {
                (sx, sy): [
                    rows[1 + sy][1 + 16 * bx + sx : 17 + 16 * bx + sx, 128 * half : 128 * half + 128]
                    for half in range(2)
                ]
                for sx, sy in STAR
            }
            inside = row != (0 if bx == 0 else 15)
            parts = pair_terms(grid, [keep & inside for keep in keeps])
            for n in range(5):
                add(3 * bx + 2 * side, n, jnp.sum(parts[n], axis=0, keepdims=True))

    to_slot, finder = brick_tables(ids[...], targets[...], count[0])
    found = jnp.zeros((8, SLOTS), F32)
    for b in range(6):
        found = found + exact_dot(
            stack[8 * b : 8 * b + 8, :], finder(128, lambda at: 16 * b + at // 8)
        )
    for side in range(2):
        window = (under, planes[0], planes[1]) if side == 0 else (planes[2], planes[3], over)

        def cut(plane, step_x, step_y):
            part = window[plane][1 + step_x : 33 + step_x]
            return pltpu.roll(part, (-step_y) % 128, 1) if step_y else part

        high, low = cut(1, 1, 0), cut(1, -1, 0)
        right, left = cut(1, 0, 1), cut(1, 0, -1)
        above, below = cut(2, 0, 0), cut(0, 0, 0)
        terms = five_terms(
            cut(1, 0, 0), None,
            high - low, high + low, right - left, right + left, above - below, above + below,
            (cut(1, 1, 1) - cut(1, -1, 1)) - (cut(1, 1, -1) - cut(1, -1, -1)),
            (cut(2, 1, 0) - cut(2, -1, 0)) - (cut(0, 1, 0) - cut(0, -1, 0)),
            (cut(2, 0, 1) - cut(2, 0, -1)) - (cut(0, 0, 1) - cut(0, 0, -1)),
        )
        for bx in range(2):
            rows = [jnp.sum(term[16 * bx : 16 * bx + 16], axis=0, keepdims=True) for term in terms]
            rows = jnp.concatenate(rows + [jnp.zeros((3, 128), F32)], axis=0)
            found = found + exact_dot(
                rows,
                finder(
                    128,
                    lambda at: jnp.where(at < CY, 48 * bx + 16 * (at // 16) + 15 * side, -1),
                ),
            )
    scale = 2.0 / 3.0 / (BRICK * BRICK)
    row = lax.broadcasted_iota(jnp.int32, (8, SLOTS), 0)
    found = found * jnp.where(row == 1, F32(scale), F32(0.5 * scale))
    for c in range(2):
        record[:, 8 * c : 8 * c + 8] = exact_dot(to_slot[c], found, (((1,), (1,)), ((), ())))


def arrange_kernel(received, out):
    source = lax.broadcasted_iota(jnp.int32, (PEERS, SLOTS), 0)
    slot = lax.broadcasted_iota(jnp.int32, (PEERS, SLOTS), 1)
    total = jnp.zeros((8, SLOTS), F32)
    for c in range(2):
        total = total + exact_dot(
            received[:, 8 * c : 8 * c + 8], (slot == 2 * source + c).astype(F32),
            (((0,), (0,)), ((), ())),
        )
    for n in range(5):
        out[0, 0, n] = total[n : n + 1]


def arrange(received):
    return pl.pallas_call(
        arrange_kernel,
        out_shape=jax.ShapeDtypeStruct((1, 1, 5, 1, SLOTS), F32),
        in_specs=vmem_specs(1),
        out_specs=vmem_specs(1)[0],
        compiler_params=pltpu.CompilerParams(vmem_limit_bytes=VMEM_LIMIT),
        name="arrange",
    )(received)


def inner_bricks(v):
    return pl.pallas_call(
        inner_kernel,
        out_shape=jax.ShapeDtypeStruct((48, 128), F32),
        in_specs=vmem_specs(1),
        out_specs=vmem_specs(1)[0],
        scratch_shapes=[pltpu.VMEM((2, CX, 64, 128), F32)],
        compiler_params=pltpu.CompilerParams(vmem_limit_bytes=VMEM_LIMIT),
        cost_estimate=pl.CostEstimate(flops=20000000, bytes_accessed=6000000, transcendentals=400000),
        name="inner_bricks",
    )(v)


def edge_bricks(parity, count, inner, v, halos, y_rows, planes, ids, targets):
    return pl.pallas_call(
        edge_kernel,
        out_shape=jax.ShapeDtypeStruct((PEERS, 16), F32),
        in_specs=[pl.BlockSpec(memory_space=pltpu.SMEM)] * 2 + vmem_specs(12),
        out_specs=vmem_specs(1)[0],
        scratch_shapes=[
            pltpu.VMEM((2, 3, 64, 128), F32),
            pltpu.VMEM((48, 128), F32),
        ],
        compiler_params=pltpu.CompilerParams(vmem_limit_bytes=VMEM_LIMIT),
        name="edge_bricks",
    )(parity, count, inner, v, *halos, y_rows, planes, ids, targets)


def swap(value, axis, phase):
    count = lax.axis_size(axis)
    if phase == 0:
        pairs = [(i, i ^ 1) for i in range(count)]
    else:
        pairs = [(i, (i - 1 if i % 2 == 0 else i + 1) % count) for i in range(count)]
    return lax.ppermute(value, axis, pairs)


def exchange(faces):
    xa, xb, ya, yb, za, zb = faces
    zb = swap(zb, "gz", 1)
    yb = swap(yb, "gy", 1)
    ya = swap(ya, "gy", 0)
    za = swap(za, "gz", 0)
    xb = swap(xb, "gx", 1)
    xa = swap(xa, "gx", 0)
    return xa, xb, ya, yb, za, zb


def per_device(phi_start, band_ids, band_count, owners):
    parity = jnp.stack([lax.axis_index(name) % 2 for name in ("gx", "gy", "gz")])
    parity = parity.astype(jnp.int32)
    v, sigma, pace, *faces = pack(parity, phi_start)
    za0, zb0 = faces[4:]
    for number in range(STEPS):
        v, *faces = step(
            parity, sigma, pace, za0, zb0, v, faces[4], faces[5], exchange(faces),
            number == STEPS - 1,
        )
    level_set = unpack(v)

    xa, xb, ylo, yhi, own = faces
    xb = swap(xb, "gx", 1)
    xa = swap(xa, "gx", 0)
    ya, yb, y_rows = row_faces(parity, xa, xb, ylo, yhi)
    inner = inner_bricks(v)
    yb = swap(yb, "gy", 1)
    ya = swap(ya, "gy", 0)
    ya, yb, inner = lax.optimization_barrier((ya, yb, inner))
    planes, za, zb = plane_faces(parity, xa, xb, ya, yb, own)
    zb = swap(zb, "gz", 1)
    za = swap(za, "gz", 0)
    record = edge_bricks(
        parity, band_count.reshape(1), inner, v, (xa, xb, ya, yb, za, zb), y_rows, planes,
        band_ids.reshape(1, SLOTS), owners.reshape(1, SLOTS),
    )
    received = lax.all_to_all(record, ("gx", "gy"), split_axis=0, concat_axis=0, tiled=True)
    return level_set, jnp.swapaxes(arrange(received), 2, 3)


def solution(mesh):
    placed = (
        P("gx", "gy", "gz"),
        P("gx", "gy", "gz", None),
        P("gx", "gy", "gz"),
        P("gx", "gy", "gz", None),
    )
    return jax.shard_map(
        per_device,
        mesh=mesh,
        in_specs=placed,
        out_specs=(P("gx", "gy", "gz"), P("gx", "gy", "gz", None, None)),
        check_vma=False,
    )
```

```python
import functools

import jax
import jax.numpy as jnp
from jax import lax
from jax.experimental import pallas as pl
from jax.experimental.pallas import tpu as pltpu
from jax.sharding import PartitionSpec as P

STEPS = 3
BRICK = 16
SLOTS = 64
PAIR = 8
PEERS = 32
CX, CY, CZ = 32, 48, 256
ROWS = CX * CY
YT = CY // 8
WENO_EPS = 1e-06
F32 = jnp.float32
VMEM_LIMIT = 16 * 1024 * 1024


def rcp(value):
    return pltpu.reciprocal(value, approx=True)


def smooth_weights(e_low, e_high, third):
    twice = third + third
    middle = e_low * e_high + (third * third * (4.0 / 3.0) + WENO_EPS)
    q_a = rcp(middle - e_low * twice)
    q_b = rcp(middle)
    q_c = rcp(middle + e_high * twice)
    return q_a * q_a, 6.0 * (q_b * q_b), q_c * q_c


def biased_parts(wa_next, wb, wc_prev, t_prev, t_here, t_next):
    x = wc_prev * (t_here - t_prev)
    y = wa_next * (t_next - t_here)
    both = x + y
    both = both + both
    total = (wa_next + wb) + wc_prev
    left = t_here + (both + y) * rcp(total + (wa_next + wa_next))
    right = t_here - (both + x) * rcp(total + (wc_prev + wc_prev))
    return left, right


def upwind_square(centre, left, right, sigma):
    return upwind_pair(centre - left, right - centre, sigma)


def upwind_pair(left, right_back, sigma):
    best = jnp.maximum(sigma * left, sigma * right_back)
    best = jnp.maximum(best, 0.0)
    return best * best


def sigma_of(value):
    return jnp.where(value > 0.0, F32(1.0), F32(-1.0))


def from_values(v_m, v_0, v_1, v_2):
    d_m, d_0, d_1 = v_0 - v_m, v_1 - v_0, v_2 - v_1
    e_0, e_1 = d_0 - d_m, d_1 - d_0
    return e_0, e_1, e_1 - e_0


def lane_down(part):
    return pltpu.roll(part, 1, 1)


def lane_up(part):
    return pltpu.roll(part, 127, 1)


def z_stage_weights(even, odd, even_down, odd_down, even_up, odd_up):
    v = {-2: even_down, -1: odd_down, 0: even, 1: odd, 2: even_up, 3: odd_up}
    d = {k: v[k + 1] - v[k] for k in range(-2, 3)}
    e = {k: d[k] - d[k - 1] for k in range(-1, 3)}
    t = {k: e[k + 1] - e[k] for k in range(-1, 2)}
    w_0 = smooth_weights(e[0], e[1], t[0])
    w_1 = smooth_weights(e[1], e[2], t[1])
    return (
        w_1[0], w_0[1], lane_down(w_1[2]), t[-1], t[0], t[1],
        lane_up(w_0[0]), w_1[1], w_0[2], lane_up(t[0]),
        3.0 * (d[-1] + d[0]), 3.0 * (d[0] + d[1]),
    )


def z_stage_parts(wa_0, wb_0, wc_0, t_m, t_0, t_1, wa_1, wb_1, wc_1, t_2, centre_0, centre_1):
    left_0, right_0 = biased_parts(wa_0, wb_0, wc_0, t_m, t_0, t_1)
    left_1, right_1 = biased_parts(wa_1, wb_1, wc_1, t_0, t_1, t_2)
    return centre_0, lane_down(left_1), right_0 - centre_0, centre_1 - left_0, right_1 - centre_1


def edge_column(window, u_ref, p_ref, u_row, p_row, sigma):
    def rows(start):
        return window[pl.ds(start, 8), :]

    e_0, e_1, t = from_values(rows(u_row - 1), rows(u_row), rows(u_row + 1), rows(u_row + 2))
    w_a, w_b, w_c = smooth_weights(e_0, e_1, t)
    for slot, part in enumerate((w_a, w_b, w_c, t)):
        u_ref[slot, pl.ds(u_row, 8), :] = part
    left, right = biased_parts(
        u_ref[0, pl.ds(p_row + 1, 8), :],
        u_ref[1, pl.ds(p_row, 8), :],
        u_ref[2, pl.ds(p_row - 1, 8), :],
        u_ref[3, pl.ds(p_row - 1, 8), :],
        u_ref[3, pl.ds(p_row, 8), :],
        u_ref[3, pl.ds(p_row + 1, 8), :],
    )
    p_ref[0, pl.ds(p_row, 8), :] = left
    p_ref[1, pl.ds(p_row, 8), :] = right
    centre = 3.0 * (rows(9) - rows(7))
    return upwind_square(
        centre, p_ref[0, pl.ds(7, 8), :], p_ref[1, pl.ds(8, 8), :], sigma
    )


def z_faces(source, zlo, zhi):
    for chunk in range(CX // 8):
        columns = slice(8 * CY * chunk, 8 * CY * (chunk + 1))
        for parity in range(2):
            part = source[8 * chunk : 8 * chunk + 8, :, 128 * parity : 128 * parity + 128]
            part = part.reshape(8 * CY, 128).T
            for k in range(4):
                zlo[2 * k + parity : 2 * k + parity + 1, columns] = part[k : k + 1]
                zhi[2 * k + parity : 2 * k + parity + 1, columns] = part[124 + k : 125 + k]


def y_faces(source, ylo, yhi, width):
    for x in range(CX):
        for k in range(width):
            ylo[k, x : x + 1, :] = source[x, k : k + 1, :]
            yhi[k, x : x + 1, :] = source[x, CY - width + k : CY - width + 1 + k, :]


def write_swap(parity, low, high, out_a, out_b):
    odd = parity == 1
    out_a[...] = jnp.where(odd, low, high)
    out_b[...] = jnp.where(odd, high, low)


def write_faces(parity, source, xa, xb, ya, yb, za, zb, yf, zf):
    y_faces(source, yf.at[0], yf.at[1], 3)
    write_swap(parity[1], yf[0], yf[1], ya, yb)
    write_swap(parity[0], source[0:3], source[CX - 3 : CX], xa, xb)
    z_faces(source, zf.at[0], zf.at[1])
    write_swap(parity[2], zf[0], zf[1], za, zb)


def low_high(parity, part_a, part_b):
    odd = parity == 1
    return jnp.where(odd, part_a, part_b), jnp.where(odd, part_b, part_a)


def pack_kernel(parity, phi, mixed, xa, xb, ya, yb, za, zb, turned, yf, zf):
    for chunk in range(CX // 8):
        planes = slice(8 * chunk, 8 * chunk + 8)
        for half in range(2):
            part = phi[planes, :, 128 * half : 128 * half + 128]
            part = part.reshape(8 * CY, 128).T
            for c in range(3):
                turned[c, 128 * half : 128 * half + 128, :] = part[:, 128 * c : 128 * c + 128]
        for which in range(2):
            part = [turned[c, pl.ds(which, 128, stride=2), :].T for c in range(3)]
            part = jnp.concatenate(part, axis=0)
            mixed[planes, :, 128 * which : 128 * which + 128] = part.reshape(8, CY, 128)
    write_faces(parity, mixed, xa, xb, ya, yb, za, zb, yf, zf)


def signs_kernel(start, sigma, pace):
    def signs(x, carry):
        value = start[x]
        sigma[x] = sigma_of(value)
        pace[x] = (0.05 * value) * lax.rsqrt(value * value + 1.0)
        return carry

    lax.fori_loop(0, CX, signs, 0)


def unpack_kernel(mixed, out, turned):
    for chunk in range(CX // 8):
        planes = slice(8 * chunk, 8 * chunk + 8)
        for parity in range(2):
            part = mixed[planes, :, 128 * parity : 128 * parity + 128]
            part = part.reshape(8 * CY, 128).T
            for c in range(3):
                turned[c, pl.ds(parity, 128, stride=2), :] = part[:, 128 * c : 128 * c + 128]
        for half in range(2):
            part = [turned[c, 128 * half : 128 * half + 128, :].T for c in range(3)]
            part = jnp.concatenate(part, axis=0)
            out[planes, :, 128 * half : 128 * half + 128] = part.reshape(8, CY, 128)


def edge_lanes():
    lane = lax.broadcasted_iota(jnp.int32, (8, 128), 1)
    return [(lane < 2) | (lane == 127), (lane < 1) | (lane > 125)]


def run_stages(stages, count):
    depth = len(stages) - 1

    def run(at, low, high):
        for delay in range(high, low - 1, -1):
            stages[delay](at - delay)

    def body(at, carry):
        run(at, 0, depth)
        return carry

    for at in range(depth):
        run(at, 0, at)
    lax.fori_loop(depth, count, body, 0)
    for at in range(depth):
        run(count + at, at + 1, depth)


def xz_kernel(parity, sigma_in, v, xa_in, xb_in, summed, xh, rolled, zs, zp):
    xh[0], xh[1] = low_high(parity[0], xa_in[...], xb_in[...])

    def x_pass(yt, carry):
        row = pl.multiple_of(8 * yt, 8)
        for zt in range(2):
            lanes = pl.ds(128 * zt, 128)

            def cell(x):
                if x < 0:
                    return xh[0, 3 + x, pl.ds(row, 8), lanes]
                if x >= CX:
                    return xh[1, x - CX, pl.ds(row, 8), lanes]
                return v[x, pl.ds(row, 8), lanes]

            d, e, t, weights, lefts, rights = {}, {}, {}, {}, {}, {}
            d[-3] = cell(-2) - cell(-3)
            d[-2] = cell(-1) - cell(-2)
            e[-2] = d[-2] - d[-3]
            for j in range(-2, CX + 1):
                d[j + 1] = cell(j + 2) - cell(j + 1)
                e[j + 1] = d[j + 1] - d[j]
                t[j] = e[j + 1] - e[j]
                weights[j] = smooth_weights(e[j], e[j + 1], t[j])
                p = j - 1
                if p >= -1:
                    lefts[p], rights[p] = biased_parts(
                        weights[p + 1][0], weights[p][1], weights[p - 1][2], t[p - 1], t[p], t[p + 1]
                    )
                if p >= 0:
                    sigma = sigma_in[p, pl.ds(row, 8), lanes]
                    centre = 3.0 * (d[p - 1] + d[p])
                    summed[zt, p, pl.ds(row, 8), :] = upwind_square(
                        centre, lefts[p - 1], rights[p], sigma
                    )
        return carry

    lax.fori_loop(0, YT, x_pass, 0)
    edge = edge_lanes()

    def tile(x, half, k):
        return v[x, 8 * k : 8 * k + 8, 128 * half : 128 * half + 128]

    def spots(item):
        for sub in range(PAIR):
            for k in range(YT):
                start = CY * sub + 8 * k
                yield PAIR * item + sub, k, slice(start, start + 8)

    def turn(item):
        for x, k, at in spots(item):
            for half in range(2):
                part = tile(x, half, k)
                rolled[half, at, :] = lane_down(part)
                rolled[2 + half, at, :] = lane_up(part)

    def weigh(item):
        for x, k, at in spots(item):
            parts = z_stage_weights(
                tile(x, 0, k), tile(x, 1, k), *[rolled[slot, at, :] for slot in range(4)]
            )
            for slot, part in enumerate(parts):
                zs[slot, at, :] = part

    def blend(item):
        for x, k, at in spots(item):
            parts = z_stage_parts(*[zs[slot, at, :] for slot in range(12)])
            for slot, part in enumerate(parts):
                zp[slot, at, :] = part

    def add(item):
        for x, k, at in spots(item):
            rows = slice(8 * k, 8 * k + 8)
            for half in range(2):
                sigma = sigma_in[x, rows, 128 * half : 128 * half + 128]
                if half == 0:
                    along = upwind_pair(zp[0, at, :] - zp[1, at, :], zp[2, at, :], sigma)
                else:
                    along = upwind_pair(zp[3, at, :], zp[4, at, :], sigma)
                summed[half, x, rows, :] += jnp.where(edge[half], 0.0, along)

    run_stages((turn, weigh, blend, add), CX // PAIR)


def step_kernel(
    last,
    parity, sigma_in, pace, za0, zb0, v, za_own, zb_own, summed, ya_in, yb_in, za_in, zb_in,
    *refs,
):
    faces = 6 if last else 7
    step_body(last, parity, sigma_in, pace, za0, zb0, v, za_own, zb_own, summed, ya_in,
              yb_in, za_in, zb_in, refs[:faces], *refs[faces:])


def step_body(
    last,
    parity, sigma_in, pace, za0, zb0, v, za_own, zb_own, summed, ya_in, yb_in, za_in, zb_in,
    outs,
    vs, u_ref, p_ref, window, zu_ref, zp_ref, edges, fixes, yf, zf,
):
    out = outs[0]

    def fill(x, carry):
        for zt in range(2):
            vs[zt, x, 8 : 8 + CY, :] = v[x, :, pl.ds(128 * zt, 128)]
        return carry

    lax.fori_loop(0, CX, fill, 0)
    yf[0], yf[1] = low_high(parity[1], ya_in[...], yb_in[...])
    for x in range(CX):
        for zt in range(2):
            lanes = slice(128 * zt, 128 * zt + 128)
            for k in range(3):
                vs[zt, x, 5 + k : 6 + k, :] = yf[0, k, x : x + 1, lanes]
                vs[zt, x, 8 + CY + k : 9 + CY + k, :] = yf[1, k, x : x + 1, lanes]

    z_low, z_high = low_high(parity[2], za_in[...], zb_in[...])
    zlo0, zhi0 = low_high(parity[2], za0[...], zb0[...])
    zlo_own, zhi_own = low_high(parity[2], za_own[...], zb_own[...])
    window[5:8, :] = z_low[5:8]
    window[8:16, :] = zlo_own
    fixed = edge_column(window, zu_ref, zp_ref, 6, 7, sigma_of(zlo0))
    for half, lane_at, cell_at in ((0, 0, 0), (0, 1, 2), (1, 0, 1)):
        edges[half, lane_at : lane_at + 1, :] = fixed[cell_at : cell_at + 1]
    window[8:16, :] = zhi_own
    window[16:19, :] = z_high[0:3]
    fixed = edge_column(window, zu_ref, zp_ref, 9, 8, sigma_of(zhi0))
    for half, lane_at, cell_at in ((0, 127, 6), (1, 126, 5), (1, 127, 7)):
        edges[half, lane_at : lane_at + 1, :] = fixed[cell_at : cell_at + 1]
    for half in range(2):
        fixes[half] = edges[half].T

    edge = edge_lanes()

    def y_weights(x, zt, k):
        start = 6 + 8 * k
        e_0, e_1, t = from_values(
            *[vs[zt, x, pl.ds(start + shift, 8), :] for shift in (-1, 0, 1, 2)]
        )
        w_a, w_b, w_c = smooth_weights(e_0, e_1, t)
        for slot, part in enumerate((w_a, w_b, w_c, t)):
            u_ref[zt, slot, pl.ds(8 * k, 8), :] = part

    def y_parts(zt, k):
        def read(slot, row):
            return u_ref[zt, slot, pl.ds(row, 8), :]

        row = 8 * k + 1
        left, right = biased_parts(
            read(0, row + 1), read(1, row), read(2, row - 1),
            read(3, row - 1), read(3, row), read(3, row + 1),
        )
        p_ref[zt, 0, pl.ds(8 * k, 8), :] = left
        p_ref[zt, 1, pl.ds(8 * k, 8), :] = right

    def weigh(x):
        for zt in range(2):
            for k in range(YT + 1):
                y_weights(x, zt, k)

    def blend(x):
        for zt in range(2):
            for k in range(YT + 1):
                y_parts(zt, k)

    def update(x):
        flat = pl.multiple_of(x * CY, 8)
        for zt in range(2):
            for k in range(YT):
                rows = slice(8 * k, 8 * k + 8)
                lanes = slice(128 * zt, 128 * zt + 128)
                centre = 3.0 * (
                    vs[zt, x, 9 + 8 * k : 17 + 8 * k, :] - vs[zt, x, 7 + 8 * k : 15 + 8 * k, :]
                )
                along = upwind_square(
                    centre, p_ref[zt, 0, rows, :], p_ref[zt, 1, 8 * k + 1 : 8 * k + 9, :],
                    sigma_in[x, rows, lanes],
                )
                fix = jnp.where(edge[zt], fixes[zt, pl.ds(flat + 8 * k, 8), :], 0.0)
                total = summed[zt, x, rows, :] + along + fix
                root = total * lax.rsqrt(jnp.maximum(total, 1e-30))
                out[x, rows, lanes] = v[x, rows, lanes] - pace[x, rows, lanes] * (root - 6.0)

    run_stages((weigh, blend, update), CX)
    if last:
        xa, xb, ylo, yhi, planes = outs[1:]
        write_swap(parity[0], out[0:1], out[CX - 1 : CX], xa, xb)
        y_faces(out, ylo, yhi, 2)
        planes[...] = jnp.zeros((4, CX, 128), F32)
        for chunk in range(CX // 8):
            for half in range(2):
                part = out[8 * chunk : 8 * chunk + 8, :, 128 * half : 128 * half + 128]
                part = part.reshape(8 * CY, 128).T
                for x in range(8):
                    lanes = slice(CY * x, CY * x + CY)
                    at = slice(8 * chunk + x, 8 * chunk + x + 1)
                    planes[half, at, 0:CY] = part[0:1, lanes]
                    planes[2 + half, at, 0:CY] = part[127:128, lanes]
    else:
        write_faces(parity, out, *outs[1:], yf, zf)


def rows_kernel(parity, xa, xb, ylo, yhi, ya, yb, y_rows):
    x_low, x_high = low_high(parity[0], xa[0], xb[0])
    for at, (source, layer, row) in enumerate(
        ((ylo, 0, 0), (ylo, 1, 1), (yhi, 0, CY - 2), (yhi, 1, CY - 1))
    ):
        y_rows[at, 0:1, :] = x_low[row : row + 1]
        y_rows[at, 1 : CX + 1, :] = source[layer]
        y_rows[at, CX + 1 : CX + 2, :] = x_high[row : row + 1]
    write_swap(parity[1], y_rows[0], y_rows[3], ya, yb)


def planes_kernel(parity, xa, xb, ya, yb, own, planes, za, zb):
    x_sides = low_high(parity[0], xa[0], xb[0])
    y_low, y_high = low_high(parity[1], ya[...], yb[...])
    planes[...] = jnp.zeros((4, 40, 128), F32)
    for q in range(4):
        planes[q, 1 : CX + 1, :] = own[q]
    for side in range(2):
        row = (CX + 1) * side
        for half in range(2):
            turned = x_sides[side][:, 128 * half : 128 * half + 128].T
            planes[half, row : row + 1, 0:CY] = turned[0:1]
            planes[2 + half, row : row + 1, 0:CY] = turned[127:128]
    lane = lax.broadcasted_iota(jnp.int32, (CX + 2, 128), 1)
    for q in range(4):
        lanes = slice(128 * (q % 2), 128 * (q % 2) + 128)
        start = 0 if q < 2 else 127
        low = y_low[:, lanes]
        if start != 127:
            low = pltpu.roll(low, 127 - start, 1)
        high = pltpu.roll(y_high[:, lanes], (CY - start) % 128, 1)
        planes[q, 0 : CX + 2, :] = jnp.where(
            lane == 127, low, jnp.where(lane == CY, high, planes[q, 0 : CX + 2, :])
        )
    write_swap(parity[2], planes[0], planes[3], za, zb)


def face_shapes(width):
    shapes = [(width, CY, CZ)] * 2 + [(max(width, 2), CX, CZ)] * 2
    shapes += [(8, ROWS)] * 2 if width == 3 else [(4, CX, 128)]
    return [jax.ShapeDtypeStruct(shape, F32) for shape in shapes]


def row_faces(parity, xa, xb, ylo, yhi):
    return pl.pallas_call(
        rows_kernel,
        out_shape=[jax.ShapeDtypeStruct((CX + 2, CZ), F32)] * 2
        + [jax.ShapeDtypeStruct((4, CX + 2, CZ), F32)],
        in_specs=parity_specs(4),
        out_specs=vmem_specs(3),
        compiler_params=pltpu.CompilerParams(vmem_limit_bytes=VMEM_LIMIT),
        name="row_faces",
    )(parity, xa, xb, ylo, yhi)


def plane_faces(parity, xa, xb, ya, yb, own):
    return pl.pallas_call(
        planes_kernel,
        out_shape=[jax.ShapeDtypeStruct(shape, F32) for shape in ((4, 40, 128), (40, 128), (40, 128))],
        in_specs=parity_specs(5),
        out_specs=vmem_specs(3),
        compiler_params=pltpu.CompilerParams(vmem_limit_bytes=VMEM_LIMIT),
        name="plane_faces",
    )(parity, xa, xb, ya, yb, own)


BLOCK = jax.ShapeDtypeStruct((CX, CY, CZ), F32)
FACE_SCRATCH = [pltpu.VMEM((2, 3, CX, CZ), F32), pltpu.VMEM((2, 8, ROWS), F32)]


def vmem_specs(count):
    return [pl.BlockSpec(memory_space=pltpu.VMEM)] * count


def parity_specs(count):
    return [pl.BlockSpec(memory_space=pltpu.SMEM)] + vmem_specs(count)


def pack(parity, phi):
    return pl.pallas_call(
        pack_kernel,
        out_shape=[BLOCK] + face_shapes(3),
        in_specs=parity_specs(1),
        out_specs=vmem_specs(7),
        scratch_shapes=[pltpu.VMEM((3, CZ, 128), F32)]
        + FACE_SCRATCH,
        compiler_params=pltpu.CompilerParams(vmem_limit_bytes=VMEM_LIMIT),
        name="pack",
    )(parity, phi)


def sign_fields(start):
    return pl.pallas_call(
        signs_kernel,
        out_shape=[BLOCK] * 2,
        in_specs=vmem_specs(1),
        out_specs=vmem_specs(2),
        compiler_params=pltpu.CompilerParams(vmem_limit_bytes=VMEM_LIMIT),
        cost_estimate=pl.CostEstimate(flops=2000000, bytes_accessed=4700000, transcendentals=400000),
        name="sign_fields",
    )(start)


def unpack(mixed):
    return pl.pallas_call(
        unpack_kernel,
        out_shape=BLOCK,
        in_specs=vmem_specs(1),
        out_specs=vmem_specs(1)[0],
        scratch_shapes=[pltpu.VMEM((3, CZ, 128), F32)],
        compiler_params=pltpu.CompilerParams(vmem_limit_bytes=VMEM_LIMIT),
        name="unpack",
    )(mixed)


def xz_sums(parity, sigma, v, xa, xb):
    return pl.pallas_call(
        xz_kernel,
        out_shape=jax.ShapeDtypeStruct((2, CX, CY, 128), F32),
        in_specs=parity_specs(4),
        out_specs=vmem_specs(1)[0],
        scratch_shapes=[
            pltpu.VMEM((2, 3, CY, CZ), F32),
            pltpu.VMEM((4, PAIR * CY, 128), F32),
            pltpu.VMEM((12, PAIR * CY, 128), F32),
            pltpu.VMEM((5, PAIR * CY, 128), F32),
        ],
        compiler_params=pltpu.CompilerParams(vmem_limit_bytes=VMEM_LIMIT),
        cost_estimate=pl.CostEstimate(flops=20000000, bytes_accessed=6000000, transcendentals=400000),
        name="xz_sums",
    )(parity, sigma, v, xa, xb)


def step(parity, sigma_in, pace, za0, zb0, v, za_own, zb_own, halos, last):
    xa, xb, *others = halos
    summed = xz_sums(parity, sigma_in, v, xa, xb)
    return pl.pallas_call(
        functools.partial(step_kernel, last),
        out_shape=[BLOCK] + face_shapes(1 if last else 3),
        in_specs=parity_specs(12),
        out_specs=vmem_specs(6 if last else 7),
        scratch_shapes=[
            pltpu.VMEM((2, CX, 64, 128), F32),
            pltpu.VMEM((2, 4, 64, 128), F32),
            pltpu.VMEM((2, 2, 64, 128), F32),
            pltpu.VMEM((24, ROWS), F32),
            pltpu.VMEM((4, 24, ROWS), F32),
            pltpu.VMEM((2, 24, ROWS), F32),
            pltpu.VMEM((2, 128, ROWS), F32),
            pltpu.VMEM((2, ROWS, 128), F32),
        ]
        + FACE_SCRATCH,
        compiler_params=pltpu.CompilerParams(vmem_limit_bytes=VMEM_LIMIT),
        name="step",
    )(parity, sigma_in, pace, za0, zb0, v, za_own, zb_own, summed, *others)


HALF_COS = [
    0.9999999991256178, -0.23370050635094053, 0.019968606689123116,
    -0.0008935362743290266, 2.3601076640059624e-05,
]
BAND_SQUARE = 1.5 * 1.5


def half_cosine(value):
    square = jnp.minimum(value * value, BAND_SQUARE)
    shape = F32(HALF_COS[4] / BAND_SQUARE**5)
    for k in (3, 2, 1, 0):
        shape = shape * square + F32(HALF_COS[k] / BAND_SQUARE ** (k + 1))
    return (BAND_SQUARE - square) * shape


def five_terms(centre, keep, dx, sx, dy, sy, dz, sz, dxy, dxz, dyz):
    twice = centre + centre
    xx, yy, zz = dx * dx, dy * dy, dz * dz
    squares = jnp.maximum(xx + yy + zz, 1.0)
    root = lax.rsqrt(squares)
    bend = (sx - twice) * (yy + zz) + (sy - twice) * (xx + zz) + (sz - twice) * (xx + yy)
    bend = bend - 0.5 * (dx * (dy * dxy + dz * dxz) + dy * dz * dyz)
    cosine = half_cosine(centre)
    spread = cosine * cosine
    if keep is not None:
        spread = jnp.where(keep, spread, 0.0)
    return (
        spread * (squares * root),
        spread * bend * (root * root),
        spread * dx,
        spread * dy,
        spread * dz,
    )


def brick_tables(ids, targets, live_count):
    entry = lax.broadcasted_iota(jnp.int32, (1, SLOTS), 1)
    live = entry < live_count
    row = lax.broadcasted_iota(jnp.int32, (SLOTS, SLOTS), 0)
    column = lax.broadcasted_iota(jnp.int32, (SLOTS, SLOTS), 1)
    owner = targets.astype(F32)
    down = jnp.sum(jnp.where(row == column, owner, 0.0), axis=1, keepdims=True)
    earlier = (row < column) & (row < live_count) & (down == owner)
    rank = jnp.sum(earlier.astype(F32), axis=0, keepdims=True)
    owner_at = jnp.where(live, owner, F32(SLOTS))
    peers = lax.broadcasted_iota(jnp.int32, (PEERS, SLOTS), 0).astype(F32)
    to_slot = [((owner_at == peers) & (rank == F32(c))).astype(F32) for c in range(2)]

    def finder(count, brick_of):
        at = lax.broadcasted_iota(jnp.int32, (count, SLOTS), 0)
        return (ids == brick_of(at)).astype(F32)

    return to_slot, finder


def exact_dot(left, right, dims=(((1,), (0,)), ((), ()))):
    return lax.dot_general(
        left, right, dims, precision=lax.Precision.HIGHEST, preferred_element_type=F32
    )


def neighbours(pair):
    return ((lane_down(pair[1]), pair[1]), (pair[0], lane_up(pair[0])))


def pair_terms(grid, keeps):
    two = range(2)

    def diff(first, second):
        return [grid[first][half] - grid[second][half] for half in two]

    def summed(first, second):
        return [grid[first][half] + grid[second][half] for half in two]

    dx, sx = diff((1, 0), (-1, 0)), summed((1, 0), (-1, 0))
    dy, sy = diff((0, 1), (0, -1)), summed((0, 1), (0, -1))
    over, under = diff((1, 1), (-1, 1)), diff((1, -1), (-1, -1))
    around, dx_around, dy_around = neighbours(grid[0, 0]), neighbours(dx), neighbours(dy)
    results = []
    for half in two:
        results.append(
            five_terms(
                grid[0, 0][half], keeps[half], dx[half], sx[half], dy[half], sy[half],
                around[half][1] - around[half][0], around[half][1] + around[half][0],
                over[half] - under[half],
                dx_around[half][1] - dx_around[half][0],
                dy_around[half][1] - dy_around[half][0],
            )
        )
    return [results[0][n] + results[1][n] for n in range(5)]


STAR = [(0, 0), (1, 0), (-1, 0), (0, 1), (0, -1), (1, 1), (1, -1), (-1, 1), (-1, -1)]


def tile_terms(vs, plane, k, keeps):
    grid = {
        (sx, sy): [vs[half, plane + sx, pl.ds(8 + 8 * k + sy, 8), :] for half in range(2)]
        for sx, sy in STAR
    }
    return pair_terms(grid, keeps)


def z_keeps(rows):
    lane = lax.broadcasted_iota(jnp.int32, (rows, 128), 1)
    return [lane != 0, lane != 127]


def inner_kernel(v, stack, vs):
    def fill(x, carry):
        for half in range(2):
            vs[half, x, 8 : 8 + CY, :] = v[x, :, pl.ds(128 * half, 128)]
            vs[half, x, 7:8, :] = jnp.zeros((1, 128), F32)
            vs[half, x, 8 + CY : 9 + CY, :] = jnp.zeros((1, 128), F32)
        return carry

    lax.fori_loop(0, CX, fill, 0)
    keeps = z_keeps(8)
    row = lax.broadcasted_iota(jnp.int32, (8, 128), 0)
    first = [keep & (row != 0) for keep in keeps]
    last = [keep & (row != 7) for keep in keeps]
    zeros = jnp.zeros((8, 128), F32)
    for bx in range(2):

        def body(step_at, sums):
            sums = list(sums)
            for sub in range(3):
                x = BRICK * bx + (1 - bx) + 3 * step_at + sub
                for k in range(YT):
                    parts = tile_terms(vs, x, k, first if k == 0 else last if k == 5 else keeps)
                    for n in range(5):
                        slot = 5 * (k // 2) + n
                        sums[slot] = sums[slot] + parts[n]
            return tuple(sums)

        sums = lax.fori_loop(0, 5, body, (zeros,) * 15)
        for by in range(3):
            row_at = 8 * (3 * bx + by)
            for n in range(5):
                total = jnp.sum(sums[5 * by + n], axis=0, keepdims=True)
                stack[row_at + n : row_at + n + 1, :] = total
            stack[row_at + 5 : row_at + 8, :] = jnp.zeros((3, 128), F32)


def edge_kernel(
    parity, count, inner, v, xa, xb, ya, yb, za, zb, y_rows, planes, ids, targets, record,
    vs, stack,
):
    x_sides = low_high(parity[0], xa[0], xb[0])
    y_sides = low_high(parity[1], ya[...], yb[...])
    under, over = low_high(parity[2], za[...], zb[...])
    stack[...] = inner[...]

    def add(b, n, row):
        stack[8 * b + n : 8 * b + n + 1, :] += row

    keeps = z_keeps(8)
    for side in range(2):
        for half in range(2):
            lanes = slice(128 * half, 128 * half + 128)
            for at in range(3):
                x = at - 1 if side == 0 else CX - 2 + at
                if 0 <= x < CX:
                    vs[half, at, 8 : 8 + CY, :] = v[x, :, lanes]
                else:
                    vs[half, at, 8 : 8 + CY, :] = x_sides[side][:, lanes]
                vs[half, at, 7:8, :] = y_sides[0][x + 1 : x + 2, lanes]
                vs[half, at, 8 + CY : 9 + CY, :] = y_sides[1][x + 1 : x + 2, lanes]
        for by in range(3):
            parts = [tile_terms(vs, 1, 2 * by + sub, keeps) for sub in range(2)]
            for n in range(5):
                add(3 * side + by, n, jnp.sum(parts[0][n] + parts[1][n], axis=0, keepdims=True))

    keeps = z_keeps(16)
    row = lax.broadcasted_iota(jnp.int32, (16, 128), 0)
    for side in range(2):
        if side == 0:
            rows = (y_sides[0], y_rows[0], y_rows[1])
        else:
            rows = (y_rows[2], y_rows[3], y_sides[1])
        for bx in range(2):
            grid = {
                (sx, sy): [
                    rows[1 + sy][1 + 16 * bx + sx : 17 + 16 * bx + sx, 128 * half : 128 * half + 128]
                    for half in range(2)
                ]
                for sx, sy in STAR
            }
            inside = row != (0 if bx == 0 else 15)
            parts = pair_terms(grid, [keep & inside for keep in keeps])
            for n in range(5):
                add(3 * bx + 2 * side, n, jnp.sum(parts[n], axis=0, keepdims=True))

    to_slot, finder = brick_tables(ids[...], targets[...], count[0])
    found = jnp.zeros((8, SLOTS), F32)
    for b in range(6):
        found = found + exact_dot(
            stack[8 * b : 8 * b + 8, :], finder(128, lambda at: 16 * b + at // 8)
        )
    for side in range(2):
        window = (under, planes[0], planes[1]) if side == 0 else (planes[2], planes[3], over)

        def cut(plane, step_x, step_y):
            part = window[plane][1 + step_x : 33 + step_x]
            return pltpu.roll(part, (-step_y) % 128, 1) if step_y else part

        high, low = cut(1, 1, 0), cut(1, -1, 0)
        right, left = cut(1, 0, 1), cut(1, 0, -1)
        above, below = cut(2, 0, 0), cut(0, 0, 0)
        terms = five_terms(
            cut(1, 0, 0), None,
            high - low, high + low, right - left, right + left, above - below, above + below,
            (cut(1, 1, 1) - cut(1, -1, 1)) - (cut(1, 1, -1) - cut(1, -1, -1)),
            (cut(2, 1, 0) - cut(2, -1, 0)) - (cut(0, 1, 0) - cut(0, -1, 0)),
            (cut(2, 0, 1) - cut(2, 0, -1)) - (cut(0, 0, 1) - cut(0, 0, -1)),
        )
        for bx in range(2):
            rows = [jnp.sum(term[16 * bx : 16 * bx + 16], axis=0, keepdims=True) for term in terms]
            rows = jnp.concatenate(rows + [jnp.zeros((3, 128), F32)], axis=0)
            found = found + exact_dot(
                rows,
                finder(
                    128,
                    lambda at: jnp.where(at < CY, 48 * bx + 16 * (at // 16) + 15 * side, -1),
                ),
            )
    scale = 2.0 / 3.0 / (BRICK * BRICK)
    row = lax.broadcasted_iota(jnp.int32, (8, SLOTS), 0)
    found = found * jnp.where(row == 1, F32(scale), F32(0.5 * scale))
    for c in range(2):
        record[:, 8 * c : 8 * c + 8] = exact_dot(to_slot[c], found, (((1,), (1,)), ((), ())))


def arrange_kernel(received, out):
    source = lax.broadcasted_iota(jnp.int32, (PEERS, SLOTS), 0)
    slot = lax.broadcasted_iota(jnp.int32, (PEERS, SLOTS), 1)
    total = jnp.zeros((8, SLOTS), F32)
    for c in range(2):
        total = total + exact_dot(
            received[:, 8 * c : 8 * c + 8], (slot == 2 * source + c).astype(F32),
            (((0,), (0,)), ((), ())),
        )
    for n in range(5):
        out[0, 0, n] = total[n : n + 1]


def arrange(received):
    return pl.pallas_call(
        arrange_kernel,
        out_shape=jax.ShapeDtypeStruct((1, 1, 5, 1, SLOTS), F32),
        in_specs=vmem_specs(1),
        out_specs=vmem_specs(1)[0],
        compiler_params=pltpu.CompilerParams(vmem_limit_bytes=VMEM_LIMIT),
        name="arrange",
    )(received)


def inner_bricks(v):
    return pl.pallas_call(
        inner_kernel,
        out_shape=jax.ShapeDtypeStruct((48, 128), F32),
        in_specs=vmem_specs(1),
        out_specs=vmem_specs(1)[0],
        scratch_shapes=[pltpu.VMEM((2, CX, 64, 128), F32)],
        compiler_params=pltpu.CompilerParams(vmem_limit_bytes=VMEM_LIMIT),
        cost_estimate=pl.CostEstimate(flops=20000000, bytes_accessed=6000000, transcendentals=400000),
        name="inner_bricks",
    )(v)


def edge_bricks(parity, count, inner, v, halos, y_rows, planes, ids, targets):
    return pl.pallas_call(
        edge_kernel,
        out_shape=jax.ShapeDtypeStruct((PEERS, 16), F32),
        in_specs=[pl.BlockSpec(memory_space=pltpu.SMEM)] * 2 + vmem_specs(12),
        out_specs=vmem_specs(1)[0],
        scratch_shapes=[
            pltpu.VMEM((2, 3, 64, 128), F32),
            pltpu.VMEM((48, 128), F32),
        ],
        compiler_params=pltpu.CompilerParams(vmem_limit_bytes=VMEM_LIMIT),
        name="edge_bricks",
    )(parity, count, inner, v, *halos, y_rows, planes, ids, targets)


def swap(value, axis, phase):
    count = lax.axis_size(axis)
    if phase == 0:
        pairs = [(i, i ^ 1) for i in range(count)]
    else:
        pairs = [(i, (i - 1 if i % 2 == 0 else i + 1) % count) for i in range(count)]
    return lax.ppermute(value, axis, pairs)


def exchange(faces):
    xa, xb, ya, yb, za, zb = faces
    zb = swap(zb, "gz", 1)
    yb = swap(yb, "gy", 1)
    ya = swap(ya, "gy", 0)
    za = swap(za, "gz", 0)
    xb = swap(xb, "gx", 1)
    xa = swap(xa, "gx", 0)
    return xa, xb, ya, yb, za, zb


def per_device(phi_start, band_ids, band_count, owners):
    parity = jnp.stack([lax.axis_index(name) % 2 for name in ("gx", "gy", "gz")])
    parity = parity.astype(jnp.int32)
    v, *faces = pack(parity, phi_start)
    sigma, pace = sign_fields(v)
    za0, zb0 = faces[4:]
    for number in range(STEPS):
        v, *faces = step(
            parity, sigma, pace, za0, zb0, v, faces[4], faces[5], exchange(faces),
            number == STEPS - 1,
        )
    level_set = unpack(v)

    xa, xb, ylo, yhi, own = faces
    xb = swap(xb, "gx", 1)
    xa = swap(xa, "gx", 0)
    ya, yb, y_rows = row_faces(parity, xa, xb, ylo, yhi)
    inner = inner_bricks(v)
    yb = swap(yb, "gy", 1)
    ya = swap(ya, "gy", 0)
    ya, yb, inner = lax.optimization_barrier((ya, yb, inner))
    planes, za, zb = plane_faces(parity, xa, xb, ya, yb, own)
    zb = swap(zb, "gz", 1)
    za = swap(za, "gz", 0)
    record = edge_bricks(
        parity, band_count.reshape(1), inner, v, (xa, xb, ya, yb, za, zb), y_rows, planes,
        band_ids.reshape(1, SLOTS), owners.reshape(1, SLOTS),
    )
    received = lax.all_to_all(record, ("gx", "gy"), split_axis=0, concat_axis=0, tiled=True)
    return level_set, jnp.swapaxes(arrange(received), 2, 3)


def solution(mesh):
    placed = (
        P("gx", "gy", "gz"),
        P("gx", "gy", "gz", None),
        P("gx", "gy", "gz"),
        P("gx", "gy", "gz", None),
    )
    return jax.shard_map(
        per_device,
        mesh=mesh,
        in_specs=placed,
        out_specs=(P("gx", "gy", "gz"), P("gx", "gy", "gz", None, None)),
        check_vma=False,
    )
```

```python
import functools

import jax
import jax.numpy as jnp
from jax import lax
from jax.experimental import pallas as pl
from jax.experimental.pallas import tpu as pltpu
from jax.sharding import PartitionSpec as P

STEPS = 3
BRICK = 16
SLOTS = 64
FIND_ROWS = 1280
PAIR = 8
ROW_PAIR = 4
PEERS = 32
CX, CY, CZ = 32, 48, 256
ROWS = CX * CY
YT = CY // 8
WENO_EPS = 1e-06
F32 = jnp.float32
VMEM_LIMIT = 16 * 1024 * 1024


def rcp(value):
    return pltpu.reciprocal(value, approx=True)


def smooth_weights(e_low, e_high, third):
    twice = third + third
    middle = e_low * e_high + (third * third * (4.0 / 3.0) + WENO_EPS)
    q_a = rcp(middle - e_low * twice)
    q_b = rcp(middle)
    q_c = rcp(middle + e_high * twice)
    return q_a * q_a, 6.0 * (q_b * q_b), q_c * q_c


def biased_parts(wa_next, wb, wc_prev, t_prev, t_here, t_next):
    x = wc_prev * (t_here - t_prev)
    y = wa_next * (t_next - t_here)
    both = x + y
    both = both + both
    total = (wa_next + wb) + wc_prev
    left = t_here + (both + y) * rcp(total + (wa_next + wa_next))
    right = t_here - (both + x) * rcp(total + (wc_prev + wc_prev))
    return left, right


def upwind_square(centre, left, right, sigma):
    return upwind_pair(centre - left, right - centre, sigma)


def upwind_pair(left, right_back, sigma):
    best = jnp.maximum(sigma * left, sigma * right_back)
    best = jnp.maximum(best, 0.0)
    return best * best


def sigma_of(value):
    return jnp.where(value > 0.0, F32(1.0), F32(-1.0))


def from_values(v_m, v_0, v_1, v_2):
    d_m, d_0, d_1 = v_0 - v_m, v_1 - v_0, v_2 - v_1
    e_0, e_1 = d_0 - d_m, d_1 - d_0
    return e_0, e_1, e_1 - e_0


def lane_down(part):
    return pltpu.roll(part, 1, 1)


def lane_up(part):
    return pltpu.roll(part, 127, 1)


def z_stage_weights(even, odd, even_down, odd_down, even_up, odd_up):
    v = {-2: even_down, -1: odd_down, 0: even, 1: odd, 2: even_up, 3: odd_up}
    d = {k: v[k + 1] - v[k] for k in range(-2, 3)}
    e = {k: d[k] - d[k - 1] for k in range(-1, 3)}
    t = {k: e[k + 1] - e[k] for k in range(-1, 2)}
    w_0 = smooth_weights(e[0], e[1], t[0])
    w_1 = smooth_weights(e[1], e[2], t[1])
    return (
        w_1[0], w_0[1], lane_down(w_1[2]), t[-1], t[0], t[1],
        lane_up(w_0[0]), w_1[1], w_0[2], lane_up(t[0]),
        3.0 * (d[-1] + d[0]), 3.0 * (d[0] + d[1]),
    )


def z_stage_parts(wa_0, wb_0, wc_0, t_m, t_0, t_1, wa_1, wb_1, wc_1, t_2, centre_0, centre_1):
    left_0, right_0 = biased_parts(wa_0, wb_0, wc_0, t_m, t_0, t_1)
    left_1, right_1 = biased_parts(wa_1, wb_1, wc_1, t_0, t_1, t_2)
    return centre_0, lane_down(left_1), right_0 - centre_0, centre_1 - left_0, right_1 - centre_1


def edge_column(window, u_ref, p_ref, u_row, p_row, sigma):
    def rows(start):
        return window[pl.ds(start, 8), :]

    e_0, e_1, t = from_values(rows(u_row - 1), rows(u_row), rows(u_row + 1), rows(u_row + 2))
    w_a, w_b, w_c = smooth_weights(e_0, e_1, t)
    for slot, part in enumerate((w_a, w_b, w_c, t)):
        u_ref[slot, pl.ds(u_row, 8), :] = part
    left, right = biased_parts(
        u_ref[0, pl.ds(p_row + 1, 8), :],
        u_ref[1, pl.ds(p_row, 8), :],
        u_ref[2, pl.ds(p_row - 1, 8), :],
        u_ref[3, pl.ds(p_row - 1, 8), :],
        u_ref[3, pl.ds(p_row, 8), :],
        u_ref[3, pl.ds(p_row + 1, 8), :],
    )
    p_ref[0, pl.ds(p_row, 8), :] = left
    p_ref[1, pl.ds(p_row, 8), :] = right
    centre = 3.0 * (rows(9) - rows(7))
    return upwind_square(
        centre, p_ref[0, pl.ds(7, 8), :], p_ref[1, pl.ds(8, 8), :], sigma
    )


def z_faces(source, zlo, zhi):
    for chunk in range(CX // 8):
        columns = slice(8 * CY * chunk, 8 * CY * (chunk + 1))
        for parity in range(2):
            part = source[8 * chunk : 8 * chunk + 8, :, 128 * parity : 128 * parity + 128]
            part = part.reshape(8 * CY, 128).T
            for k in range(4):
                zlo[2 * k + parity : 2 * k + parity + 1, columns] = part[k : k + 1]
                zhi[2 * k + parity : 2 * k + parity + 1, columns] = part[124 + k : 125 + k]


def y_faces(source, ylo, yhi, width):
    for x in range(CX):
        for k in range(width):
            ylo[k, x : x + 1, :] = source[x, k : k + 1, :]
            yhi[k, x : x + 1, :] = source[x, CY - width + k : CY - width + 1 + k, :]


def write_swap(parity, low, high, out_a, out_b):
    odd = parity == 1
    out_a[...] = jnp.where(odd, low, high)
    out_b[...] = jnp.where(odd, high, low)


def write_faces(parity, source, xa, xb, ya, yb, za, zb, yf, zf):
    y_faces(source, yf.at[0], yf.at[1], 3)
    write_swap(parity[1], yf[0], yf[1], ya, yb)
    write_swap(parity[0], source[0:3], source[CX - 3 : CX], xa, xb)
    z_faces(source, zf.at[0], zf.at[1])
    write_swap(parity[2], zf[0], zf[1], za, zb)


def low_high(parity, part_a, part_b):
    odd = parity == 1
    return jnp.where(odd, part_a, part_b), jnp.where(odd, part_b, part_a)


def pack_kernel(parity, phi, mixed, xa, xb, ya, yb, za, zb, turned, yf, zf):
    for chunk in range(CX // 8):
        planes = slice(8 * chunk, 8 * chunk + 8)
        for half in range(2):
            part = phi[planes, :, 128 * half : 128 * half + 128]
            part = part.reshape(8 * CY, 128).T
            for c in range(3):
                turned[c, 128 * half : 128 * half + 128, :] = part[:, 128 * c : 128 * c + 128]
        for which in range(2):
            part = [turned[c, pl.ds(which, 128, stride=2), :].T for c in range(3)]
            part = jnp.concatenate(part, axis=0)
            mixed[planes, :, 128 * which : 128 * which + 128] = part.reshape(8, CY, 128)
    write_faces(parity, mixed, xa, xb, ya, yb, za, zb, yf, zf)


def signs_kernel(start, sigma, pace):
    def signs(x, carry):
        value = start[x]
        sigma[x] = sigma_of(value)
        pace[x] = (0.05 * value) * lax.rsqrt(value * value + 1.0)
        return carry

    lax.fori_loop(0, CX, signs, 0)


def unpack_kernel(mixed, out, turned):
    for chunk in range(CX // 8):
        planes = slice(8 * chunk, 8 * chunk + 8)
        for parity in range(2):
            part = mixed[planes, :, 128 * parity : 128 * parity + 128]
            part = part.reshape(8 * CY, 128).T
            for c in range(3):
                turned[c, pl.ds(parity, 128, stride=2), :] = part[:, 128 * c : 128 * c + 128]
        for half in range(2):
            part = [turned[c, 128 * half : 128 * half + 128, :].T for c in range(3)]
            part = jnp.concatenate(part, axis=0)
            out[planes, :, 128 * half : 128 * half + 128] = part.reshape(8, CY, 128)


def edge_lanes():
    lane = lax.broadcasted_iota(jnp.int32, (8, 128), 1)
    return [(lane < 2) | (lane == 127), (lane < 1) | (lane > 125)]


def run_stages(stages, count):
    depth = len(stages) - 1

    def run(at, low, high):
        for delay in range(high, low - 1, -1):
            stages[delay](at - delay)

    def body(at, carry):
        run(at, 0, depth)
        return carry

    for at in range(depth):
        run(at, 0, at)
    lax.fori_loop(depth, count, body, 0)
    for at in range(depth):
        run(count + at, at + 1, depth)


def xz_kernel(parity, sigma_in, v, xa_in, xb_in, summed, xh, rolled, zs, zp):
    xh[0], xh[1] = low_high(parity[0], xa_in[...], xb_in[...])

    def x_pass(yt, carry):
        row = pl.multiple_of(8 * yt, 8)
        for zt in range(2):
            lanes = pl.ds(128 * zt, 128)

            def cell(x):
                if x < 0:
                    return xh[0, 3 + x, pl.ds(row, 8), lanes]
                if x >= CX:
                    return xh[1, x - CX, pl.ds(row, 8), lanes]
                return v[x, pl.ds(row, 8), lanes]

            d, e, t, weights, lefts, rights = {}, {}, {}, {}, {}, {}
            d[-3] = cell(-2) - cell(-3)
            d[-2] = cell(-1) - cell(-2)
            e[-2] = d[-2] - d[-3]
            for j in range(-2, CX + 1):
                d[j + 1] = cell(j + 2) - cell(j + 1)
                e[j + 1] = d[j + 1] - d[j]
                t[j] = e[j + 1] - e[j]
                weights[j] = smooth_weights(e[j], e[j + 1], t[j])
                p = j - 1
                if p >= -1:
                    lefts[p], rights[p] = biased_parts(
                        weights[p + 1][0], weights[p][1], weights[p - 1][2], t[p - 1], t[p], t[p + 1]
                    )
                if p >= 0:
                    sigma = sigma_in[p, pl.ds(row, 8), lanes]
                    centre = 3.0 * (d[p - 1] + d[p])
                    summed[zt, p, pl.ds(row, 8), :] = upwind_square(
                        centre, lefts[p - 1], rights[p], sigma
                    )
        return carry

    lax.fori_loop(0, YT, x_pass, 0)
    edge = edge_lanes()

    def tile(x, half, k):
        return v[x, 8 * k : 8 * k + 8, 128 * half : 128 * half + 128]

    def spots(item):
        for sub in range(PAIR):
            for k in range(YT):
                start = CY * sub + 8 * k
                yield PAIR * item + sub, k, slice(start, start + 8)

    def turn(item):
        for x, k, at in spots(item):
            for half in range(2):
                part = tile(x, half, k)
                rolled[half, at, :] = lane_down(part)
                rolled[2 + half, at, :] = lane_up(part)

    def weigh(item):
        for x, k, at in spots(item):
            parts = z_stage_weights(
                tile(x, 0, k), tile(x, 1, k), *[rolled[slot, at, :] for slot in range(4)]
            )
            for slot, part in enumerate(parts):
                zs[slot, at, :] = part

    def blend(item):
        for x, k, at in spots(item):
            parts = z_stage_parts(*[zs[slot, at, :] for slot in range(12)])
            for slot, part in enumerate(parts):
                zp[slot, at, :] = part

    def add(item):
        for x, k, at in spots(item):
            rows = slice(8 * k, 8 * k + 8)
            for half in range(2):
                sigma = sigma_in[x, rows, 128 * half : 128 * half + 128]
                if half == 0:
                    along = upwind_pair(zp[0, at, :] - zp[1, at, :], zp[2, at, :], sigma)
                else:
                    along = upwind_pair(zp[3, at, :], zp[4, at, :], sigma)
                summed[half, x, rows, :] += jnp.where(edge[half], 0.0, along)

    run_stages((turn, weigh, blend, add), CX // PAIR)


def step_kernel(
    last,
    parity, sigma_in, pace, za0, zb0, v, za_own, zb_own, summed, ya_in, yb_in, za_in, zb_in,
    *refs,
):
    faces = 6 if last else 7
    step_body(last, parity, sigma_in, pace, za0, zb0, v, za_own, zb_own, summed, ya_in,
              yb_in, za_in, zb_in, refs[:faces], *refs[faces:])


def step_body(
    last,
    parity, sigma_in, pace, za0, zb0, v, za_own, zb_own, summed, ya_in, yb_in, za_in, zb_in,
    outs,
    vs, u_ref, p_ref, window, zu_ref, zp_ref, edges, fixes, yf, zf,
):
    out = outs[0]

    def fill(x, carry):
        for zt in range(2):
            vs[zt, x, 8 : 8 + CY, :] = v[x, :, pl.ds(128 * zt, 128)]
        return carry

    lax.fori_loop(0, CX, fill, 0)
    yf[0], yf[1] = low_high(parity[1], ya_in[...], yb_in[...])
    for x in range(CX):
        for zt in range(2):
            lanes = slice(128 * zt, 128 * zt + 128)
            for k in range(3):
                vs[zt, x, 5 + k : 6 + k, :] = yf[0, k, x : x + 1, lanes]
                vs[zt, x, 8 + CY + k : 9 + CY + k, :] = yf[1, k, x : x + 1, lanes]

    z_low, z_high = low_high(parity[2], za_in[...], zb_in[...])
    zlo0, zhi0 = low_high(parity[2], za0[...], zb0[...])
    zlo_own, zhi_own = low_high(parity[2], za_own[...], zb_own[...])
    window[5:8, :] = z_low[5:8]
    window[8:16, :] = zlo_own
    fixed = edge_column(window, zu_ref, zp_ref, 6, 7, sigma_of(zlo0))
    for half, lane_at, cell_at in ((0, 0, 0), (0, 1, 2), (1, 0, 1)):
        edges[half, lane_at : lane_at + 1, :] = fixed[cell_at : cell_at + 1]
    window[8:16, :] = zhi_own
    window[16:19, :] = z_high[0:3]
    fixed = edge_column(window, zu_ref, zp_ref, 9, 8, sigma_of(zhi0))
    for half, lane_at, cell_at in ((0, 127, 6), (1, 126, 5), (1, 127, 7)):
        edges[half, lane_at : lane_at + 1, :] = fixed[cell_at : cell_at + 1]
    for half in range(2):
        fixes[half] = edges[half].T

    edge = edge_lanes()

    def y_weights(x, spot, zt, k):
        start = 6 + 8 * k
        e_0, e_1, t = from_values(
            *[vs[zt, x, pl.ds(start + shift, 8), :] for shift in (-1, 0, 1, 2)]
        )
        w_a, w_b, w_c = smooth_weights(e_0, e_1, t)
        for slot, part in enumerate((w_a, w_b, w_c, t)):
            u_ref[spot, slot, pl.ds(8 * k, 8), :] = part

    def y_parts(spot, k):
        def read(slot, row):
            return u_ref[spot, slot, pl.ds(row, 8), :]

        row = 8 * k + 1
        left, right = biased_parts(
            read(0, row + 1), read(1, row), read(2, row - 1),
            read(3, row - 1), read(3, row), read(3, row + 1),
        )
        p_ref[spot, 0, pl.ds(8 * k, 8), :] = left
        p_ref[spot, 1, pl.ds(8 * k, 8), :] = right

    def weigh(item):
        for sub in range(ROW_PAIR):
            for zt in range(2):
                for k in range(YT + 1):
                    y_weights(ROW_PAIR * item + sub, 2 * sub + zt, zt, k)

    def blend(item):
        for spot in range(2 * ROW_PAIR):
            for k in range(YT + 1):
                y_parts(spot, k)

    def update(item):
        for sub in range(ROW_PAIR):
            update_plane(ROW_PAIR * item + sub, 2 * sub)

    def update_plane(x, spot):
        flat = pl.multiple_of(x * CY, 8)
        for zt in range(2):
            for k in range(YT):
                rows = slice(8 * k, 8 * k + 8)
                lanes = slice(128 * zt, 128 * zt + 128)
                centre = 3.0 * (
                    vs[zt, x, 9 + 8 * k : 17 + 8 * k, :] - vs[zt, x, 7 + 8 * k : 15 + 8 * k, :]
                )
                along = upwind_square(
                    centre, p_ref[spot + zt, 0, rows, :],
                    p_ref[spot + zt, 1, 8 * k + 1 : 8 * k + 9, :],
                    sigma_in[x, rows, lanes],
                )
                fix = jnp.where(edge[zt], fixes[zt, pl.ds(flat + 8 * k, 8), :], 0.0)
                total = summed[zt, x, rows, :] + along + fix
                root = total * lax.rsqrt(jnp.maximum(total, 1e-30))
                out[x, rows, lanes] = v[x, rows, lanes] - pace[x, rows, lanes] * (root - 6.0)

    run_stages((weigh, blend, update), CX // ROW_PAIR)
    if last:
        xa, xb, ylo, yhi, planes = outs[1:]
        write_swap(parity[0], out[0:1], out[CX - 1 : CX], xa, xb)
        y_faces(out, ylo, yhi, 2)
        planes[...] = jnp.zeros((4, CX, 128), F32)
        for chunk in range(CX // 8):
            for half in range(2):
                part = out[8 * chunk : 8 * chunk + 8, :, 128 * half : 128 * half + 128]
                part = part.reshape(8 * CY, 128).T
                for x in range(8):
                    lanes = slice(CY * x, CY * x + CY)
                    at = slice(8 * chunk + x, 8 * chunk + x + 1)
                    planes[half, at, 0:CY] = part[0:1, lanes]
                    planes[2 + half, at, 0:CY] = part[127:128, lanes]
    else:
        write_faces(parity, out, *outs[1:], yf, zf)


def rows_kernel(parity, xa, xb, ylo, yhi, ya, yb, y_rows):
    x_low, x_high = low_high(parity[0], xa[0], xb[0])
    for at, (source, layer, row) in enumerate(
        ((ylo, 0, 0), (ylo, 1, 1), (yhi, 0, CY - 2), (yhi, 1, CY - 1))
    ):
        y_rows[at, 0:1, :] = x_low[row : row + 1]
        y_rows[at, 1 : CX + 1, :] = source[layer]
        y_rows[at, CX + 1 : CX + 2, :] = x_high[row : row + 1]
    write_swap(parity[1], y_rows[0], y_rows[3], ya, yb)


def fill_planes(parity, xa, xb, own, planes):
    x_sides = low_high(parity[0], xa[0], xb[0])
    planes[...] = jnp.zeros((4, 40, 128), F32)
    for q in range(4):
        planes[q, 1 : CX + 1, :] = own[q]
    for side in range(2):
        row = (CX + 1) * side
        for half in range(2):
            turned = x_sides[side][:, 128 * half : 128 * half + 128].T
            planes[half, row : row + 1, 0:CY] = turned[0:1]
            planes[2 + half, row : row + 1, 0:CY] = turned[127:128]


def planes_kernel(parity, ya, yb, partial, planes, za, zb):
    y_low, y_high = low_high(parity[1], ya[...], yb[...])
    planes[...] = partial[...]
    lane = lax.broadcasted_iota(jnp.int32, (CX + 2, 128), 1)
    for q in range(4):
        lanes = slice(128 * (q % 2), 128 * (q % 2) + 128)
        start = 0 if q < 2 else 127
        low = y_low[:, lanes]
        if start != 127:
            low = pltpu.roll(low, 127 - start, 1)
        high = pltpu.roll(y_high[:, lanes], (CY - start) % 128, 1)
        planes[q, 0 : CX + 2, :] = jnp.where(
            lane == 127, low, jnp.where(lane == CY, high, partial[q, 0 : CX + 2, :])
        )
    write_swap(parity[2], planes[0], planes[3], za, zb)


def face_shapes(width):
    shapes = [(width, CY, CZ)] * 2 + [(max(width, 2), CX, CZ)] * 2
    shapes += [(8, ROWS)] * 2 if width == 3 else [(4, CX, 128)]
    return [jax.ShapeDtypeStruct(shape, F32) for shape in shapes]


def row_faces(parity, xa, xb, ylo, yhi):
    return pl.pallas_call(
        rows_kernel,
        out_shape=[jax.ShapeDtypeStruct((CX + 2, CZ), F32)] * 2
        + [jax.ShapeDtypeStruct((4, CX + 2, CZ), F32)],
        in_specs=parity_specs(4),
        out_specs=vmem_specs(3),
        compiler_params=pltpu.CompilerParams(vmem_limit_bytes=VMEM_LIMIT),
        name="row_faces",
    )(parity, xa, xb, ylo, yhi)


def plane_faces(parity, ya, yb, partial):
    return pl.pallas_call(
        planes_kernel,
        out_shape=[jax.ShapeDtypeStruct(shape, F32) for shape in ((4, 40, 128), (40, 128), (40, 128))],
        in_specs=parity_specs(3),
        out_specs=vmem_specs(3),
        compiler_params=pltpu.CompilerParams(vmem_limit_bytes=VMEM_LIMIT),
        name="plane_faces",
    )(parity, ya, yb, partial)


BLOCK = jax.ShapeDtypeStruct((CX, CY, CZ), F32)
FACE_SCRATCH = [pltpu.VMEM((2, 3, CX, CZ), F32), pltpu.VMEM((2, 8, ROWS), F32)]


def vmem_specs(count):
    return [pl.BlockSpec(memory_space=pltpu.VMEM)] * count


def parity_specs(count):
    return [pl.BlockSpec(memory_space=pltpu.SMEM)] + vmem_specs(count)


def pack(parity, phi):
    return pl.pallas_call(
        pack_kernel,
        out_shape=[BLOCK] + face_shapes(3),
        in_specs=parity_specs(1),
        out_specs=vmem_specs(7),
        scratch_shapes=[pltpu.VMEM((3, CZ, 128), F32)]
        + FACE_SCRATCH,
        compiler_params=pltpu.CompilerParams(vmem_limit_bytes=VMEM_LIMIT),
        name="pack",
    )(parity, phi)


def sign_fields(start):
    return pl.pallas_call(
        signs_kernel,
        out_shape=[BLOCK] * 2,
        in_specs=vmem_specs(1),
        out_specs=vmem_specs(2),
        compiler_params=pltpu.CompilerParams(vmem_limit_bytes=VMEM_LIMIT),
        cost_estimate=pl.CostEstimate(flops=2000000, bytes_accessed=4700000, transcendentals=400000),
        name="sign_fields",
    )(start)


def unpack(mixed):
    return pl.pallas_call(
        unpack_kernel,
        out_shape=BLOCK,
        in_specs=vmem_specs(1),
        out_specs=vmem_specs(1)[0],
        scratch_shapes=[pltpu.VMEM((3, CZ, 128), F32)],
        compiler_params=pltpu.CompilerParams(vmem_limit_bytes=VMEM_LIMIT),
        name="unpack",
    )(mixed)


def xz_sums(parity, sigma, v, xa, xb):
    return pl.pallas_call(
        xz_kernel,
        out_shape=jax.ShapeDtypeStruct((2, CX, CY, 128), F32),
        in_specs=parity_specs(4),
        out_specs=vmem_specs(1)[0],
        scratch_shapes=[
            pltpu.VMEM((2, 3, CY, CZ), F32),
            pltpu.VMEM((4, PAIR * CY, 128), F32),
            pltpu.VMEM((12, PAIR * CY, 128), F32),
            pltpu.VMEM((5, PAIR * CY, 128), F32),
        ],
        compiler_params=pltpu.CompilerParams(vmem_limit_bytes=VMEM_LIMIT),
        cost_estimate=pl.CostEstimate(flops=20000000, bytes_accessed=6000000, transcendentals=400000),
        name="xz_sums",
    )(parity, sigma, v, xa, xb)


def step(parity, sigma_in, pace, za0, zb0, v, za_own, zb_own, halos, last):
    xa, xb, *others = halos
    summed = xz_sums(parity, sigma_in, v, xa, xb)
    return pl.pallas_call(
        functools.partial(step_kernel, last),
        out_shape=[BLOCK] + face_shapes(1 if last else 3),
        in_specs=parity_specs(12),
        out_specs=vmem_specs(6 if last else 7),
        scratch_shapes=[
            pltpu.VMEM((2, CX, 64, 128), F32),
            pltpu.VMEM((2 * ROW_PAIR, 4, 64, 128), F32),
            pltpu.VMEM((2 * ROW_PAIR, 2, 64, 128), F32),
            pltpu.VMEM((24, ROWS), F32),
            pltpu.VMEM((4, 24, ROWS), F32),
            pltpu.VMEM((2, 24, ROWS), F32),
            pltpu.VMEM((2, 128, ROWS), F32),
            pltpu.VMEM((2, ROWS, 128), F32),
        ]
        + FACE_SCRATCH,
        compiler_params=pltpu.CompilerParams(vmem_limit_bytes=VMEM_LIMIT),
        name="step",
    )(parity, sigma_in, pace, za0, zb0, v, za_own, zb_own, summed, *others)


HALF_COS = [
    0.9999999991256178, -0.23370050635094053, 0.019968606689123116,
    -0.0008935362743290266, 2.3601076640059624e-05,
]
BAND_SQUARE = 1.5 * 1.5


def half_cosine(value):
    square = jnp.minimum(value * value, BAND_SQUARE)
    shape = F32(HALF_COS[4] / BAND_SQUARE**5)
    for k in (3, 2, 1, 0):
        shape = shape * square + F32(HALF_COS[k] / BAND_SQUARE ** (k + 1))
    return (BAND_SQUARE - square) * shape


def five_terms(centre, keep, dx, sx, dy, sy, dz, sz, dxy, dxz, dyz):
    twice = centre + centre
    xx, yy, zz = dx * dx, dy * dy, dz * dz
    squares = jnp.maximum(xx + yy + zz, 1.0)
    root = lax.rsqrt(squares)
    bend = (sx - twice) * (yy + zz) + (sy - twice) * (xx + zz) + (sz - twice) * (xx + yy)
    bend = bend - 0.5 * (dx * (dy * dxy + dz * dxz) + dy * dz * dyz)
    cosine = half_cosine(centre)
    spread = cosine * cosine
    if keep is not None:
        spread = jnp.where(keep, spread, 0.0)
    return (
        spread * (squares * root),
        spread * bend * (root * root),
        spread * dx,
        spread * dy,
        spread * dz,
    )


def brick_tables(ids, targets, live_count):
    entry = lax.broadcasted_iota(jnp.int32, (1, SLOTS), 1)
    live = entry < live_count
    row = lax.broadcasted_iota(jnp.int32, (SLOTS, SLOTS), 0)
    column = lax.broadcasted_iota(jnp.int32, (SLOTS, SLOTS), 1)
    owner = targets.astype(F32)
    down = jnp.sum(jnp.where(row == column, owner, 0.0), axis=1, keepdims=True)
    earlier = (row < column) & (row < live_count) & (down == owner)
    rank = jnp.sum(earlier.astype(F32), axis=0, keepdims=True)
    owner_at = jnp.where(live, owner, F32(SLOTS))
    peers = lax.broadcasted_iota(jnp.int32, (PEERS, SLOTS), 0).astype(F32)
    to_slot = [((owner_at == peers) & (rank == F32(c))).astype(F32) for c in range(2)]

    at = lax.broadcasted_iota(jnp.int32, (FIND_ROWS, SLOTS), 0)
    inner = 16 * (at // 128) + at % 128 // 8
    face = at - 768
    y = face % 128
    end = 48 * (face // 128 % 2) + 16 * (y // 16) + 15 * (face // 256)
    brick = jnp.where(at < 768, inner, jnp.where(y < CY, end, -1))
    return to_slot, (ids == brick).astype(F32)


def exact_dot(left, right, dims=(((1,), (0,)), ((), ()))):
    return lax.dot_general(
        left, right, dims, precision=lax.Precision.HIGHEST, preferred_element_type=F32
    )


def neighbours(pair):
    return ((lane_down(pair[1]), pair[1]), (pair[0], lane_up(pair[0])))


def pair_terms(grid, keeps):
    two = range(2)

    def diff(first, second):
        return [grid[first][half] - grid[second][half] for half in two]

    def summed(first, second):
        return [grid[first][half] + grid[second][half] for half in two]

    dx, sx = diff((1, 0), (-1, 0)), summed((1, 0), (-1, 0))
    dy, sy = diff((0, 1), (0, -1)), summed((0, 1), (0, -1))
    over, under = diff((1, 1), (-1, 1)), diff((1, -1), (-1, -1))
    around, dx_around, dy_around = neighbours(grid[0, 0]), neighbours(dx), neighbours(dy)
    results = []
    for half in two:
        results.append(
            five_terms(
                grid[0, 0][half], keeps[half], dx[half], sx[half], dy[half], sy[half],
                around[half][1] - around[half][0], around[half][1] + around[half][0],
                over[half] - under[half],
                dx_around[half][1] - dx_around[half][0],
                dy_around[half][1] - dy_around[half][0],
            )
        )
    return [results[0][n] + results[1][n] for n in range(5)]


STAR = [(0, 0), (1, 0), (-1, 0), (0, 1), (0, -1), (1, 1), (1, -1), (-1, 1), (-1, -1)]


def tile_terms(vs, plane, k, keeps):
    grid = {
        (sx, sy): [vs[half, plane + sx, pl.ds(8 + 8 * k + sy, 8), :] for half in range(2)]
        for sx, sy in STAR
    }
    return pair_terms(grid, keeps)


def z_keeps(rows):
    lane = lax.broadcasted_iota(jnp.int32, (rows, 128), 1)
    return [lane != 0, lane != 127]


def inner_kernel(
    parity, count, v, xa, xb, own, ids, targets, stack, partial, to_slot, finder, vs
):
    fill_planes(parity, xa, xb, own, partial)
    slots, found = brick_tables(ids[...], targets[...], count[0])
    for c in range(2):
        to_slot[c] = slots[c]
    finder[...] = found

    def fill(x, carry):
        for half in range(2):
            vs[half, x, 8 : 8 + CY, :] = v[x, :, pl.ds(128 * half, 128)]
            vs[half, x, 7:8, :] = jnp.zeros((1, 128), F32)
            vs[half, x, 8 + CY : 9 + CY, :] = jnp.zeros((1, 128), F32)
        return carry

    lax.fori_loop(0, CX, fill, 0)
    keeps = z_keeps(8)
    row = lax.broadcasted_iota(jnp.int32, (8, 128), 0)
    first = [keep & (row != 0) for keep in keeps]
    last = [keep & (row != 7) for keep in keeps]
    zeros = jnp.zeros((8, 128), F32)
    for bx in range(2):

        def body(step_at, sums):
            sums = list(sums)
            for sub in range(3):
                x = BRICK * bx + (1 - bx) + 3 * step_at + sub
                for k in range(YT):
                    parts = tile_terms(vs, x, k, first if k == 0 else last if k == 5 else keeps)
                    for n in range(5):
                        slot = 5 * (k // 2) + n
                        sums[slot] = sums[slot] + parts[n]
            return tuple(sums)

        sums = lax.fori_loop(0, 5, body, (zeros,) * 15)
        for by in range(3):
            row_at = 8 * (3 * bx + by)
            for n in range(5):
                total = jnp.sum(sums[5 * by + n], axis=0, keepdims=True)
                stack[row_at + n : row_at + n + 1, :] = total
            stack[row_at + 5 : row_at + 8, :] = jnp.zeros((3, 128), F32)


def edge_kernel(
    parity, inner, v, xa, xb, ya, yb, za, zb, y_rows, planes, to_slot, finder, record,
    vs, stack, gathered,
):
    x_sides = low_high(parity[0], xa[0], xb[0])
    y_sides = low_high(parity[1], ya[...], yb[...])
    under, over = low_high(parity[2], za[...], zb[...])
    stack[...] = inner[...]

    def add(b, n, row):
        stack[8 * b + n : 8 * b + n + 1, :] += row

    keeps = z_keeps(8)
    for side in range(2):
        for half in range(2):
            lanes = slice(128 * half, 128 * half + 128)
            for at in range(3):
                x = at - 1 if side == 0 else CX - 2 + at
                if 0 <= x < CX:
                    vs[half, at, 8 : 8 + CY, :] = v[x, :, lanes]
                else:
                    vs[half, at, 8 : 8 + CY, :] = x_sides[side][:, lanes]
                vs[half, at, 7:8, :] = y_sides[0][x + 1 : x + 2, lanes]
                vs[half, at, 8 + CY : 9 + CY, :] = y_sides[1][x + 1 : x + 2, lanes]
        for by in range(3):
            parts = [tile_terms(vs, 1, 2 * by + sub, keeps) for sub in range(2)]
            for n in range(5):
                add(3 * side + by, n, jnp.sum(parts[0][n] + parts[1][n], axis=0, keepdims=True))

    keeps = z_keeps(16)
    row = lax.broadcasted_iota(jnp.int32, (16, 128), 0)
    for side in range(2):
        if side == 0:
            rows = (y_sides[0], y_rows[0], y_rows[1])
        else:
            rows = (y_rows[2], y_rows[3], y_sides[1])
        for bx in range(2):
            grid = {
                (sx, sy): [
                    rows[1 + sy][1 + 16 * bx + sx : 17 + 16 * bx + sx, 128 * half : 128 * half + 128]
                    for half in range(2)
                ]
                for sx, sy in STAR
            }
            inside = row != (0 if bx == 0 else 15)
            parts = pair_terms(grid, [keep & inside for keep in keeps])
            for n in range(5):
                add(3 * bx + 2 * side, n, jnp.sum(parts[n], axis=0, keepdims=True))

    for b in range(6):
        gathered[:, 128 * b : 128 * b + 128] = stack[8 * b : 8 * b + 8, :]
    for side in range(2):
        window = (under, planes[0], planes[1]) if side == 0 else (planes[2], planes[3], over)

        def cut(plane, step_x, step_y):
            part = window[plane][1 + step_x : 33 + step_x]
            return pltpu.roll(part, (-step_y) % 128, 1) if step_y else part

        high, low = cut(1, 1, 0), cut(1, -1, 0)
        right, left = cut(1, 0, 1), cut(1, 0, -1)
        above, below = cut(2, 0, 0), cut(0, 0, 0)
        terms = five_terms(
            cut(1, 0, 0), None,
            high - low, high + low, right - left, right + left, above - below, above + below,
            (cut(1, 1, 1) - cut(1, -1, 1)) - (cut(1, 1, -1) - cut(1, -1, -1)),
            (cut(2, 1, 0) - cut(2, -1, 0)) - (cut(0, 1, 0) - cut(0, -1, 0)),
            (cut(2, 0, 1) - cut(2, 0, -1)) - (cut(0, 0, 1) - cut(0, 0, -1)),
        )
        for bx in range(2):
            rows = [jnp.sum(term[16 * bx : 16 * bx + 16], axis=0, keepdims=True) for term in terms]
            rows = jnp.concatenate(rows + [jnp.zeros((3, 128), F32)], axis=0)
            start = 768 + 256 * side + 128 * bx
            gathered[:, start : start + 128] = rows
    found = exact_dot(gathered[...], finder[...])
    scale = 2.0 / 3.0 / (BRICK * BRICK)
    row = lax.broadcasted_iota(jnp.int32, (8, SLOTS), 0)
    found = found * jnp.where(row == 1, F32(scale), F32(0.5 * scale))
    for c in range(2):
        record[:, 8 * c : 8 * c + 8] = exact_dot(to_slot[c], found, (((1,), (1,)), ((), ())))


def arrange_kernel(received, out):
    source = lax.broadcasted_iota(jnp.int32, (PEERS, SLOTS), 0)
    slot = lax.broadcasted_iota(jnp.int32, (PEERS, SLOTS), 1)
    total = jnp.zeros((8, SLOTS), F32)
    for c in range(2):
        total = total + exact_dot(
            received[:, 8 * c : 8 * c + 8], (slot == 2 * source + c).astype(F32),
            (((0,), (0,)), ((), ())),
        )
    for n in range(5):
        out[0, 0, n] = total[n : n + 1]


def arrange(received):
    return pl.pallas_call(
        arrange_kernel,
        out_shape=jax.ShapeDtypeStruct((1, 1, 5, 1, SLOTS), F32),
        in_specs=vmem_specs(1),
        out_specs=vmem_specs(1)[0],
        compiler_params=pltpu.CompilerParams(vmem_limit_bytes=VMEM_LIMIT),
        name="arrange",
    )(received)


def inner_bricks(parity, count, v, xa, xb, own, ids, targets):
    shapes = [(48, 128), (4, 40, 128), (2, PEERS, SLOTS), (FIND_ROWS, SLOTS)]
    return pl.pallas_call(
        inner_kernel,
        out_shape=[jax.ShapeDtypeStruct(shape, F32) for shape in shapes],
        in_specs=[pl.BlockSpec(memory_space=pltpu.SMEM)] * 2 + vmem_specs(6),
        out_specs=vmem_specs(4),
        scratch_shapes=[pltpu.VMEM((2, CX, 64, 128), F32)],
        compiler_params=pltpu.CompilerParams(vmem_limit_bytes=VMEM_LIMIT),
        cost_estimate=pl.CostEstimate(flops=20000000, bytes_accessed=6000000, transcendentals=400000),
        name="inner_bricks",
    )(parity, count, v, xa, xb, own, ids, targets)


def edge_bricks(parity, inner, v, halos, y_rows, planes, to_slot, finder):
    return pl.pallas_call(
        edge_kernel,
        out_shape=jax.ShapeDtypeStruct((PEERS, 16), F32),
        in_specs=parity_specs(12),
        out_specs=vmem_specs(1)[0],
        scratch_shapes=[
            pltpu.VMEM((2, 3, 64, 128), F32),
            pltpu.VMEM((48, 128), F32),
            pltpu.VMEM((8, FIND_ROWS), F32),
        ],
        compiler_params=pltpu.CompilerParams(vmem_limit_bytes=VMEM_LIMIT),
        name="edge_bricks",
    )(parity, inner, v, *halos, y_rows, planes, to_slot, finder)


def swap(value, axis, phase):
    count = lax.axis_size(axis)
    if phase == 0:
        pairs = [(i, i ^ 1) for i in range(count)]
    else:
        pairs = [(i, (i - 1 if i % 2 == 0 else i + 1) % count) for i in range(count)]
    return lax.ppermute(value, axis, pairs)


def exchange(faces):
    xa, xb, ya, yb, za, zb = faces
    zb = swap(zb, "gz", 1)
    yb = swap(yb, "gy", 1)
    ya = swap(ya, "gy", 0)
    za = swap(za, "gz", 0)
    xb = swap(xb, "gx", 1)
    xa = swap(xa, "gx", 0)
    return xa, xb, ya, yb, za, zb


def per_device(phi_start, band_ids, band_count, owners):
    parity = jnp.stack([lax.axis_index(name) % 2 for name in ("gx", "gy", "gz")])
    parity = parity.astype(jnp.int32)
    v, *faces = pack(parity, phi_start)
    sigma, pace = sign_fields(v)
    za0, zb0 = faces[4:]
    for number in range(STEPS):
        v, *faces = step(
            parity, sigma, pace, za0, zb0, v, faces[4], faces[5], exchange(faces),
            number == STEPS - 1,
        )
    level_set = unpack(v)

    xa, xb, ylo, yhi, own = faces
    xb = swap(xb, "gx", 1)
    xa = swap(xa, "gx", 0)
    ya, yb, y_rows = row_faces(parity, xa, xb, ylo, yhi)
    inner, partial, to_slot, finder = inner_bricks(
        parity, band_count.reshape(1), v, xa, xb, own,
        band_ids.reshape(1, SLOTS), owners.reshape(1, SLOTS),
    )
    yb = swap(yb, "gy", 1)
    ya = swap(ya, "gy", 0)
    planes, za, zb = plane_faces(parity, ya, yb, partial)
    zb = swap(zb, "gz", 1)
    za = swap(za, "gz", 0)
    record = edge_bricks(
        parity, inner, v, (xa, xb, ya, yb, za, zb), y_rows, planes, to_slot, finder
    )
    received = lax.all_to_all(record, ("gx", "gy"), split_axis=0, concat_axis=0, tiled=True)
    return level_set, jnp.swapaxes(arrange(received), 2, 3)


def solution(mesh):
    placed = (
        P("gx", "gy", "gz"),
        P("gx", "gy", "gz", None),
        P("gx", "gy", "gz"),
        P("gx", "gy", "gz", None),
    )
    return jax.shard_map(
        per_device,
        mesh=mesh,
        in_specs=placed,
        out_specs=(P("gx", "gy", "gz"), P("gx", "gy", "gz", None, None)),
        check_vma=False,
    )
```

```python
import functools

import jax
import jax.numpy as jnp
from jax import lax
from jax.experimental import pallas as pl
from jax.experimental.pallas import tpu as pltpu
from jax.sharding import PartitionSpec as P

STEPS = 3
BRICK = 16
SLOTS = 64
FIND_ROWS = 1280
PAIR = 8
ROW_PAIR = 2
PEERS = 32
CX, CY, CZ = 32, 48, 256
ROWS = CX * CY
YT = CY // 8
WENO_EPS = 1e-06
F32 = jnp.float32
VMEM_LIMIT = 16 * 1024 * 1024


def rcp(value):
    return pltpu.reciprocal(value, approx=True)


def smooth_weights(e_low, e_high, third):
    twice = third + third
    middle = e_low * e_high + (third * third * (4.0 / 3.0) + WENO_EPS)
    q_a = rcp(middle - e_low * twice)
    q_b = rcp(middle)
    q_c = rcp(middle + e_high * twice)
    return q_a * q_a, 6.0 * (q_b * q_b), q_c * q_c


def biased_parts(wa_next, wb, wc_prev, t_prev, t_here, t_next):
    x = wc_prev * (t_here - t_prev)
    y = wa_next * (t_next - t_here)
    both = x + y
    both = both + both
    total = (wa_next + wb) + wc_prev
    left = t_here + (both + y) * rcp(total + (wa_next + wa_next))
    right = t_here - (both + x) * rcp(total + (wc_prev + wc_prev))
    return left, right


def upwind_square(centre, left, right, sigma):
    return upwind_pair(centre - left, right - centre, sigma)


def upwind_pair(left, right_back, sigma):
    best = jnp.maximum(sigma * left, sigma * right_back)
    best = jnp.maximum(best, 0.0)
    return best * best


def sigma_of(value):
    return jnp.where(value > 0.0, F32(1.0), F32(-1.0))


def from_values(v_m, v_0, v_1, v_2):
    d_m, d_0, d_1 = v_0 - v_m, v_1 - v_0, v_2 - v_1
    e_0, e_1 = d_0 - d_m, d_1 - d_0
    return e_0, e_1, e_1 - e_0


def lane_down(part):
    return pltpu.roll(part, 1, 1)


def lane_up(part):
    return pltpu.roll(part, 127, 1)


def z_stage_weights(even, odd, even_down, odd_down, even_up, odd_up):
    v = {-2: even_down, -1: odd_down, 0: even, 1: odd, 2: even_up, 3: odd_up}
    d = {k: v[k + 1] - v[k] for k in range(-2, 3)}
    e = {k: d[k] - d[k - 1] for k in range(-1, 3)}
    t = {k: e[k + 1] - e[k] for k in range(-1, 2)}
    w_0 = smooth_weights(e[0], e[1], t[0])
    w_1 = smooth_weights(e[1], e[2], t[1])
    return (
        w_1[0], w_0[1], lane_down(w_1[2]), t[-1], t[0], t[1],
        lane_up(w_0[0]), w_1[1], w_0[2], lane_up(t[0]),
        3.0 * (d[-1] + d[0]), 3.0 * (d[0] + d[1]),
    )


def z_stage_parts(wa_0, wb_0, wc_0, t_m, t_0, t_1, wa_1, wb_1, wc_1, t_2, centre_0, centre_1):
    left_0, right_0 = biased_parts(wa_0, wb_0, wc_0, t_m, t_0, t_1)
    left_1, right_1 = biased_parts(wa_1, wb_1, wc_1, t_0, t_1, t_2)
    return centre_0, lane_down(left_1), right_0 - centre_0, centre_1 - left_0, right_1 - centre_1


def edge_column(window, u_ref, p_ref, u_row, p_row, sigma):
    def rows(start):
        return window[pl.ds(start, 8), :]

    e_0, e_1, t = from_values(rows(u_row - 1), rows(u_row), rows(u_row + 1), rows(u_row + 2))
    w_a, w_b, w_c = smooth_weights(e_0, e_1, t)
    for slot, part in enumerate((w_a, w_b, w_c, t)):
        u_ref[slot, pl.ds(u_row, 8), :] = part
    left, right = biased_parts(
        u_ref[0, pl.ds(p_row + 1, 8), :],
        u_ref[1, pl.ds(p_row, 8), :],
        u_ref[2, pl.ds(p_row - 1, 8), :],
        u_ref[3, pl.ds(p_row - 1, 8), :],
        u_ref[3, pl.ds(p_row, 8), :],
        u_ref[3, pl.ds(p_row + 1, 8), :],
    )
    p_ref[0, pl.ds(p_row, 8), :] = left
    p_ref[1, pl.ds(p_row, 8), :] = right
    centre = 3.0 * (rows(9) - rows(7))
    return upwind_square(
        centre, p_ref[0, pl.ds(7, 8), :], p_ref[1, pl.ds(8, 8), :], sigma
    )


def z_faces(source, zlo, zhi):
    for chunk in range(CX // 8):
        columns = slice(8 * CY * chunk, 8 * CY * (chunk + 1))
        for parity in range(2):
            part = source[8 * chunk : 8 * chunk + 8, :, 128 * parity : 128 * parity + 128]
            part = part.reshape(8 * CY, 128).T
            for k in range(4):
                zlo[2 * k + parity : 2 * k + parity + 1, columns] = part[k : k + 1]
                zhi[2 * k + parity : 2 * k + parity + 1, columns] = part[124 + k : 125 + k]


def y_faces(source, ylo, yhi, width):
    for x in range(CX):
        for k in range(width):
            ylo[k, x : x + 1, :] = source[x, k : k + 1, :]
            yhi[k, x : x + 1, :] = source[x, CY - width + k : CY - width + 1 + k, :]


def write_swap(parity, low, high, out_a, out_b):
    odd = parity == 1
    out_a[...] = jnp.where(odd, low, high)
    out_b[...] = jnp.where(odd, high, low)


def write_faces(parity, source, xa, xb, ya, yb, za, zb, yf, zf):
    y_faces(source, yf.at[0], yf.at[1], 3)
    write_swap(parity[1], yf[0], yf[1], ya, yb)
    write_swap(parity[0], source[0:3], source[CX - 3 : CX], xa, xb)
    z_faces(source, zf.at[0], zf.at[1])
    write_swap(parity[2], zf[0], zf[1], za, zb)


def low_high(parity, part_a, part_b):
    odd = parity == 1
    return jnp.where(odd, part_a, part_b), jnp.where(odd, part_b, part_a)


def pack_kernel(parity, phi, mixed, xa, xb, ya, yb, za, zb, turned, yf, zf):
    for chunk in range(CX // 8):
        planes = slice(8 * chunk, 8 * chunk + 8)
        for half in range(2):
            part = phi[planes, :, 128 * half : 128 * half + 128]
            part = part.reshape(8 * CY, 128).T
            for c in range(3):
                turned[c, 128 * half : 128 * half + 128, :] = part[:, 128 * c : 128 * c + 128]
        for which in range(2):
            part = [turned[c, pl.ds(which, 128, stride=2), :].T for c in range(3)]
            part = jnp.concatenate(part, axis=0)
            mixed[planes, :, 128 * which : 128 * which + 128] = part.reshape(8, CY, 128)
    write_faces(parity, mixed, xa, xb, ya, yb, za, zb, yf, zf)


def signs_kernel(start, sigma, pace):
    def signs(x, carry):
        value = start[x]
        sigma[x] = sigma_of(value)
        pace[x] = (0.05 * value) * lax.rsqrt(value * value + 1.0)
        return carry

    lax.fori_loop(0, CX, signs, 0)


def unpack_kernel(mixed, out, turned):
    for chunk in range(CX // 8):
        planes = slice(8 * chunk, 8 * chunk + 8)
        for parity in range(2):
            part = mixed[planes, :, 128 * parity : 128 * parity + 128]
            part = part.reshape(8 * CY, 128).T
            for c in range(3):
                turned[c, pl.ds(parity, 128, stride=2), :] = part[:, 128 * c : 128 * c + 128]
        for half in range(2):
            part = [turned[c, 128 * half : 128 * half + 128, :].T for c in range(3)]
            part = jnp.concatenate(part, axis=0)
            out[planes, :, 128 * half : 128 * half + 128] = part.reshape(8, CY, 128)


def edge_lanes():
    lane = lax.broadcasted_iota(jnp.int32, (8, 128), 1)
    return [(lane < 2) | (lane == 127), (lane < 1) | (lane > 125)]


def run_stages(stages, count):
    depth = len(stages) - 1

    def run(at, low, high):
        for delay in range(high, low - 1, -1):
            stages[delay](at - delay)

    def body(at, carry):
        run(at, 0, depth)
        return carry

    for at in range(depth):
        run(at, 0, at)
    lax.fori_loop(depth, count, body, 0)
    for at in range(depth):
        run(count + at, at + 1, depth)


def xz_kernel(parity, sigma_in, v, xa_in, xb_in, summed, xh, rolled, zs, zp):
    xh[0], xh[1] = low_high(parity[0], xa_in[...], xb_in[...])

    def x_pass(yt, carry):
        row = pl.multiple_of(8 * yt, 8)
        for zt in range(2):
            lanes = pl.ds(128 * zt, 128)

            def cell(x):
                if x < 0:
                    return xh[0, 3 + x, pl.ds(row, 8), lanes]
                if x >= CX:
                    return xh[1, x - CX, pl.ds(row, 8), lanes]
                return v[x, pl.ds(row, 8), lanes]

            d, e, t, weights, lefts, rights = {}, {}, {}, {}, {}, {}
            d[-3] = cell(-2) - cell(-3)
            d[-2] = cell(-1) - cell(-2)
            e[-2] = d[-2] - d[-3]
            for j in range(-2, CX + 1):
                d[j + 1] = cell(j + 2) - cell(j + 1)
                e[j + 1] = d[j + 1] - d[j]
                t[j] = e[j + 1] - e[j]
                weights[j] = smooth_weights(e[j], e[j + 1], t[j])
                p = j - 1
                if p >= -1:
                    lefts[p], rights[p] = biased_parts(
                        weights[p + 1][0], weights[p][1], weights[p - 1][2], t[p - 1], t[p], t[p + 1]
                    )
                if p >= 0:
                    sigma = sigma_in[p, pl.ds(row, 8), lanes]
                    centre = 3.0 * (d[p - 1] + d[p])
                    summed[zt, p, pl.ds(row, 8), :] = upwind_square(
                        centre, lefts[p - 1], rights[p], sigma
                    )
        return carry

    lax.fori_loop(0, YT, x_pass, 0)
    edge = edge_lanes()

    def tile(x, half, k):
        return v[x, 8 * k : 8 * k + 8, 128 * half : 128 * half + 128]

    def spots(item):
        for sub in range(PAIR):
            for k in range(YT):
                start = CY * sub + 8 * k
                yield PAIR * item + sub, k, slice(start, start + 8)

    def turn(item):
        for x, k, at in spots(item):
            for half in range(2):
                part = tile(x, half, k)
                rolled[half, at, :] = lane_down(part)
                rolled[2 + half, at, :] = lane_up(part)

    def weigh(item):
        for x, k, at in spots(item):
            parts = z_stage_weights(
                tile(x, 0, k), tile(x, 1, k), *[rolled[slot, at, :] for slot in range(4)]
            )
            for slot, part in enumerate(parts):
                zs[slot, at, :] = part

    def blend(item):
        for x, k, at in spots(item):
            parts = z_stage_parts(*[zs[slot, at, :] for slot in range(12)])
            for slot, part in enumerate(parts):
                zp[slot, at, :] = part

    def add(item):
        for x, k, at in spots(item):
            rows = slice(8 * k, 8 * k + 8)
            for half in range(2):
                sigma = sigma_in[x, rows, 128 * half : 128 * half + 128]
                if half == 0:
                    along = upwind_pair(zp[0, at, :] - zp[1, at, :], zp[2, at, :], sigma)
                else:
                    along = upwind_pair(zp[3, at, :], zp[4, at, :], sigma)
                summed[half, x, rows, :] += jnp.where(edge[half], 0.0, along)

    run_stages((turn, weigh, blend, add), CX // PAIR)


def step_kernel(
    last,
    parity, sigma_in, pace, za0, zb0, v, za_own, zb_own, summed, ya_in, yb_in, za_in, zb_in,
    *refs,
):
    faces = 6 if last else 7
    step_body(last, parity, sigma_in, pace, za0, zb0, v, za_own, zb_own, summed, ya_in,
              yb_in, za_in, zb_in, refs[:faces], *refs[faces:])


def step_body(
    last,
    parity, sigma_in, pace, za0, zb0, v, za_own, zb_own, summed, ya_in, yb_in, za_in, zb_in,
    outs,
    vs, u_ref, p_ref, window, zu_ref, zp_ref, edges, fixes, yf, zf,
):
    out = outs[0]

    def fill(x, carry):
        for zt in range(2):
            vs[zt, x, 8 : 8 + CY, :] = v[x, :, pl.ds(128 * zt, 128)]
        return carry

    lax.fori_loop(0, CX, fill, 0)
    yf[0], yf[1] = low_high(parity[1], ya_in[...], yb_in[...])
    for x in range(CX):
        for zt in range(2):
            lanes = slice(128 * zt, 128 * zt + 128)
            for k in range(3):
                vs[zt, x, 5 + k : 6 + k, :] = yf[0, k, x : x + 1, lanes]
                vs[zt, x, 8 + CY + k : 9 + CY + k, :] = yf[1, k, x : x + 1, lanes]

    z_low, z_high = low_high(parity[2], za_in[...], zb_in[...])
    zlo0, zhi0 = low_high(parity[2], za0[...], zb0[...])
    zlo_own, zhi_own = low_high(parity[2], za_own[...], zb_own[...])
    window[5:8, :] = z_low[5:8]
    window[8:16, :] = zlo_own
    fixed = edge_column(window, zu_ref, zp_ref, 6, 7, sigma_of(zlo0))
    for half, lane_at, cell_at in ((0, 0, 0), (0, 1, 2), (1, 0, 1)):
        edges[half, lane_at : lane_at + 1, :] = fixed[cell_at : cell_at + 1]
    window[8:16, :] = zhi_own
    window[16:19, :] = z_high[0:3]
    fixed = edge_column(window, zu_ref, zp_ref, 9, 8, sigma_of(zhi0))
    for half, lane_at, cell_at in ((0, 127, 6), (1, 126, 5), (1, 127, 7)):
        edges[half, lane_at : lane_at + 1, :] = fixed[cell_at : cell_at + 1]
    for half in range(2):
        fixes[half] = edges[half].T

    edge = edge_lanes()

    def y_weights(x, spot, zt, k):
        start = 6 + 8 * k
        e_0, e_1, t = from_values(
            *[vs[zt, x, pl.ds(start + shift, 8), :] for shift in (-1, 0, 1, 2)]
        )
        w_a, w_b, w_c = smooth_weights(e_0, e_1, t)
        for slot, part in enumerate((w_a, w_b, w_c, t)):
            u_ref[spot, slot, pl.ds(8 * k, 8), :] = part

    def y_parts(spot, k):
        def read(slot, row):
            return u_ref[spot, slot, pl.ds(row, 8), :]

        row = 8 * k + 1
        left, right = biased_parts(
            read(0, row + 1), read(1, row), read(2, row - 1),
            read(3, row - 1), read(3, row), read(3, row + 1),
        )
        p_ref[spot, 0, pl.ds(8 * k, 8), :] = left
        p_ref[spot, 1, pl.ds(8 * k, 8), :] = right

    def weigh(item):
        for sub in range(ROW_PAIR):
            for zt in range(2):
                for k in range(YT + 1):
                    y_weights(ROW_PAIR * item + sub, 2 * sub + zt, zt, k)

    def blend(item):
        for spot in range(2 * ROW_PAIR):
            for k in range(YT + 1):
                y_parts(spot, k)

    def update(item):
        for sub in range(ROW_PAIR):
            update_plane(ROW_PAIR * item + sub, 2 * sub)

    def update_plane(x, spot):
        flat = pl.multiple_of(x * CY, 8)
        for zt in range(2):
            for k in range(YT):
                rows = slice(8 * k, 8 * k + 8)
                lanes = slice(128 * zt, 128 * zt + 128)
                centre = 3.0 * (
                    vs[zt, x, 9 + 8 * k : 17 + 8 * k, :] - vs[zt, x, 7 + 8 * k : 15 + 8 * k, :]
                )
                along = upwind_square(
                    centre, p_ref[spot + zt, 0, rows, :],
                    p_ref[spot + zt, 1, 8 * k + 1 : 8 * k + 9, :],
                    sigma_in[x, rows, lanes],
                )
                fix = jnp.where(edge[zt], fixes[zt, pl.ds(flat + 8 * k, 8), :], 0.0)
                total = summed[zt, x, rows, :] + along + fix
                root = total * lax.rsqrt(jnp.maximum(total, 1e-30))
                out[x, rows, lanes] = v[x, rows, lanes] - pace[x, rows, lanes] * (root - 6.0)

    run_stages((weigh, blend, update), CX // ROW_PAIR)
    if last:
        xa, xb, ylo, yhi, planes = outs[1:]
        write_swap(parity[0], out[0:1], out[CX - 1 : CX], xa, xb)
        y_faces(out, ylo, yhi, 2)
        planes[...] = jnp.zeros((4, CX, 128), F32)
        for chunk in range(CX // 8):
            for half in range(2):
                part = out[8 * chunk : 8 * chunk + 8, :, 128 * half : 128 * half + 128]
                part = part.reshape(8 * CY, 128).T
                for x in range(8):
                    lanes = slice(CY * x, CY * x + CY)
                    at = slice(8 * chunk + x, 8 * chunk + x + 1)
                    planes[half, at, 0:CY] = part[0:1, lanes]
                    planes[2 + half, at, 0:CY] = part[127:128, lanes]
    else:
        write_faces(parity, out, *outs[1:], yf, zf)


def rows_kernel(parity, xa, xb, ylo, yhi, ya, yb, y_rows):
    x_low, x_high = low_high(parity[0], xa[0], xb[0])
    for at, (source, layer, row) in enumerate(
        ((ylo, 0, 0), (ylo, 1, 1), (yhi, 0, CY - 2), (yhi, 1, CY - 1))
    ):
        y_rows[at, 0:1, :] = x_low[row : row + 1]
        y_rows[at, 1 : CX + 1, :] = source[layer]
        y_rows[at, CX + 1 : CX + 2, :] = x_high[row : row + 1]
    write_swap(parity[1], y_rows[0], y_rows[3], ya, yb)


def fill_planes(parity, xa, xb, own, planes):
    x_sides = low_high(parity[0], xa[0], xb[0])
    planes[...] = jnp.zeros((4, 40, 128), F32)
    for q in range(4):
        planes[q, 1 : CX + 1, :] = own[q]
    for side in range(2):
        row = (CX + 1) * side
        for half in range(2):
            turned = x_sides[side][:, 128 * half : 128 * half + 128].T
            planes[half, row : row + 1, 0:CY] = turned[0:1]
            planes[2 + half, row : row + 1, 0:CY] = turned[127:128]


def planes_kernel(parity, ya, yb, partial, planes, za, zb):
    y_low, y_high = low_high(parity[1], ya[...], yb[...])
    planes[...] = partial[...]
    lane = lax.broadcasted_iota(jnp.int32, (CX + 2, 128), 1)
    for q in range(4):
        lanes = slice(128 * (q % 2), 128 * (q % 2) + 128)
        start = 0 if q < 2 else 127
        low = y_low[:, lanes]
        if start != 127:
            low = pltpu.roll(low, 127 - start, 1)
        high = pltpu.roll(y_high[:, lanes], (CY - start) % 128, 1)
        planes[q, 0 : CX + 2, :] = jnp.where(
            lane == 127, low, jnp.where(lane == CY, high, partial[q, 0 : CX + 2, :])
        )
    write_swap(parity[2], planes[0], planes[3], za, zb)


def face_shapes(width):
    shapes = [(width, CY, CZ)] * 2 + [(max(width, 2), CX, CZ)] * 2
    shapes += [(8, ROWS)] * 2 if width == 3 else [(4, CX, 128)]
    return [jax.ShapeDtypeStruct(shape, F32) for shape in shapes]


def row_faces(parity, xa, xb, ylo, yhi):
    return pl.pallas_call(
        rows_kernel,
        out_shape=[jax.ShapeDtypeStruct((CX + 2, CZ), F32)] * 2
        + [jax.ShapeDtypeStruct((4, CX + 2, CZ), F32)],
        in_specs=parity_specs(4),
        out_specs=vmem_specs(3),
        compiler_params=pltpu.CompilerParams(vmem_limit_bytes=VMEM_LIMIT),
        name="row_faces",
    )(parity, xa, xb, ylo, yhi)


def plane_faces(parity, ya, yb, partial):
    return pl.pallas_call(
        planes_kernel,
        out_shape=[jax.ShapeDtypeStruct(shape, F32) for shape in ((4, 40, 128), (40, 128), (40, 128))],
        in_specs=parity_specs(3),
        out_specs=vmem_specs(3),
        compiler_params=pltpu.CompilerParams(vmem_limit_bytes=VMEM_LIMIT),
        name="plane_faces",
    )(parity, ya, yb, partial)


BLOCK = jax.ShapeDtypeStruct((CX, CY, CZ), F32)
FACE_SCRATCH = [pltpu.VMEM((2, 3, CX, CZ), F32), pltpu.VMEM((2, 8, ROWS), F32)]


def vmem_specs(count):
    return [pl.BlockSpec(memory_space=pltpu.VMEM)] * count


def parity_specs(count):
    return [pl.BlockSpec(memory_space=pltpu.SMEM)] + vmem_specs(count)


def pack(parity, phi):
    return pl.pallas_call(
        pack_kernel,
        out_shape=[BLOCK] + face_shapes(3),
        in_specs=parity_specs(1),
        out_specs=vmem_specs(7),
        scratch_shapes=[pltpu.VMEM((3, CZ, 128), F32)]
        + FACE_SCRATCH,
        compiler_params=pltpu.CompilerParams(vmem_limit_bytes=VMEM_LIMIT),
        name="pack",
    )(parity, phi)


def sign_fields(start):
    return pl.pallas_call(
        signs_kernel,
        out_shape=[BLOCK] * 2,
        in_specs=vmem_specs(1),
        out_specs=vmem_specs(2),
        compiler_params=pltpu.CompilerParams(vmem_limit_bytes=VMEM_LIMIT),
        cost_estimate=pl.CostEstimate(flops=2000000, bytes_accessed=4700000, transcendentals=400000),
        name="sign_fields",
    )(start)


def unpack(mixed):
    return pl.pallas_call(
        unpack_kernel,
        out_shape=BLOCK,
        in_specs=vmem_specs(1),
        out_specs=vmem_specs(1)[0],
        scratch_shapes=[pltpu.VMEM((3, CZ, 128), F32)],
        compiler_params=pltpu.CompilerParams(vmem_limit_bytes=VMEM_LIMIT),
        name="unpack",
    )(mixed)


def xz_sums(parity, sigma, v, xa, xb):
    return pl.pallas_call(
        xz_kernel,
        out_shape=jax.ShapeDtypeStruct((2, CX, CY, 128), F32),
        in_specs=parity_specs(4),
        out_specs=vmem_specs(1)[0],
        scratch_shapes=[
            pltpu.VMEM((2, 3, CY, CZ), F32),
            pltpu.VMEM((4, PAIR * CY, 128), F32),
            pltpu.VMEM((12, PAIR * CY, 128), F32),
            pltpu.VMEM((5, PAIR * CY, 128), F32),
        ],
        compiler_params=pltpu.CompilerParams(vmem_limit_bytes=VMEM_LIMIT),
        cost_estimate=pl.CostEstimate(flops=20000000, bytes_accessed=6000000, transcendentals=400000),
        name="xz_sums",
    )(parity, sigma, v, xa, xb)


def step(parity, sigma_in, pace, za0, zb0, v, za_own, zb_own, halos, last):
    xa, xb, *others = halos
    summed = xz_sums(parity, sigma_in, v, xa, xb)
    return pl.pallas_call(
        functools.partial(step_kernel, last),
        out_shape=[BLOCK] + face_shapes(1 if last else 3),
        in_specs=parity_specs(12),
        out_specs=vmem_specs(6 if last else 7),
        scratch_shapes=[
            pltpu.VMEM((2, CX, 64, 128), F32),
            pltpu.VMEM((2 * ROW_PAIR, 4, 64, 128), F32),
            pltpu.VMEM((2 * ROW_PAIR, 2, 64, 128), F32),
            pltpu.VMEM((24, ROWS), F32),
            pltpu.VMEM((4, 24, ROWS), F32),
            pltpu.VMEM((2, 24, ROWS), F32),
            pltpu.VMEM((2, 128, ROWS), F32),
            pltpu.VMEM((2, ROWS, 128), F32),
        ]
        + FACE_SCRATCH,
        compiler_params=pltpu.CompilerParams(vmem_limit_bytes=VMEM_LIMIT),
        name="step",
    )(parity, sigma_in, pace, za0, zb0, v, za_own, zb_own, summed, *others)


HALF_COS = [
    0.9999999991256178, -0.23370050635094053, 0.019968606689123116,
    -0.0008935362743290266, 2.3601076640059624e-05,
]
BAND_SQUARE = 1.5 * 1.5


def half_cosine(value):
    square = jnp.minimum(value * value, BAND_SQUARE)
    shape = F32(HALF_COS[4] / BAND_SQUARE**5)
    for k in (3, 2, 1, 0):
        shape = shape * square + F32(HALF_COS[k] / BAND_SQUARE ** (k + 1))
    return (BAND_SQUARE - square) * shape


def five_terms(centre, keep, dx, sx, dy, sy, dz, sz, dxy, dxz, dyz):
    twice = centre + centre
    xx, yy, zz = dx * dx, dy * dy, dz * dz
    squares = jnp.maximum(xx + yy + zz, 1.0)
    root = lax.rsqrt(squares)
    bend = (sx - twice) * (yy + zz) + (sy - twice) * (xx + zz) + (sz - twice) * (xx + yy)
    bend = bend - 0.5 * (dx * (dy * dxy + dz * dxz) + dy * dz * dyz)
    cosine = half_cosine(centre)
    spread = cosine * cosine
    if keep is not None:
        spread = jnp.where(keep, spread, 0.0)
    return (
        spread * (squares * root),
        spread * bend * (root * root),
        spread * dx,
        spread * dy,
        spread * dz,
    )


def brick_tables(ids, targets, live_count):
    entry = lax.broadcasted_iota(jnp.int32, (1, SLOTS), 1)
    live = entry < live_count
    row = lax.broadcasted_iota(jnp.int32, (SLOTS, SLOTS), 0)
    column = lax.broadcasted_iota(jnp.int32, (SLOTS, SLOTS), 1)
    owner = targets.astype(F32)
    down = jnp.sum(jnp.where(row == column, owner, 0.0), axis=1, keepdims=True)
    earlier = (row < column) & (row < live_count) & (down == owner)
    rank = jnp.sum(earlier.astype(F32), axis=0, keepdims=True)
    owner_at = jnp.where(live, owner, F32(SLOTS))
    peers = lax.broadcasted_iota(jnp.int32, (PEERS, SLOTS), 0).astype(F32)
    to_slot = [((owner_at == peers) & (rank == F32(c))).astype(F32) for c in range(2)]

    at = lax.broadcasted_iota(jnp.int32, (FIND_ROWS, SLOTS), 0)
    inner = 16 * (at // 128) + at % 128 // 8
    face = at - 768
    y = face % 128
    end = 48 * (face // 128 % 2) + 16 * (y // 16) + 15 * (face // 256)
    brick = jnp.where(at < 768, inner, jnp.where(y < CY, end, -1))
    return to_slot, (ids == brick).astype(F32)


def exact_dot(left, right, dims=(((1,), (0,)), ((), ()))):
    return lax.dot_general(
        left, right, dims, precision=lax.Precision.HIGHEST, preferred_element_type=F32
    )


def neighbours(pair):
    return ((lane_down(pair[1]), pair[1]), (pair[0], lane_up(pair[0])))


def pair_terms(grid, keeps):
    two = range(2)

    def diff(first, second):
        return [grid[first][half] - grid[second][half] for half in two]

    def summed(first, second):
        return [grid[first][half] + grid[second][half] for half in two]

    dx, sx = diff((1, 0), (-1, 0)), summed((1, 0), (-1, 0))
    dy, sy = diff((0, 1), (0, -1)), summed((0, 1), (0, -1))
    over, under = diff((1, 1), (-1, 1)), diff((1, -1), (-1, -1))
    around, dx_around, dy_around = neighbours(grid[0, 0]), neighbours(dx), neighbours(dy)
    results = []
    for half in two:
        results.append(
            five_terms(
                grid[0, 0][half], keeps[half], dx[half], sx[half], dy[half], sy[half],
                around[half][1] - around[half][0], around[half][1] + around[half][0],
                over[half] - under[half],
                dx_around[half][1] - dx_around[half][0],
                dy_around[half][1] - dy_around[half][0],
            )
        )
    return [results[0][n] + results[1][n] for n in range(5)]


STAR = [(0, 0), (1, 0), (-1, 0), (0, 1), (0, -1), (1, 1), (1, -1), (-1, 1), (-1, -1)]


def tile_terms(vs, plane, k, keeps):
    grid = {
        (sx, sy): [vs[half, plane + sx, pl.ds(8 + 8 * k + sy, 8), :] for half in range(2)]
        for sx, sy in STAR
    }
    return pair_terms(grid, keeps)


def z_keeps(rows):
    lane = lax.broadcasted_iota(jnp.int32, (rows, 128), 1)
    return [lane != 0, lane != 127]


def inner_kernel(
    parity, count, v, xa, xb, own, ids, targets, stack, partial, to_slot, finder, vs
):
    fill_planes(parity, xa, xb, own, partial)
    slots, found = brick_tables(ids[...], targets[...], count[0])
    for c in range(2):
        to_slot[c] = slots[c]
    finder[...] = found

    def fill(x, carry):
        for half in range(2):
            vs[half, x, 8 : 8 + CY, :] = v[x, :, pl.ds(128 * half, 128)]
            vs[half, x, 7:8, :] = jnp.zeros((1, 128), F32)
            vs[half, x, 8 + CY : 9 + CY, :] = jnp.zeros((1, 128), F32)
        return carry

    lax.fori_loop(0, CX, fill, 0)
    keeps = z_keeps(8)
    row = lax.broadcasted_iota(jnp.int32, (8, 128), 0)
    first = [keep & (row != 0) for keep in keeps]
    last = [keep & (row != 7) for keep in keeps]
    zeros = jnp.zeros((8, 128), F32)
    for bx in range(2):

        def body(step_at, sums):
            sums = list(sums)
            for sub in range(3):
                x = BRICK * bx + (1 - bx) + 3 * step_at + sub
                for k in range(YT):
                    parts = tile_terms(vs, x, k, first if k == 0 else last if k == 5 else keeps)
                    for n in range(5):
                        slot = 5 * (k // 2) + n
                        sums[slot] = sums[slot] + parts[n]
            return tuple(sums)

        sums = lax.fori_loop(0, 5, body, (zeros,) * 15)
        for by in range(3):
            row_at = 8 * (3 * bx + by)
            for n in range(5):
                total = jnp.sum(sums[5 * by + n], axis=0, keepdims=True)
                stack[row_at + n : row_at + n + 1, :] = total
            stack[row_at + 5 : row_at + 8, :] = jnp.zeros((3, 128), F32)


def edge_kernel(
    parity, inner, v, xa, xb, ya, yb, za, zb, y_rows, planes, to_slot, finder, record,
    vs, stack, gathered,
):
    x_sides = low_high(parity[0], xa[0], xb[0])
    y_sides = low_high(parity[1], ya[...], yb[...])
    under, over = low_high(parity[2], za[...], zb[...])
    stack[...] = inner[...]

    def add(b, n, row):
        stack[8 * b + n : 8 * b + n + 1, :] += row

    keeps = z_keeps(8)
    for side in range(2):
        for half in range(2):
            lanes = slice(128 * half, 128 * half + 128)
            for at in range(3):
                x = at - 1 if side == 0 else CX - 2 + at
                if 0 <= x < CX:
                    vs[half, at, 8 : 8 + CY, :] = v[x, :, lanes]
                else:
                    vs[half, at, 8 : 8 + CY, :] = x_sides[side][:, lanes]
                vs[half, at, 7:8, :] = y_sides[0][x + 1 : x + 2, lanes]
                vs[half, at, 8 + CY : 9 + CY, :] = y_sides[1][x + 1 : x + 2, lanes]
        for by in range(3):
            parts = [tile_terms(vs, 1, 2 * by + sub, keeps) for sub in range(2)]
            for n in range(5):
                add(3 * side + by, n, jnp.sum(parts[0][n] + parts[1][n], axis=0, keepdims=True))

    keeps = z_keeps(16)
    row = lax.broadcasted_iota(jnp.int32, (16, 128), 0)
    for side in range(2):
        if side == 0:
            rows = (y_sides[0], y_rows[0], y_rows[1])
        else:
            rows = (y_rows[2], y_rows[3], y_sides[1])
        for bx in range(2):
            grid = {
                (sx, sy): [
                    rows[1 + sy][1 + 16 * bx + sx : 17 + 16 * bx + sx, 128 * half : 128 * half + 128]
                    for half in range(2)
                ]
                for sx, sy in STAR
            }
            inside = row != (0 if bx == 0 else 15)
            parts = pair_terms(grid, [keep & inside for keep in keeps])
            for n in range(5):
                add(3 * bx + 2 * side, n, jnp.sum(parts[n], axis=0, keepdims=True))

    for b in range(6):
        gathered[:, 128 * b : 128 * b + 128] = stack[8 * b : 8 * b + 8, :]
    for side in range(2):
        window = (under, planes[0], planes[1]) if side == 0 else (planes[2], planes[3], over)

        def cut(plane, step_x, step_y):
            part = window[plane][1 + step_x : 33 + step_x]
            return pltpu.roll(part, (-step_y) % 128, 1) if step_y else part

        high, low = cut(1, 1, 0), cut(1, -1, 0)
        right, left = cut(1, 0, 1), cut(1, 0, -1)
        above, below = cut(2, 0, 0), cut(0, 0, 0)
        terms = five_terms(
            cut(1, 0, 0), None,
            high - low, high + low, right - left, right + left, above - below, above + below,
            (cut(1, 1, 1) - cut(1, -1, 1)) - (cut(1, 1, -1) - cut(1, -1, -1)),
            (cut(2, 1, 0) - cut(2, -1, 0)) - (cut(0, 1, 0) - cut(0, -1, 0)),
            (cut(2, 0, 1) - cut(2, 0, -1)) - (cut(0, 0, 1) - cut(0, 0, -1)),
        )
        for bx in range(2):
            rows = [jnp.sum(term[16 * bx : 16 * bx + 16], axis=0, keepdims=True) for term in terms]
            rows = jnp.concatenate(rows + [jnp.zeros((3, 128), F32)], axis=0)
            start = 768 + 256 * side + 128 * bx
            gathered[:, start : start + 128] = rows
    found = exact_dot(gathered[...], finder[...])
    scale = 2.0 / 3.0 / (BRICK * BRICK)
    row = lax.broadcasted_iota(jnp.int32, (8, SLOTS), 0)
    found = found * jnp.where(row == 1, F32(scale), F32(0.5 * scale))
    for c in range(2):
        record[:, 8 * c : 8 * c + 8] = exact_dot(to_slot[c], found, (((1,), (1,)), ((), ())))


def arrange_kernel(received, out):
    source = lax.broadcasted_iota(jnp.int32, (PEERS, SLOTS), 0)
    slot = lax.broadcasted_iota(jnp.int32, (PEERS, SLOTS), 1)
    total = jnp.zeros((8, SLOTS), F32)
    for c in range(2):
        total = total + exact_dot(
            received[:, 8 * c : 8 * c + 8], (slot == 2 * source + c).astype(F32),
            (((0,), (0,)), ((), ())),
        )
    for n in range(5):
        out[0, 0, n] = total[n : n + 1]


def arrange(received):
    return pl.pallas_call(
        arrange_kernel,
        out_shape=jax.ShapeDtypeStruct((1, 1, 5, 1, SLOTS), F32),
        in_specs=vmem_specs(1),
        out_specs=vmem_specs(1)[0],
        compiler_params=pltpu.CompilerParams(vmem_limit_bytes=VMEM_LIMIT),
        name="arrange",
    )(received)


def inner_bricks(parity, count, v, xa, xb, own, ids, targets):
    shapes = [(48, 128), (4, 40, 128), (2, PEERS, SLOTS), (FIND_ROWS, SLOTS)]
    return pl.pallas_call(
        inner_kernel,
        out_shape=[jax.ShapeDtypeStruct(shape, F32) for shape in shapes],
        in_specs=[pl.BlockSpec(memory_space=pltpu.SMEM)] * 2 + vmem_specs(6),
        out_specs=vmem_specs(4),
        scratch_shapes=[pltpu.VMEM((2, CX, 64, 128), F32)],
        compiler_params=pltpu.CompilerParams(vmem_limit_bytes=VMEM_LIMIT),
        cost_estimate=pl.CostEstimate(flops=20000000, bytes_accessed=6000000, transcendentals=400000),
        name="inner_bricks",
    )(parity, count, v, xa, xb, own, ids, targets)


def edge_bricks(parity, inner, v, halos, y_rows, planes, to_slot, finder):
    return pl.pallas_call(
        edge_kernel,
        out_shape=jax.ShapeDtypeStruct((PEERS, 16), F32),
        in_specs=parity_specs(12),
        out_specs=vmem_specs(1)[0],
        scratch_shapes=[
            pltpu.VMEM((2, 3, 64, 128), F32),
            pltpu.VMEM((48, 128), F32),
            pltpu.VMEM((8, FIND_ROWS), F32),
        ],
        compiler_params=pltpu.CompilerParams(vmem_limit_bytes=VMEM_LIMIT),
        name="edge_bricks",
    )(parity, inner, v, *halos, y_rows, planes, to_slot, finder)


def swap(value, axis, phase):
    count = lax.axis_size(axis)
    if phase == 0:
        pairs = [(i, i ^ 1) for i in range(count)]
    else:
        pairs = [(i, (i - 1 if i % 2 == 0 else i + 1) % count) for i in range(count)]
    return lax.ppermute(value, axis, pairs)


def exchange(faces):
    xa, xb, ya, yb, za, zb = faces
    zb = swap(zb, "gz", 1)
    yb = swap(yb, "gy", 1)
    ya = swap(ya, "gy", 0)
    za = swap(za, "gz", 0)
    xb = swap(xb, "gx", 1)
    xa = swap(xa, "gx", 0)
    return xa, xb, ya, yb, za, zb


def per_device(phi_start, band_ids, band_count, owners):
    parity = jnp.stack([lax.axis_index(name) % 2 for name in ("gx", "gy", "gz")])
    parity = parity.astype(jnp.int32)
    v, *faces = pack(parity, phi_start)
    sigma, pace = sign_fields(v)
    za0, zb0 = faces[4:]
    for number in range(STEPS):
        v, *faces = step(
            parity, sigma, pace, za0, zb0, v, faces[4], faces[5], exchange(faces),
            number == STEPS - 1,
        )
    level_set = unpack(v)

    xa, xb, ylo, yhi, own = faces
    xb = swap(xb, "gx", 1)
    xa = swap(xa, "gx", 0)
    ya, yb, y_rows = row_faces(parity, xa, xb, ylo, yhi)
    inner, partial, to_slot, finder = inner_bricks(
        parity, band_count.reshape(1), v, xa, xb, own,
        band_ids.reshape(1, SLOTS), owners.reshape(1, SLOTS),
    )
    yb = swap(yb, "gy", 1)
    ya = swap(ya, "gy", 0)
    planes, za, zb = plane_faces(parity, ya, yb, partial)
    zb = swap(zb, "gz", 1)
    za = swap(za, "gz", 0)
    record = edge_bricks(
        parity, inner, v, (xa, xb, ya, yb, za, zb), y_rows, planes, to_slot, finder
    )
    received = lax.all_to_all(record, ("gx", "gy"), split_axis=0, concat_axis=0, tiled=True)
    return level_set, jnp.swapaxes(arrange(received), 2, 3)


def solution(mesh):
    placed = (
        P("gx", "gy", "gz"),
        P("gx", "gy", "gz", None),
        P("gx", "gy", "gz"),
        P("gx", "gy", "gz", None),
    )
    return jax.shard_map(
        per_device,
        mesh=mesh,
        in_specs=placed,
        out_specs=(P("gx", "gy", "gz"), P("gx", "gy", "gz", None, None)),
        check_vma=False,
    )
```
